256 devices in a mesh: chain: 16 (over z, core), tile: 16 (over y, x).
Axes of the slice: x: 4, y: 4, z: 8, core: 2. Of those that a mesh axis runs over, the one named last changes fastest.
Arguments:
- inverse_diag: bfloat16 [32, 768, 768], P('chain', 'tile'), as said below
- sub_diag: bfloat16 [32, 768, 768], P('chain', 'tile')
- arrow_rows: bfloat16 [32, 128, 768], P('chain', 'tile'), may hold values from -0.3125 to 0.3125
- arrow_inverse: bfloat16 [128, 128], replicated, as said below
Outputs:
- diag_inverse: float32 [32, 768, 768], P('chain', 'tile')
- arrow_blocks: float32 [32, 128, 768], P('chain', 'tile')
The draws below stay inside these ranges and needn't reach their ends.
Inputs may be any that keep to these rules, and one draw needn't show every extreme that they name: `inverse_diag`: every block is lower triangular with a positive diagonal. `arrow_inverse`: lower triangular with a positive diagonal.
All inputs are finite; a program needn't handle non-finite values.
Results may differ from the reference program's by a relative error of at most 0.019.
Values may be sent and summed in bfloat16 or wider, within the bound.
A program may use at most 64 MiB of HBM per device.

```python
import math
import jax
import jax.numpy as jnp
from jax import lax

NODES = 768
ARROW = 128
BLOCKS = 32


def lower_factor(key, batch_count, matrix_order, lower_end, upper_end, spread_scale):
    first_key, second_key = jax.random.split(key)
    spread = jax.random.normal(first_key, (batch_count, matrix_order, matrix_order), jnp.float32) * (spread_scale / math.sqrt(matrix_order))
    diagonal = jnp.exp(jax.random.uniform(second_key, (batch_count, matrix_order), jnp.float32, math.log(lower_end), math.log(upper_end)))
    indices = jnp.arange(matrix_order)
    strict = indices[:, None] > indices[None, :]
    on_diagonal = indices[:, None] == indices[None, :]
    return jnp.where(strict[None], spread, 0.0) + jnp.where(on_diagonal[None], diagonal[:, :, None], 0.0)


def mixing_blocks(key, batch_count, matrix_order, overall_gain):
    keys = jax.random.split(key, 4)
    row_keys = jax.random.split(keys[0], batch_count)
    col_keys = jax.random.split(keys[1], batch_count)
    row_order = jax.vmap(lambda k: jax.random.permutation(k, matrix_order))(row_keys).astype(jnp.int32)
    col_order = jax.vmap(lambda k: jax.random.permutation(k, matrix_order))(col_keys).astype(jnp.int32)
    row_signs = jnp.where(jax.random.bernoulli(keys[2], 0.5, (batch_count, matrix_order)), 1.0, -1.0).astype(jnp.float32)
    col_signs = jnp.where(jax.random.bernoulli(keys[3], 0.5, (batch_count, matrix_order)), 1.0, -1.0).astype(jnp.float32)
    phase = (2 * row_order[:, :, None] + 1) * col_order[:, None, :] % (4 * matrix_order)
    angle = phase.astype(jnp.float32) * (math.pi / (2.0 * matrix_order))
    column_scale = jnp.where(col_order == 0, 1.0 / math.sqrt(2.0), 1.0).astype(jnp.float32)
    scale = column_scale * col_signs * (overall_gain * math.sqrt(2.0 / matrix_order))
    return row_signs[:, :, None] * scale[:, None, :] * jnp.cos(angle)


def draw_inverse_diag(key, part):
    key = jax.random.fold_in(key, 11)
    values = lower_factor(key, BLOCKS, NODES, 0.9, 1.1, 0.35)
    return values.astype(jnp.bfloat16)


def draw_sub_diag(key, part):
    key = jax.random.fold_in(key, 37)
    values = mixing_blocks(key, BLOCKS, NODES, 0.915)
    return values.astype(jnp.bfloat16)


def draw_arrow_inverse(key, part):
    key = jax.random.fold_in(key, 23)
    values = lower_factor(key, 1, ARROW, 0.6, 1.4, 0.6)
    return values[0].astype(jnp.bfloat16)


def shard_levels(key, shape, cuts, smallest, top_value):
    loudness, own = 1.0, jax.random.fold_in(key, 6)
    for position, parts in cuts:
        draws = jnp.exp(jax.random.uniform(jax.random.fold_in(own, position), (parts,), jnp.float32, smallest / len(cuts), top_value / len(cuts)))
        loudness = loudness * jnp.repeat(draws, shape[position] // parts).reshape([-1 if axis == position else 1 for axis in range(len(shape))])
    return loudness


def bell_draw(stream_key, extent, scale, most, cuts=(), dtype=jnp.bfloat16):
    factor_of = shard_levels(stream_key, extent, cuts, -0.22, 0.18) if cuts else 1.0
    drawn = jax.random.normal(stream_key, extent, jnp.float32) * scale * factor_of
    return jnp.minimum(jnp.maximum(drawn, -most), most).astype(dtype)


def setup_inputs(seed: int = 0) -> dict:
    arg_keys = jax.random.split(jax.random.key(seed), 5)
    inverse_diag = draw_inverse_diag(jax.random.fold_in(arg_keys[4], 71), 0)
    sub_diag = draw_sub_diag(jax.random.fold_in(arg_keys[4], 71), 0)
    arrow_rows = bell_draw(arg_keys[2], (BLOCKS, ARROW, NODES), (NODES // 2) ** -0.5, 0.3125, ((0, 16), (1, 16)))
    arrow_inverse = draw_arrow_inverse(jax.random.fold_in(arg_keys[4], 71), 0)
    return dict(inverse_diag=inverse_diag, sub_diag=sub_diag, arrow_rows=arrow_rows, arrow_inverse=arrow_inverse)


def reference(inverse_diag, sub_diag, arrow_rows, arrow_inverse):
    highest = lax.Precision.HIGHEST
    factor = arrow_inverse.astype(jnp.float32)
    sigma_aa = jnp.dot(factor.T, factor, precision=highest)

    def backward(carried_state, block_data):
        state_diag, state_arrow = carried_state
        inverse, lower, arrow = block_data
        coupling = jnp.dot(lower, inverse, preferred_element_type=jnp.float32).astype(jnp.bfloat16)
        arrow_map = jnp.dot(arrow, inverse, preferred_element_type=jnp.float32).astype(jnp.bfloat16)
        coupling, arrow_map = lax.optimization_barrier((coupling, arrow_map))
        coupling = coupling.astype(jnp.float32)
        arrow_map = arrow_map.astype(jnp.float32)
        inverse_full = inverse.astype(jnp.float32)
        w_first = jnp.dot(state_diag, coupling, precision=highest) + jnp.dot(state_arrow.T, arrow_map, precision=highest)
        w_second = jnp.dot(state_arrow, coupling, precision=highest) + jnp.dot(sigma_aa, arrow_map, precision=highest)
        new_diag = jnp.dot(inverse_full.T, inverse_full, precision=highest)
        new_diag = new_diag + jnp.dot(coupling.T, w_first, precision=highest) + jnp.dot(arrow_map.T, w_second, precision=highest)
        new_arrow = -w_second
        return (new_diag, new_arrow), (new_diag, new_arrow)

    initial = (jnp.zeros((NODES, NODES), jnp.float32), jnp.zeros((ARROW, NODES), jnp.float32))
    final_state, outputs = lax.scan(backward, initial, (inverse_diag, sub_diag, arrow_rows), reverse=True)
    return outputs[0], outputs[1]
```

```python
import functools
import jax
import jax.numpy as jnp
from jax import lax
from jax.experimental import pallas as pl
from jax.experimental.pallas import tpu as pltpu
from jax.sharding import PartitionSpec as P

MESH = pl.DeviceIdType.MESH
BF, F32 = jnp.bfloat16, jnp.float32
SIDE = 4
ODD, PAIR, PLANE, TRIPLE, EVEN, SCAN1, SCAN2, SCAN3 = range(8)
OFFSETS = [(dy, dx) for dy in range(SIDE) for dx in range(SIDE) if dy or dx]
OFFSETS.sort(key=lambda o: min(o[0], 4 - o[0]) + min(o[1], 4 - o[1]))
RING = (1, 3, 2)


def tdot(a, b):
    return lax.dot_general(a, b, (((0,), (0,)), ((), ())), preferred_element_type=F32)


def dot(a, b):
    return jnp.dot(a, b, preferred_element_type=F32)


def kernel(
    planes, sizes,
    l_ref, b_ref, a_ref, z_ref, diag_ref, arrow_ref,
    full_l, full_b, full_a, wide, odd_map, odd_diag, cols, rows, tile, q_tile, m_tile,
    far_map, far_diag, part_out, part_in, part_own, q_send,
    last_m, last_q, m_row, m_col, m_total, x_send, x_in, weight, out_send, out_in, sigma,
    send_sem, recv_sem, l_send, l_recv,
):
    row, node, panel, own_arrow = sizes
    arrow = own_arrow * SIDE
    chain = lax.axis_index("chain")
    t = lax.axis_index("tile")
    z, core = chain // 2, chain % 2
    y, x = t // SIDE, t % SIDE
    widths = [min(node, -(-panel * (i + 1) // 128) * 128) for i in range(SIDE)]

    def dev(dz=0, dcore=0, dy=0, dx=0):
        zz = lax.rem(z + dz + planes, planes)
        cc = lax.rem(core + dcore, 2)
        return (zz * 2 + cc, lax.rem(y + dy + SIDE, SIDE) * SIDE + lax.rem(x + dx + SIDE, SIDE))

    used = [0]

    def take(n):
        used[0] += n
        assert used[0] <= send_sem.shape[0]
        return used[0] - n

    def copy(src, dst, sem, where):
        return pltpu.make_async_remote_copy(
            src_ref=src, dst_ref=dst, send_sem=send_sem.at[sem], recv_sem=recv_sem.at[sem],
            device_id=where, device_id_type=MESH)

    class Gather:
        def __init__(self, buf, along_x):
            self.buf, self.along_x, self.base = buf, along_x, take(3)

        def each(self, arriving):
            me = x if self.along_x else y
            for n, d in enumerate(RING):
                where = dev(dx=d) if self.along_x else dev(dy=d)
                to = lax.rem(me + SIDE - d, SIDE) if arriving else me
                yield copy(self.buf(me), self.buf(to), self.base + n, where)

        def start(self):
            for c in self.each(False):
                c.start()

        def wait(self):
            for c in self.each(True):
                c.wait_recv()
            for c in self.each(False):
                c.wait_send()

    peers = [dev(dy=dy, dx=dx) for dy, dx in OFFSETS] + [dev(dcore=1)]
    peers += [dev(dz=d) for d in (1, -1, 2, -2, 4)] + [dev(dz=1, dcore=1), dev(dz=-1, dcore=1)]
    barrier = pltpu.get_barrier_semaphore()
    for peer in peers:
        pl.semaphore_signal(barrier, inc=1, device_id=peer, device_id_type=MESH)

    my_rows = pl.ds(pl.multiple_of(t * row, 16), row)
    panel_rows = pl.ds(pl.multiple_of(x * row, 16), row)
    for b in range(2):
        for i in range(SIDE - 1):
            if widths[i] < node:
                full_l[b, panel * i:panel * (i + 1), widths[i]:] = jnp.zeros((panel, node - widths[i]), BF)
        full_l[b, my_rows, :] = l_ref[b]
        full_b[b, panel_rows, :] = b_ref[b]
    full_a[x] = jnp.concatenate([a_ref[0].astype(F32), a_ref[1].astype(F32)], axis=0).astype(BF)
    sigma[...] = tdot(z_ref[...], z_ref[...])
    pl.semaphore_wait(barrier, len(peers))

    def l_copy(b, n, w):
        dy, dx = OFFSETS[n]
        return pltpu.make_async_remote_copy(
            src_ref=l_ref.at[b, :, :w], dst_ref=full_l.at[b, my_rows, :w],
            send_sem=l_send.at[b, n], recv_sem=l_recv.at[b, t], device_id=dev(dy=dy, dx=dx), device_id_type=MESH)

    def l_each(b, do):
        for i in range(SIDE):
            @pl.when(y == i)
            def _():
                for n in range(len(OFFSETS)):
                    do(l_copy(b, n, widths[i]))

    def l_wait(b):
        for s in range(SIDE * SIDE):
            @pl.when(t != s)
            def _():
                w = widths[s // SIDE]
                pltpu.make_async_remote_copy(
                    src_ref=l_ref.at[b, :, :w], dst_ref=full_l.at[b, pl.ds(s * row, row), :w],
                    send_sem=l_send.at[b, 0], recv_sem=l_recv.at[b, s], device_id=dev(dx=1), device_id_type=MESH,
                ).wait_recv()

    def part_rows(i):
        return pl.ds(pl.multiple_of(i * row, 16), row)

    l_each(0, lambda c: c.start())
    get_b = []
    for b in range(2):
        g = Gather(lambda i, b=b: full_b.at[b, part_rows(i)], True)
        g.start()
        get_b.append(g)
        if b == 0:
            get_a = Gather(lambda i: full_a.at[i], True)
            get_a.start()
            l_each(1, lambda c: c.start())

    def block_map(b, slot):
        for j in range(0, node, 256):
            wide[:panel, j:j + 256] = -dot(full_b[b, :, j:], full_l[b, j:, j:j + 256])
            arrows = -dot(full_a[...].reshape(SIDE * 2 * own_arrow, node)[:, j:], full_l[b, j:, j:j + 256])
            for i in range(SIDE):
                lo = 2 * own_arrow * i + own_arrow * b
                wide[panel + own_arrow * i:panel + own_arrow * (i + 1), j:j + 256] = arrows[lo:lo + own_arrow]
        for c in range(SIDE):
            piece = wide[:, panel * c:panel * (c + 1)]
            rows[slot, c] = piece[:panel].astype(BF)
            if slot == ODD:
                odd_map[c] = piece.astype(BF)

            @pl.when(x == c)
            def _():
                cols[slot, y] = piece[:panel].astype(BF)
                m_tile[slot] = piece[panel:]

    def block_diag(b, slot):
        for i in range(SIDE):
            @pl.when(y == i)
            def _():
                lo = panel * i
                wide[:panel] = tdot(full_l[b, lo:, lo:lo + panel], full_l[b, lo:, :])
        for c in range(SIDE):
            piece = wide[:panel, panel * c:panel * (c + 1)]
            if slot == ODD:
                odd_diag[c] = piece.astype(BF)

            @pl.when(x == c)
            def _():
                q_tile[slot] = piece

    def get_cols(slot):
        return Gather(lambda i: cols.at[slot, i], False)

    def get_rows(slot):
        return Gather(lambda i: rows.at[slot, i], True)

    def product(left, slot):
        total = dot(left(0), cols[slot, 0])
        for k in range(1, SIDE):
            total += dot(left(k), cols[slot, k])
        return total

    def new_map(left, near, to, spread=True):
        total = product(left, near)
        arrows = total[panel:] + m_tile[near]
        m_tile[to] = arrows
        tile[to, :panel] = total[:panel].astype(BF)
        tile[to, panel:] = arrows.astype(BF)
        if spread:
            cols[to, y] = total[:panel].astype(BF)
            rows[to, x] = total[:panel].astype(BF)

    class Congruence:
        def __init__(self, index):
            self.index, self.base = index, take(3)

        def each(self, arriving):
            for n, d in enumerate(RING):
                to = lax.rem(y + d, SIDE)
                at = lax.rem(y + SIDE - d, SIDE) if arriving else y
                yield copy(part_out.at[self.index, to], part_in.at[self.index, at], self.base + n, dev(dy=d))

        def start(self, left, near):
            right = product(left, near).astype(BF)
            for s in range(SIDE):
                piece = tdot(rows[near, s], right)
                part_out[self.index, s] = piece.astype(BF)

                @pl.when(y == s)
                def _():
                    part_own[...] = piece
            for c in self.each(False):
                c.start()
            self.own = part_own[...] + q_tile[near]

        def finish(self, to):
            for c in self.each(True):
                c.wait_recv()
            total = self.own
            for d in RING:
                total += part_in[self.index, lax.rem(y + d, SIDE)].astype(F32)
            q_tile[to] = total
            q_send[to] = total.astype(BF)
            for c in self.each(False):
                c.wait_send()

    l_wait(0)
    get_b[0].wait()
    get_a.wait()
    block_map(0, EVEN)
    even_cols = get_cols(EVEN)
    even_cols.start()
    block_diag(0, EVEN)
    l_wait(1)
    get_b[1].wait()
    block_map(1, ODD)
    odd_cols = get_cols(ODD)
    odd_cols.start()
    block_diag(1, ODD)
    even_cols.wait()
    new_map(lambda k: odd_map[k], EVEN, PAIR)
    pair_cols, pair_rows = get_cols(PAIR), get_rows(PAIR)
    pair_cols.start()
    pair_rows.start()
    sibling = take(2)

    def sibling_copy(n):
        if n:
            return copy(q_send.at[PAIR], far_diag.at[0, x], sibling + 1, dev(dcore=1))
        return copy(tile.at[PAIR], far_map.at[0, x], sibling, dev(dcore=1))

    @pl.when(core == 1)
    def _():
        sibling_copy(0).start()

    pair = Congruence(0)
    pair.start(lambda k: odd_diag[k], EVEN)
    pair.finish(PAIR)

    @pl.when(core == 1)
    def _():
        sibling_copy(1).start()

    odd_cols.wait()
    pair_cols.wait()
    pair_rows.wait()

    shifts = (1, 2, 4)
    slots = (PLANE, SCAN1, SCAN2, SCAN3)
    z_base = take(8)

    def z_copy(n, diag):
        src = q_send.at[slots[n]] if diag else tile.at[slots[n]]
        dst = far_diag.at[n + 1, x] if diag else far_map.at[n + 1, x]
        return copy(src, dst, z_base + 2 * n + diag, dev(dz=-shifts[n]))

    last_base = take(4)

    def last_copy(to_core, diag):
        src = q_send.at[SCAN3] if diag else tile.at[SCAN3, pl.ds(panel, arrow)]
        dst = last_q.at[x] if diag else last_m.at[x]
        return copy(src, dst, last_base + 2 * to_core + diag, dev(dz=-1, dcore=to_core))

    far_maps = [Gather(lambda i, n=n: far_map.at[n, i], True) for n in range(4)]
    far_diags = [Gather(lambda i, n=n: far_diag.at[n, i], True) for n in range(4)]
    triple_cols, triple_rows = get_cols(TRIPLE), get_rows(TRIPLE)
    scan_cols = [get_cols(s) for s in slots[:3]]
    scan_rows = [get_rows(s) for s in slots[:3]]
    triple = Congruence(1)
    scans = [Congruence(2 + n) for n in range(4)]

    @pl.when(core == 0)
    def _():
        sibling_copy(0).wait_recv()
        far_maps[0].start()
        sibling_copy(1).wait_recv()
        far_diags[0].start()
        far_maps[0].wait()
        new_map(lambda k: far_map[0, k], PAIR, PLANE)
        scan_cols[0].start()
        scan_rows[0].start()

        @pl.when(z >= 1)
        def _():
            z_copy(0, 0).start()

        new_map(lambda k: far_map[0, k], ODD, TRIPLE)
        far_diags[0].wait()
        scans[0].start(lambda k: far_diag[0, k], PAIR)
        triple_cols.start()
        triple_rows.start()
        triple.start(lambda k: far_diag[0, k], ODD)

        @pl.when(z < planes - 1)
        def _():
            z_copy(0, 0).wait_recv()
            far_maps[1].start()

        scans[0].finish(PLANE)

        @pl.when(z >= 1)
        def _():
            z_copy(0, 1).start()

        triple.finish(TRIPLE)
        triple_cols.wait()
        triple_rows.wait()
        scan_cols[0].wait()
        scan_rows[0].wait()
        for n in range(3):
            near, to, shift = slots[n], slots[n + 1], shifts[n]

            def send_map():
                if n < 2:
                    @pl.when(z >= shifts[n + 1])
                    def _():
                        z_copy(n + 1, 0).start()
                else:
                    @pl.when(z >= 1)
                    def _():
                        last_copy(0, 0).start()
                        last_copy(1, 0).start()

            def send_diag():
                if n < 2:
                    @pl.when(z >= shifts[n + 1])
                    def _():
                        z_copy(n + 1, 1).start()
                else:
                    @pl.when(z >= 1)
                    def _():
                        last_copy(0, 1).start()
                        last_copy(1, 1).start()

            @pl.when(z + shift < planes)
            def _():
                far_maps[n + 1].wait()
                new_map(lambda k: far_map[n + 1, k], near, to, n < 2)
                send_map()
                if n < 2:
                    @pl.when(z + shifts[n + 1] < planes)
                    def _():
                        scan_cols[n + 1].start()
                        scan_rows[n + 1].start()
                z_copy(n, 1).wait_recv()
                far_diags[n + 1].start()
                far_diags[n + 1].wait()
                scans[n + 1].start(lambda k: far_diag[n + 1, k], near)
                if n < 2:
                    @pl.when(z + shifts[n + 1] < planes)
                    def _():
                        z_copy(n + 1, 0).wait_recv()
                        far_maps[n + 2].start()
                scans[n + 1].finish(to)
                send_diag()
                if n < 2:
                    @pl.when(z + shifts[n + 1] < planes)
                    def _():
                        scan_cols[n + 1].wait()
                        scan_rows[n + 1].wait()

            @pl.when(z + shift >= planes)
            def _():
                tile[to] = tile[near]
                m_tile[to] = m_tile[near]
                q_send[to] = q_send[near]
                send_map()
                send_diag()

        for n in range(3):
            @pl.when(z >= shifts[n])
            def _():
                z_copy(n, 0).wait_send()
                z_copy(n, 1).wait_send()

        @pl.when(z >= 1)
        def _():
            for k in range(2):
                last_copy(k, 0).wait_send()
                last_copy(k, 1).wait_send()

    @pl.when(core == 1)
    def _():
        sibling_copy(0).wait_send()
        sibling_copy(1).wait_send()

    finals = (jnp.where(core == 0, PLANE, PAIR), jnp.where(core == 0, TRIPLE, ODD))
    get_m = Gather(lambda i: last_m.at[i], True)
    get_q = Gather(lambda i: last_q.at[i], True)

    def last_wait(diag):
        for k in range(2):
            @pl.when(core == k)
            def _():
                last_copy(k, diag).wait_recv()

    @pl.when(z < planes - 1)
    def _():
        last_wait(0)
        get_m.start()
        get_m.wait()

    get_mr, get_mc = [], []
    for j in range(2):
        @pl.when(z < planes - 1)
        def _():
            m_total[j] = product(lambda k: last_m[k], finals[j]) + m_tile[finals[j]]

        @pl.when(z == planes - 1)
        def _():
            m_total[j] = m_tile[finals[j]]

        m_row[j, x] = m_total[j].astype(BF)
        m_col[j, y] = m_total[j].astype(BF)
        get_mr.append(Gather(lambda i, j=j: m_row.at[j, i], True))
        get_mc.append(Gather(lambda i, j=j: m_col.at[j, i], False))
        get_mr[j].start()
        get_mc[j].start()
    x_base = take(6)

    def x_each(j, arriving):
        for n, d in enumerate(RING):
            to = lax.rem(x + d, SIDE)
            at = lax.rem(x + SIDE - d, SIDE) if arriving else x
            src = x_send.at[j, pl.ds(pl.multiple_of(to * own_arrow, 8), own_arrow)]
            yield copy(src, x_in.at[j, at], x_base + 3 * j + n, dev(dx=d))

    sigma_rows = sigma[pl.ds(pl.multiple_of(y * arrow, 8), arrow)]
    for j in range(2):
        get_mr[j].wait()
        get_mc[j].wait()
        x_send[j] = lax.dot_general(
            sigma_rows, m_col[j].reshape(SIDE * arrow, panel).astype(F32), (((1,), (0,)), ((), ())),
            precision=lax.Precision.HIGHEST, preferred_element_type=F32)
        x_in[j, x] = x_send[j, pl.ds(pl.multiple_of(x * own_arrow, 8), own_arrow)]
        for c in x_each(j, False):
            c.start()

    @pl.when(z < planes - 1)
    def _():
        last_wait(1)
        get_q.start()
        get_q.wait()
        for j in range(2):
            weight[j] = product(lambda k: last_q[k], finals[j]).astype(BF)

    @pl.when(z == planes - 1)
    def _():
        weight[...] = jnp.zeros_like(weight)

    out_base = take(2 * len(OFFSETS))

    def out_each(j, arriving):
        for n, (dy, dx) in enumerate(OFFSETS):
            ty, tx = lax.rem(y + dy, SIDE), lax.rem(x + dx, SIDE)
            at = (lax.rem(y + SIDE - dy, SIDE), lax.rem(x + SIDE - dx, SIDE)) if arriving else (y, x)
            src = out_send.at[j, ty, pl.ds(pl.multiple_of(tx * row, 16), row)]
            yield copy(src, out_in.at[j, at[0], at[1]], out_base + len(OFFSETS) * j + n, dev(dy=dy, dx=dx))

    for j in range(2):
        arrows = x_send[j].astype(BF)
        for s in range(SIDE):
            part_own[...] = tdot(rows[finals[j], s], weight[j]) + tdot(m_row[j, s], arrows)

            @pl.when(y == s)
            def _():
                part_own[...] += q_tile[finals[j]]
            out_send[j, s] = part_own[...].astype(BF)
        out_in[j, y, x] = out_send[j, y, pl.ds(pl.multiple_of(x * row, 16), row)]
        for c in out_each(j, False):
            c.start()
    for j in range(2):
        for c in x_each(j, True):
            c.wait_recv()
        for i in range(SIDE):
            arrow_ref[j, :, panel * i:panel * (i + 1)] = x_in[j, i]
        for c in x_each(j, False):
            c.wait_send()
    for j in range(2):
        for c in out_each(j, True):
            c.wait_recv()
        for i in range(SIDE):
            total = out_in[j, 0, i].astype(F32)
            for k in range(1, SIDE):
                total += out_in[j, k, i].astype(F32)
            diag_ref[j, :, panel * i:panel * (i + 1)] = total
    for j in range(2):
        for c in out_each(j, False):
            c.wait_send()
    for b in range(2):
        l_each(b, lambda c: c.wait_send())


def solution(mesh):
    planes = mesh.shape["chain"] // 2

    def on_device(inverse_diag, sub_diag, arrow_rows, arrow_inverse):
        count, row, node = inverse_diag.shape
        own_arrow = arrow_rows.shape[1]
        panel, arrow = row * SIDE, own_arrow * SIDE
        vm = pltpu.VMEM
        scratch = [
            vm((2, node, node), BF), vm((2, panel, node), BF), vm((SIDE, 2 * own_arrow, node), BF),
            vm((panel + arrow, node), F32),
            vm((SIDE, panel + arrow, panel), BF), vm((SIDE, panel, panel), BF),
            vm((7, SIDE, panel, panel), BF), vm((7, SIDE, panel, panel), BF),
            vm((8, panel + arrow, panel), BF), vm((8, panel, panel), F32), vm((8, arrow, panel), F32),
            vm((4, SIDE, panel + arrow, panel), BF), vm((4, SIDE, panel, panel), BF),
            vm((6, SIDE, panel, panel), BF), vm((6, SIDE, panel, panel), BF), vm((panel, panel), F32),
            vm((8, panel, panel), BF),
            vm((SIDE, arrow, panel), BF), vm((SIDE, panel, panel), BF),
            vm((2, SIDE, arrow, panel), BF), vm((2, SIDE, arrow, panel), BF), vm((2, arrow, panel), F32),
            vm((2, arrow, panel), F32), vm((2, SIDE, own_arrow, panel), F32),
            vm((2, panel, panel), BF), vm((2, SIDE, panel, panel), BF), vm((2, SIDE, SIDE, row, panel), BF),
            vm(arrow_inverse.shape, F32),
            pltpu.SemaphoreType.DMA((160,)), pltpu.SemaphoreType.DMA((160,)),
            pltpu.SemaphoreType.DMA((2, 15)), pltpu.SemaphoreType.DMA((2, 16)),
        ]
        return pl.pallas_call(
            functools.partial(kernel, planes, (row, node, panel, own_arrow)),
            out_shape=(
                jax.ShapeDtypeStruct(inverse_diag.shape, F32),
                jax.ShapeDtypeStruct(arrow_rows.shape, F32),
            ),
            in_specs=[pl.BlockSpec(memory_space=vm)] * 4,
            out_specs=(pl.BlockSpec(memory_space=vm),) * 2,
            scratch_shapes=scratch,
            compiler_params=pltpu.CompilerParams(
                collective_id=0, has_side_effects=True, vmem_limit_bytes=52 << 20),
            name="selected_inverse",
        )(inverse_diag, sub_diag, arrow_rows, arrow_inverse)

    placed = P("chain", "tile", None)
    return jax.shard_map(
        on_device, mesh=mesh, in_specs=(placed, placed, placed, P()), out_specs=(placed, placed), check_vma=False)
```

```python
import functools
import jax
import jax.numpy as jnp
from jax import lax
from jax.experimental import pallas as pl
from jax.experimental.pallas import tpu as pltpu
from jax.sharding import PartitionSpec as P

MESH = pl.DeviceIdType.MESH
BF, F32 = jnp.bfloat16, jnp.float32
SIDE = 4
ODD, PAIR, PLANE, TRIPLE, EVEN, SCAN1, SCAN2 = range(7)
LONG = 6
OFFSETS = [(dy, dx) for dy in range(SIDE) for dx in range(SIDE) if dy or dx]
OFFSETS.sort(key=lambda o: min(o[0], 4 - o[0]) + min(o[1], 4 - o[1]))
RING = (1, 3, 2)
FAN = (2, 1, 3, 0)


def tdot(a, b):
    return lax.dot_general(a, b, (((0,), (0,)), ((), ())), preferred_element_type=F32)


def dot(a, b):
    return jnp.dot(a, b, preferred_element_type=F32)


def kernel(
    planes, sizes,
    l_in, b_in, a_in, z_in, diag_ref, arrow_ref,
    l_ref, b_ref, a_ref, z_ref, full_l, full_b, full_a, both_a, wide, wide_d, arrows_all, own_tiles, even, odd_far,
    cols, rows, tile, q_tile, m_tile, far_map, far_diag, part_out, part_in, part_own, q_send,
    a_map, a_diag, b_arrow, b_diag, m_row, m_col, m_total, x_send, x_in, weight, out_send, out_in, sigma,
    send_sem, recv_sem, l_send, l_recv, load_sem,
):
    row, node, panel, own_arrow = sizes
    arrow = own_arrow * SIDE
    chain = lax.axis_index("chain")
    t = lax.axis_index("tile")
    z, core = chain // 2, chain % 2
    y, x = t // SIDE, t % SIDE
    widths = [min(node, -(-panel * (i + 1) // 128) * 128) for i in range(SIDE)]
    loads = [pltpu.make_async_copy(src, dst, load_sem.at[n]) for n, (src, dst) in enumerate(
        ((l_in, l_ref), (b_in, b_ref), (a_in, a_ref), (z_in, z_ref)))]
    for load in loads:
        load.start()

    def dev(dz=0, dcore=0, dy=0, dx=0):
        zz = lax.rem(z + dz + planes, planes)
        cc = lax.rem(core + dcore, 2)
        return (zz * 2 + cc, lax.rem(y + dy + SIDE, SIDE) * SIDE + lax.rem(x + dx + SIDE, SIDE))

    used = [0]

    def take(n):
        used[0] += n
        assert used[0] <= send_sem.shape[0]
        return used[0] - n

    def copy(src, dst, sem, where):
        return pltpu.make_async_remote_copy(
            src_ref=src, dst_ref=dst, send_sem=send_sem.at[sem], recv_sem=recv_sem.at[sem],
            device_id=where, device_id_type=MESH)

    class Gather:
        def __init__(self, buf, along_x):
            self.buf, self.along_x, self.base = buf, along_x, take(3)

        def each(self, arriving):
            me = x if self.along_x else y
            for n, d in enumerate(RING):
                where = dev(dx=d) if self.along_x else dev(dy=d)
                to = lax.rem(me + SIDE - d, SIDE) if arriving else me
                yield copy(self.buf(me), self.buf(to), self.base + n, where)

        def start(self):
            for c in self.each(False):
                c.start()

        def wait(self):
            for c in self.each(True):
                c.wait_recv()
            for c in self.each(False):
                c.wait_send()

    barrier = pltpu.get_barrier_semaphore()
    group = [dev(dy=dy, dx=dx) for dy, dx in OFFSETS]
    first = [dev(dcore=1, dx=d) for d in range(SIDE)] + [dev(dz=d) for d in (1, 2, -3)]
    second = [dev(dz=d, dcore=1) for d in (1, -3)]
    for peer in group:
        pl.semaphore_signal(barrier, inc=1, device_id=peer, device_id_type=MESH)
    for k, others in enumerate((first, second)):
        @pl.when(core == k)
        def _():
            for peer in others:
                pl.semaphore_signal(barrier, inc=1, device_id=peer, device_id_type=MESH)

    my_rows = pl.ds(pl.multiple_of(t * row, 16), row)
    panel_rows = pl.ds(pl.multiple_of(x * row, 16), row)
    mine = x // 2 == core
    block = lax.rem(x, 2)
    for i in range(SIDE - 1):
        if widths[i] < node:
            full_l[panel * i:panel * (i + 1), widths[i]:] = jnp.zeros((panel, node - widths[i]), BF)
    for load in loads:
        load.wait()
    both_a[...] = jnp.concatenate([a_ref[0].astype(F32), a_ref[1].astype(F32)], axis=0).astype(BF)
    for k, extra in enumerate((5, SIDE)):
        @pl.when(core == k)
        def _():
            pl.semaphore_wait(barrier, len(group) + extra)

    def to_column(b, dy):
        owner = 2 * core + b
        return (chain, lax.rem(y + dy, SIDE) * SIDE + owner)

    def l_copy(b, dy, w):
        return pltpu.make_async_remote_copy(
            src_ref=l_ref.at[b, :, :w], dst_ref=full_l.at[my_rows, :w], send_sem=l_send.at[b, dy],
            recv_sem=l_recv.at[t], device_id=to_column(b, dy), device_id_type=MESH)

    def b_copy(b):
        return pltpu.make_async_remote_copy(
            src_ref=b_ref.at[b], dst_ref=full_b.at[panel_rows], send_sem=l_send.at[b, 4],
            recv_sem=l_recv.at[16 + x], device_id=to_column(b, 0), device_id_type=MESH)

    def a_copy(b):
        return pltpu.make_async_remote_copy(
            src_ref=both_a, dst_ref=full_a.at[x], send_sem=l_send.at[b, 5],
            recv_sem=l_recv.at[20 + x], device_id=to_column(b, 0), device_id_type=MESH)

    def spread(do):
        for b in range(2):
            for i in range(SIDE):
                @pl.when(y == i)
                def _():
                    for dy in (1, 3, 2):
                        do(l_copy(b, dy, widths[i]))

            @pl.when(x != 2 * core + b)
            def _():
                for i in range(SIDE):
                    @pl.when(y == i)
                    def _():
                        do(l_copy(b, 0, widths[i]))
                do(b_copy(b))
                do(a_copy(b))

    spread(lambda c: c.start())
    sigma[...] = tdot(z_ref[...], z_ref[...])
    tile_base = take(3)

    def tile_send(b, n):
        to = lax.rem(x + RING[n], SIDE)
        dst = odd_far.at[to] if b else even
        return pltpu.make_async_remote_copy(
            src_ref=own_tiles.at[to], dst_ref=dst, send_sem=send_sem.at[tile_base + n],
            recv_sem=l_recv.at[24 + b], device_id=dev(dx=RING[n]), device_id_type=MESH)

    @pl.when(mine)
    def _():
        for b in range(2):
            @pl.when(block == b)
            def _():
                full_l[my_rows, :] = l_ref[b]
                full_b[panel_rows, :] = b_ref[b]
        full_a[x] = both_a[...]
        for s in range(SIDE * SIDE):
            @pl.when(t != s)
            def _():
                w = widths[s // SIDE]
                pltpu.make_async_remote_copy(
                    src_ref=l_ref.at[0, :, :w], dst_ref=full_l.at[pl.ds(s * row, row), :w],
                    send_sem=l_send.at[0, 0], recv_sem=l_recv.at[s], device_id=dev(dx=1), device_id_type=MESH,
                ).wait_recv()
        for s in range(SIDE):
            @pl.when(x != s)
            def _():
                pltpu.make_async_remote_copy(
                    src_ref=b_ref.at[0], dst_ref=full_b.at[pl.ds(s * row, row)], send_sem=l_send.at[0, 4],
                    recv_sem=l_recv.at[16 + s], device_id=dev(dx=1), device_id_type=MESH).wait_recv()
                pltpu.make_async_remote_copy(
                    src_ref=both_a, dst_ref=full_a.at[s], send_sem=l_send.at[0, 5],
                    recv_sem=l_recv.at[20 + s], device_id=dev(dx=1), device_id_type=MESH).wait_recv()
        for j in range(0, node, 256):
            wide[:panel, j:j + 256] = -dot(full_b[:, j:], full_l[j:, j:j + 256])
            arrows_all[:, j:j + 256] = -dot(full_a[...].reshape(SIDE * 2 * own_arrow, node)[:, j:], full_l[j:, j:j + 256])
        for i in range(SIDE):
            lo = pl.multiple_of(2 * own_arrow * i + own_arrow * block, 8)
            wide[panel + own_arrow * i:panel + own_arrow * (i + 1)] = arrows_all[pl.ds(lo, own_arrow)]
        for i in range(SIDE):
            @pl.when(y == i)
            def _():
                lo = panel * i
                wide_d[...] = tdot(full_l[lo:, lo:lo + panel], full_l[lo:, :])
        for c in range(SIDE):
            own_tiles[c, :panel + arrow] = wide[:, panel * c:panel * (c + 1)].astype(BF)
            own_tiles[c, panel + arrow:] = wide_d[:, panel * c:panel * (c + 1)].astype(BF)
        for b in range(2):
            @pl.when(block == b)
            def _():
                for n in range(3):
                    tile_send(b, n).start()
                if b:
                    odd_far[x] = own_tiles[x]
                else:
                    even[...] = own_tiles[x]

    def get_cols(slot):
        return Gather(lambda i: cols.at[slot, i], False)

    def get_rows(slot):
        return Gather(lambda i: rows.at[slot, i], True)

    def product(left, slot):
        total = dot(left(0), cols[slot, 0])
        for k in range(1, SIDE):
            total += dot(left(k), cols[slot, k])
        return total

    def new_map(left, near, to, spread=True):
        total = product(left, near)
        arrows = total[panel:] + m_tile[near]
        m_tile[to] = arrows
        tile[to, :panel] = total[:panel].astype(BF)
        tile[to, panel:] = arrows.astype(BF)
        if spread:
            cols[to, y] = total[:panel].astype(BF)
            rows[to, x] = total[:panel].astype(BF)

    class Congruence:
        def __init__(self, index):
            self.index, self.base = index, take(3)

        def each(self, arriving):
            for n, d in enumerate(RING):
                to = lax.rem(y + d, SIDE)
                at = lax.rem(y + SIDE - d, SIDE) if arriving else y
                yield copy(part_out.at[self.index, to], part_in.at[self.index, at], self.base + n, dev(dy=d))

        def start(self, left, near):
            right = product(left, near).astype(BF)
            for s in range(SIDE):
                piece = tdot(rows[near, s], right)
                part_out[self.index, s] = piece.astype(BF)

                @pl.when(y == s)
                def _():
                    part_own[self.index] = piece + q_tile[near]
            for c in self.each(False):
                c.start()

        def finish(self, to):
            for c in self.each(True):
                c.wait_recv()
            total = part_own[self.index]
            for d in RING:
                total += part_in[self.index, lax.rem(y + d, SIDE)].astype(F32)
            q_tile[to] = total
            q_send[to] = total.astype(BF)
            for c in self.each(False):
                c.wait_send()

    for b in (1, 0):
        @pl.when(x != 2 * core + b)
        def _():
            pltpu.make_async_remote_copy(
                src_ref=own_tiles.at[0], dst_ref=odd_far.at[x] if b else even, send_sem=send_sem.at[tile_base],
                recv_sem=l_recv.at[24 + b], device_id=dev(dx=1), device_id_type=MESH).wait_recv()
    cols[EVEN, y] = even[:panel]
    rows[EVEN, x] = even[:panel]
    even_cols, even_rows, odd_cols = get_cols(EVEN), get_rows(EVEN), get_cols(ODD)
    odd_panel = Gather(lambda i: odd_far.at[i], True)
    even_cols.start()
    odd_panel.start()
    even_rows.start()
    cols[ODD, y] = odd_far[x, :panel]
    m_tile[EVEN] = even[panel:panel + arrow].astype(F32)
    q_tile[EVEN] = even[panel + arrow:].astype(F32)
    m_tile[ODD] = odd_far[x, panel:panel + arrow].astype(F32)
    q_tile[ODD] = odd_far[x, panel + arrow:].astype(F32)
    even_cols.wait()
    odd_panel.wait()
    new_map(lambda k: odd_far[k, :panel + arrow], EVEN, PAIR)
    fan = take(8)

    def fan_copy(d, diag):
        src = q_send.at[PAIR] if diag else tile.at[PAIR]
        dst = far_diag.at[0, x] if diag else far_map.at[0, x]
        return copy(src, dst, fan + 4 * diag + d, dev(dcore=1, dx=d))

    def fan_wait(diag):
        for d in range(SIDE):
            at = lax.rem(x + SIDE - d, SIDE)
            src = q_send.at[PAIR] if diag else tile.at[PAIR]
            dst = far_diag.at[0, at] if diag else far_map.at[0, at]
            copy(src, dst, fan + 4 * diag + d, dev(dcore=1, dx=d)).wait_recv()

    @pl.when(core == 1)
    def _():
        for d in FAN:
            fan_copy(d, 0).start()

    pair_cols, pair_rows = get_cols(PAIR), get_rows(PAIR)
    pair = Congruence(0)
    even_rows.wait()
    pair.start(lambda k: odd_far[k, panel + arrow:], EVEN)
    pair_cols.start()
    pair_rows.start()
    odd_cols.start()
    for k in range(SIDE):
        rows[ODD, k] = odd_far[k, :panel]
    pair.finish(PAIR)

    @pl.when(core == 1)
    def _():
        for d in FAN:
            fan_copy(d, 1).start()

    pair_cols.wait()
    pair_rows.wait()
    odd_cols.wait()

    shifts = (1, 2)
    slots = (PLANE, SCAN1, SCAN2)
    z_base = take(4)

    def z_copy(n, diag):
        src = q_send.at[slots[n]] if diag else tile.at[slots[n]]
        dst = far_diag.at[n + 1, x] if diag else far_map.at[n + 1, x]
        return copy(src, dst, z_base + 2 * n + diag, dev(dz=-shifts[n]))

    last_base = take(8)

    def last_copy(far, to_core, diag):
        if far:
            src = q_send.at[SCAN2] if diag else tile.at[SCAN2, pl.ds(panel, arrow)]
            dst = b_diag.at[x] if diag else b_arrow.at[x]
        else:
            src = q_send.at[SCAN2] if diag else tile.at[SCAN2]
            dst = a_diag.at[x] if diag else a_map.at[x]
        return copy(src, dst, last_base + 4 * far + 2 * to_core + diag, dev(dz=-5 if far else -1, dcore=to_core))

    def last_each(diag, do):
        for far, steps in ((0, 1), (1, 5)):
            @pl.when(z >= steps)
            def _():
                for k in range(2):
                    do(last_copy(far, k, diag))

    def last_wait(far, diag):
        for k in range(2):
            @pl.when(core == k)
            def _():
                last_copy(far, k, diag).wait_recv()

    far_maps = [None] + [Gather(lambda i, n=n: far_map.at[n, i], True) for n in (1, 2)]
    far_diags = [None] + [Gather(lambda i, n=n: far_diag.at[n, i], True) for n in (1, 2)]
    triple_cols, triple_rows = get_cols(TRIPLE), get_rows(TRIPLE)
    scan_cols = [get_cols(s) for s in slots[:2]]
    scan_rows = [get_rows(s) for s in slots[:2]]
    triple = Congruence(1)
    scans = [Congruence(2 + n) for n in range(3)]
    has_a, has_b = z + 1 < planes, z + 5 < planes
    get_am = Gather(lambda i: a_map.at[i], True)
    get_bm = Gather(lambda i: b_arrow.at[i], True)
    get_aq = Gather(lambda i: a_diag.at[i], True)
    get_bq = Gather(lambda i: b_diag.at[i], True)
    long_cols, long_rows = [get_cols(LONG + j) for j in range(2)], [get_rows(LONG + j) for j in range(2)]
    finals = (jnp.where(core == 0, PLANE, PAIR), jnp.where(core == 0, TRIPLE, ODD))

    @pl.when(core == 0)
    def _():
        fan_wait(0)
        new_map(lambda k: far_map[0, k], PAIR, PLANE)

        @pl.when(z >= 1)
        def _():
            z_copy(0, 0).start()

        scan_cols[0].start()
        scan_rows[0].start()
        fan_wait(1)
        scans[0].start(lambda k: far_diag[0, k], PAIR)

        @pl.when(has_a)
        def _():
            z_copy(0, 0).wait_recv()
            far_maps[1].start()

        scans[0].finish(PLANE)

        @pl.when(z >= 1)
        def _():
            z_copy(0, 1).start()

        new_map(lambda k: far_map[0, k], ODD, TRIPLE)
        triple.start(lambda k: far_diag[0, k], ODD)
        scan_cols[0].wait()
        scan_rows[0].wait()

        @pl.when(has_a)
        def _():
            far_maps[1].wait()
            new_map(lambda k: far_map[1, k], PLANE, SCAN1)

            @pl.when(z >= 2)
            def _():
                z_copy(1, 0).start()

            @pl.when(z + 2 < planes)
            def _():
                scan_cols[1].start()
                scan_rows[1].start()
            z_copy(0, 1).wait_recv()
            far_diags[1].start()
            far_diags[1].wait()
            scans[1].start(lambda k: far_diag[1, k], PLANE)

            @pl.when(z + 2 < planes)
            def _():
                z_copy(1, 0).wait_recv()
                far_maps[2].start()
            scans[1].finish(SCAN1)

        @pl.when(z + 1 == planes)
        def _():
            tile[SCAN1] = tile[PLANE]
            m_tile[SCAN1] = m_tile[PLANE]
            q_send[SCAN1] = q_send[PLANE]
            z_copy(1, 0).start()

        @pl.when(z >= 2)
        def _():
            z_copy(1, 1).start()

        triple_cols.start()
        triple_rows.start()
        triple.finish(TRIPLE)

        @pl.when(z + 2 < planes)
        def _():
            scan_cols[1].wait()
            scan_rows[1].wait()
            far_maps[2].wait()
            new_map(lambda k: far_map[2, k], SCAN1, SCAN2, False)

        @pl.when(z + 2 >= planes)
        def _():
            tile[SCAN2] = tile[SCAN1]
            q_send[SCAN2] = q_send[SCAN1]

        last_each(0, lambda c: c.start())

        @pl.when(z + 2 >= planes)
        def _():
            last_each(1, lambda c: c.start())

        triple_cols.wait()
        triple_rows.wait()

        @pl.when(z + 2 < planes)
        def _():
            z_copy(1, 1).wait_recv()
            far_diags[2].start()

    @pl.when(has_a)
    def _():
        last_wait(0, 0)
        get_am.start()

    @pl.when(has_b)
    def _():
        last_wait(1, 0)
        get_bm.start()

    @pl.when((core == 0) & (z + 2 < planes))
    def _():
        far_diags[2].wait()
        scans[2].start(lambda k: far_diag[2, k], SCAN1)

    @pl.when(has_a)
    def _():
        get_am.wait()
        for j in range(2):
            total = product(lambda k: a_map[k], finals[j])
            m_total[j] = total[panel:] + m_tile[finals[j]]

            @pl.when(has_b)
            def _():
                cols[LONG + j, y] = total[:panel].astype(BF)
                rows[LONG + j, x] = total[:panel].astype(BF)
                long_cols[j].start()
                long_rows[j].start()

    @pl.when(z + 1 == planes)
    def _():
        for j in range(2):
            m_total[j] = m_tile[finals[j]]

    @pl.when((core == 0) & (z + 2 < planes))
    def _():
        scans[2].finish(SCAN2)
        last_each(1, lambda c: c.start())

    @pl.when(has_b)
    def _():
        get_bm.wait()
        for j in range(2):
            long_cols[j].wait()
            m_total[j] += product(lambda k: b_arrow[k], LONG + j)

    get_mr, get_mc = [], []
    for j in range(2):
        m_row[j, x] = m_total[j].astype(BF)
        m_col[j, y] = m_total[j].astype(BF)
        get_mr.append(Gather(lambda i, j=j: m_row.at[j, i], True))
        get_mc.append(Gather(lambda i, j=j: m_col.at[j, i], False))
        get_mr[j].start()
        get_mc[j].start()

    @pl.when(has_a)
    def _():
        last_wait(0, 1)
        get_aq.start()

    @pl.when(has_b)
    def _():
        last_wait(1, 1)
        get_bq.start()

    x_base = take(6)

    def x_each(j, arriving):
        for n, d in enumerate(RING):
            to = lax.rem(x + d, SIDE)
            at = lax.rem(x + SIDE - d, SIDE) if arriving else x
            src = x_send.at[j, pl.ds(pl.multiple_of(to * own_arrow, 8), own_arrow)]
            yield copy(src, x_in.at[j, at], x_base + 3 * j + n, dev(dx=d))

    sigma_rows = sigma[pl.ds(pl.multiple_of(y * arrow, 8), arrow)]
    for j in range(2):
        get_mr[j].wait()
        get_mc[j].wait()
        x_send[j] = lax.dot_general(
            sigma_rows, m_col[j].reshape(SIDE * arrow, panel).astype(F32), (((1,), (0,)), ((), ())),
            precision=lax.Precision.HIGHEST, preferred_element_type=F32)
        x_in[j, x] = x_send[j, pl.ds(pl.multiple_of(x * own_arrow, 8), own_arrow)]
        for c in x_each(j, False):
            c.start()

    @pl.when(has_a)
    def _():
        get_aq.wait()
        for j in range(2):
            weight[j] = product(lambda k: a_diag[k], finals[j]).astype(BF)

    @pl.when(has_b)
    def _():
        get_bq.wait()
        for j in range(2):
            long_rows[j].wait()
            weight[2 + j] = product(lambda k: b_diag[k], LONG + j).astype(BF)

    out_base = take(2 * len(OFFSETS))

    def out_each(j, arriving):
        for n, (dy, dx) in enumerate(OFFSETS):
            ty, tx = lax.rem(y + dy, SIDE), lax.rem(x + dx, SIDE)
            at = (lax.rem(y + SIDE - dy, SIDE), lax.rem(x + SIDE - dx, SIDE)) if arriving else (y, x)
            src = out_send.at[j, ty, pl.ds(pl.multiple_of(tx * row, 16), row)]
            yield copy(src, out_in.at[j, at[0], at[1]], out_base + len(OFFSETS) * j + n, dev(dy=dy, dx=dx))

    for j in range(2):
        arrows = x_send[j].astype(BF)
        for s in range(SIDE):
            part_own[5] = tdot(m_row[j, s], arrows)

            @pl.when(has_a)
            def _():
                part_own[5] += tdot(rows[finals[j], s], weight[j])

            @pl.when(has_b)
            def _():
                part_own[5] += tdot(rows[LONG + j, s], weight[2 + j])

            @pl.when(y == s)
            def _():
                part_own[5] += q_tile[finals[j]]
            out_send[j, s] = part_own[5].astype(BF)
        out_in[j, y, x] = out_send[j, y, pl.ds(pl.multiple_of(x * row, 16), row)]
        for c in out_each(j, False):
            c.start()
    for j in range(2):
        for c in x_each(j, True):
            c.wait_recv()
        for i in range(SIDE):
            arrow_ref[j, :, panel * i:panel * (i + 1)] = x_in[j, i]
        for c in x_each(j, False):
            c.wait_send()
    for j in range(2):
        for c in out_each(j, True):
            c.wait_recv()
        for i in range(SIDE):
            total = out_in[j, 0, i].astype(F32)
            for k in range(1, SIDE):
                total += out_in[j, k, i].astype(F32)
            diag_ref[j, :, panel * i:panel * (i + 1)] = total
    for j in range(2):
        for c in out_each(j, False):
            c.wait_send()
    spread(lambda c: c.wait_send())

    @pl.when(mine)
    def _():
        for n in range(3):
            tile_send(0, n).wait_send()

    @pl.when(core == 1)
    def _():
        for d in FAN:
            fan_copy(d, 0).wait_send()
            fan_copy(d, 1).wait_send()

    @pl.when(core == 0)
    def _():
        for n in range(2):
            @pl.when(z >= shifts[n])
            def _():
                z_copy(n, 0).wait_send()
                z_copy(n, 1).wait_send()
        last_each(0, lambda c: c.wait_send())
        last_each(1, lambda c: c.wait_send())


def solution(mesh):
    planes = mesh.shape["chain"] // 2

    def on_device(inverse_diag, sub_diag, arrow_rows, arrow_inverse):
        count, row, node = inverse_diag.shape
        own_arrow = arrow_rows.shape[1]
        panel, arrow = row * SIDE, own_arrow * SIDE
        vm = pltpu.VMEM
        scratch = [
            vm(inverse_diag.shape, BF), vm(sub_diag.shape, BF), vm(arrow_rows.shape, BF), vm(arrow_inverse.shape, BF),
            vm((node, node), BF), vm((panel, node), BF), vm((SIDE, 2 * own_arrow, node), BF), vm((2 * own_arrow, node), BF),
            vm((panel + arrow, node), F32), vm((panel, node), F32), vm((2 * arrow, node), F32),
            vm((SIDE, 2 * panel + arrow, panel), BF), vm((2 * panel + arrow, panel), BF),
            vm((SIDE, 2 * panel + arrow, panel), BF),
            vm((8, SIDE, panel, panel), BF), vm((8, SIDE, panel, panel), BF),
            vm((7, panel + arrow, panel), BF), vm((7, panel, panel), F32), vm((7, arrow, panel), F32),
            vm((3, SIDE, panel + arrow, panel), BF), vm((3, SIDE, panel, panel), BF),
            vm((5, SIDE, panel, panel), BF), vm((5, SIDE, panel, panel), BF), vm((6, panel, panel), F32),
            vm((7, panel, panel), BF),
            vm((SIDE, panel + arrow, panel), BF), vm((SIDE, panel, panel), BF),
            vm((SIDE, arrow, panel), BF), vm((SIDE, panel, panel), BF),
            vm((2, SIDE, arrow, panel), BF), vm((2, SIDE, arrow, panel), BF), vm((2, arrow, panel), F32),
            vm((2, arrow, panel), F32), vm((2, SIDE, own_arrow, panel), F32),
            vm((4, panel, panel), BF), vm((2, SIDE, panel, panel), BF), vm((2, SIDE, SIDE, row, panel), BF),
            vm(arrow_inverse.shape, F32),
            pltpu.SemaphoreType.DMA((200,)), pltpu.SemaphoreType.DMA((200,)),
            pltpu.SemaphoreType.DMA((2, 6)), pltpu.SemaphoreType.DMA((26,)), pltpu.SemaphoreType.DMA((4,)),
        ]
        return pl.pallas_call(
            functools.partial(kernel, planes, (row, node, panel, own_arrow)),
            out_shape=(
                jax.ShapeDtypeStruct(inverse_diag.shape, F32),
                jax.ShapeDtypeStruct(arrow_rows.shape, F32),
            ),
            in_specs=[pl.BlockSpec(memory_space=pl.ANY)] * 4,
            out_specs=(pl.BlockSpec(memory_space=vm),) * 2,
            scratch_shapes=scratch,
            compiler_params=pltpu.CompilerParams(
                collective_id=0, has_side_effects=True, vmem_limit_bytes=52 << 20),
            name="selected_inverse",
        )(inverse_diag, sub_diag, arrow_rows, arrow_inverse)

    placed = P("chain", "tile", None)
    return jax.shard_map(
        on_device, mesh=mesh, in_specs=(placed, placed, placed, P()), out_specs=(placed, placed), check_vma=False)
```

```python
import functools
import jax
import jax.numpy as jnp
from jax import lax
from jax.experimental import pallas as pl
from jax.experimental.pallas import tpu as pltpu
from jax.sharding import PartitionSpec as P

MESH = pl.DeviceIdType.MESH
BF, F32 = jnp.bfloat16, jnp.float32
SIDE = 4
ODD, PAIR, PLANE, TRIPLE, EVEN, TWO, THREE, FOUR = range(8)
LONG = 7
OFFSETS = [(dy, dx) for dy in range(SIDE) for dx in range(SIDE) if dy or dx]
OFFSETS.sort(key=lambda o: min(o[0], 4 - o[0]) + min(o[1], 4 - o[1]))
RING = (1, 3, 2)
FAN = (2, 1, 3, 0)


def tdot(a, b):
    return lax.dot_general(a, b, (((0,), (0,)), ((), ())), preferred_element_type=F32)


def dot(a, b):
    return jnp.dot(a, b, preferred_element_type=F32)


def kernel(
    planes, sizes,
    l_in, b_in, a_in, z_in, diag_ref, arrow_ref,
    l_ref, b_ref, a_ref, z_ref, full_l, full_b, full_a, both_a, wide, wide_d, arrows_all, own_tiles, even, odd_far,
    cols, rows, tile, q_tile, m_tile, far_map, far_diag, part_out, part_in, part_own, part_sum, q_send,
    a_map, a_diag, b_arrow, b_diag, m_row, m_col, m_total, x_send, x_in, weight, out_send, out_in, sigma,
    send_sem, recv_sem, l_send, l_recv, load_sem,
):
    row, node, panel, own_arrow = sizes
    arrow = own_arrow * SIDE
    chain = lax.axis_index("chain")
    t = lax.axis_index("tile")
    z, core = chain // 2, chain % 2
    y, x = t // SIDE, t % SIDE
    r, c = jnp.where(core == 0, y, x), jnp.where(core == 0, x, y)
    widths = [min(node, -(-panel * (i + 1) // 128) * 128) for i in range(SIDE)]
    loads = [pltpu.make_async_copy(src, dst, load_sem.at[n]) for n, (src, dst) in enumerate(
        ((l_in, l_ref), (b_in, b_ref), (a_in, a_ref), (z_in, z_ref)))]
    for load in loads:
        load.start()

    def place(core, r, c):
        return jnp.where(core == 0, r * SIDE + c, c * SIDE + r)

    def dev(dz=0, dcore=0, dr=0, dc=0):
        zz = lax.rem(z + dz + planes, planes)
        cc = lax.rem(core + dcore, 2)
        return (zz * 2 + cc, place(cc, lax.rem(r + dr, SIDE), lax.rem(c + dc, SIDE)))

    def near_by(dy, dx):
        return (chain, lax.rem(y + dy, SIDE) * SIDE + lax.rem(x + dx, SIDE))

    r_at, c_at = [lax.rem(r + d, SIDE) for d in range(SIDE)], [lax.rem(c + d, SIDE) for d in range(SIDE)]
    r_dev, c_dev = [dev(dr=d) for d in range(SIDE)], [dev(dc=d) for d in range(SIDE)]
    is_first = core == 0
    has = [None] + [z + n < planes for n in (1, 2, 3)]
    has_a, has_b = has[1], z + 5 < planes
    late = []

    used = [0]

    def take(n):
        used[0] += n
        assert used[0] <= send_sem.shape[0]
        return used[0] - n

    def copy(src, dst, sem, where):
        return pltpu.make_async_remote_copy(
            src_ref=src, dst_ref=dst, send_sem=send_sem.at[sem], recv_sem=recv_sem.at[sem],
            device_id=where, device_id_type=MESH)

    class Gather:
        def __init__(self, buf, along_c, when=None):
            self.buf, self.along_c, self.base = buf, along_c, take(3)
            late.append((when, self))

        def each(self, arriving):
            at, where = (c_at, c_dev) if self.along_c else (r_at, r_dev)
            for n, d in enumerate(RING):
                to = at[SIDE - d] if arriving else at[0]
                yield copy(self.buf(at[0]), self.buf(to), self.base + n, where[d])

        def start(self):
            for move in self.each(False):
                move.start()

        def wait(self):
            for move in self.each(True):
                move.wait_recv()

    barrier = pltpu.get_barrier_semaphore()
    group = [near_by(dy, dx) for dy, dx in OFFSETS]
    first = [dev(dcore=1, dc=d) for d in range(SIDE)] + [dev(dz=d) for d in (1, 2, 3, -3)]
    second = [dev(dz=d, dcore=1) for d in (1, -3)]
    for peer in group:
        pl.semaphore_signal(barrier, inc=1, device_id=peer, device_id_type=MESH)
    for k, others in enumerate((first, second)):
        @pl.when(core == k)
        def _():
            for peer in others:
                pl.semaphore_signal(barrier, inc=1, device_id=peer, device_id_type=MESH)

    my_rows = pl.ds(pl.multiple_of(t * row, 16), row)
    panel_rows = pl.ds(pl.multiple_of(x * row, 16), row)
    mine = c // 2 == core
    block = lax.rem(c, 2)
    for i in range(SIDE - 1):
        if widths[i] < node:
            full_l[panel * i:panel * (i + 1), widths[i]:] = jnp.zeros((panel, node - widths[i]), BF)
    for load in loads:
        load.wait()
    both_a[...] = jnp.concatenate([a_ref[0].astype(F32), a_ref[1].astype(F32)], axis=0).astype(BF)
    for k, extra in enumerate((6, SIDE)):
        @pl.when(core == k)
        def _():
            pl.semaphore_wait(barrier, len(group) + extra)

    def to_column(b, row):
        return (chain, place(core, row, 2 * core + b))

    def l_copy(b, dr, w):
        return pltpu.make_async_remote_copy(
            src_ref=l_ref.at[b, :, :w], dst_ref=full_l.at[my_rows, :w], send_sem=l_send.at[b, dr],
            recv_sem=l_recv.at[t], device_id=to_column(b, lax.rem(r + dr, SIDE)), device_id_type=MESH)

    def b_copy(b):
        return pltpu.make_async_remote_copy(
            src_ref=b_ref.at[b], dst_ref=full_b.at[panel_rows], send_sem=l_send.at[b, 4],
            recv_sem=l_recv.at[16 + x], device_id=to_column(b, y), device_id_type=MESH)

    def a_copy(b):
        return pltpu.make_async_remote_copy(
            src_ref=both_a, dst_ref=full_a.at[x], send_sem=l_send.at[b, 5],
            recv_sem=l_recv.at[20 + x], device_id=to_column(b, y), device_id_type=MESH)

    def spread(do):
        for b in range(2):
            for i in range(SIDE):
                @pl.when(y == i)
                def _():
                    for dr in (1, 3, 2):
                        do(l_copy(b, dr, widths[i]))

            @pl.when(c != 2 * core + b)
            def _():
                for i in range(SIDE):
                    @pl.when(y == i)
                    def _():
                        do(l_copy(b, 0, widths[i]))

            @pl.when((c != 2 * core + b) | (r != y))
            def _():
                do(b_copy(b))
                do(a_copy(b))

    spread(lambda move: move.start())
    sigma[...] = tdot(z_ref[...], z_ref[...])
    tile_base = take(3)

    def tile_send(b, n):
        to = c_at[RING[n]]
        dst = odd_far.at[to] if b else even
        return pltpu.make_async_remote_copy(
            src_ref=own_tiles.at[to], dst_ref=dst, send_sem=send_sem.at[tile_base + n],
            recv_sem=l_recv.at[24 + b], device_id=c_dev[RING[n]], device_id_type=MESH)

    @pl.when(mine)
    def _():
        for b in range(2):
            @pl.when(block == b)
            def _():
                full_l[my_rows, :] = l_ref[b]

                @pl.when(r == y)
                def _():
                    full_b[panel_rows, :] = b_ref[b]
                    full_a[x] = both_a[...]
        for s in range(SIDE * SIDE):
            @pl.when(t != s)
            def _():
                w = widths[s // SIDE]
                pltpu.make_async_remote_copy(
                    src_ref=l_ref.at[0, :, :w], dst_ref=full_l.at[pl.ds(s * row, row), :w],
                    send_sem=l_send.at[0, 0], recv_sem=l_recv.at[s], device_id=c_dev[1], device_id_type=MESH,
                ).wait_recv()
        for s in range(SIDE):
            @pl.when((x != s) | (r != y))
            def _():
                pltpu.make_async_remote_copy(
                    src_ref=b_ref.at[0], dst_ref=full_b.at[pl.ds(s * row, row)], send_sem=l_send.at[0, 4],
                    recv_sem=l_recv.at[16 + s], device_id=c_dev[1], device_id_type=MESH).wait_recv()
                pltpu.make_async_remote_copy(
                    src_ref=both_a, dst_ref=full_a.at[s], send_sem=l_send.at[0, 5],
                    recv_sem=l_recv.at[20 + s], device_id=c_dev[1], device_id_type=MESH).wait_recv()
        for j in range(0, node, 256):
            wide[:panel, j:j + 256] = -dot(full_b[:, j:], full_l[j:, j:j + 256])
            arrows_all[:, j:j + 256] = -dot(full_a[...].reshape(SIDE * 2 * own_arrow, node)[:, j:], full_l[j:, j:j + 256])
        for i in range(SIDE):
            lo = pl.multiple_of(2 * own_arrow * i + own_arrow * block, 8)
            wide[panel + own_arrow * i:panel + own_arrow * (i + 1)] = arrows_all[pl.ds(lo, own_arrow)]
        for i in range(SIDE):
            @pl.when(r == i)
            def _():
                lo = panel * i
                wide_d[...] = tdot(full_l[lo:, lo:lo + panel], full_l[lo:, :])
        for i in range(SIDE):
            own_tiles[i, :panel + arrow] = wide[:, panel * i:panel * (i + 1)].astype(BF)
            own_tiles[i, panel + arrow:] = wide_d[:, panel * i:panel * (i + 1)].astype(BF)
        for b in range(2):
            @pl.when(block == b)
            def _():
                for n in range(3):
                    tile_send(b, n).start()
                if b:
                    odd_far[c] = own_tiles[c]
                else:
                    even[...] = own_tiles[c]

    def get_cols(slot, when=None):
        return Gather(lambda i: cols.at[slot, i], False, when)

    def get_rows(slot, when=None):
        return Gather(lambda i: rows.at[slot, i], True, when)

    def product(left, slot):
        total = dot(left(0), cols[slot, 0])
        for k in range(1, SIDE):
            total += dot(left(k), cols[slot, k])
        return total

    def new_map(left, near, to, spread=True):
        total = product(left, near)
        arrows = total[panel:] + m_tile[near]
        m_tile[to] = arrows
        tile[to, :panel] = total[:panel].astype(BF)
        tile[to, panel:] = arrows.astype(BF)
        if spread:
            cols[to, r] = total[:panel].astype(BF)
            rows[to, c] = total[:panel].astype(BF)

    class Congruence:
        def __init__(self, index, when=None):
            self.index, self.base = index, take(3)
            late.append((when, self))

        def each(self, arriving):
            for n, d in enumerate(RING):
                at = r_at[SIDE - d] if arriving else r
                yield copy(part_out.at[self.index, r_at[d]], part_in.at[self.index, at], self.base + n, r_dev[d])

        def add(self, left, near, first):
            right = product(left, near).astype(BF)
            for s in range(SIDE):
                piece = tdot(rows[near, s], right)
                part_sum[s] = piece if first else part_sum[s] + piece

        def send(self):
            for s in range(SIDE):
                part_out[self.index, s] = part_sum[s].astype(BF)
            for move in self.each(False):
                move.start()
            part_own[self.index] = part_sum[r]

        def start(self, left, near):
            self.add(left, near, True)
            self.send()

        def finish(self, near, to):
            total = part_own[self.index] + q_tile[near]
            for move in self.each(True):
                move.wait_recv()
            for d in RING:
                total += part_in[self.index, r_at[d]].astype(F32)
            q_tile[to] = total
            q_send[to] = total.astype(BF)

    for b in (1, 0):
        @pl.when(c != 2 * core + b)
        def _():
            pltpu.make_async_remote_copy(
                src_ref=own_tiles.at[0], dst_ref=odd_far.at[c] if b else even, send_sem=send_sem.at[tile_base],
                recv_sem=l_recv.at[24 + b], device_id=c_dev[1], device_id_type=MESH).wait_recv()
    cols[EVEN, r] = even[:panel]
    rows[EVEN, c] = even[:panel]
    even_cols, even_rows, odd_cols = get_cols(EVEN), get_rows(EVEN), get_cols(ODD)
    odd_panel = Gather(lambda i: odd_far.at[i, pl.ds(0, panel + arrow)], True)
    odd_diags = Gather(lambda i: odd_far.at[i, pl.ds(panel + arrow, panel)], True)
    even_cols.start()
    odd_panel.start()
    odd_diags.start()
    even_rows.start()
    cols[ODD, r] = odd_far[c, :panel]
    m_tile[EVEN] = even[panel:panel + arrow].astype(F32)
    q_tile[EVEN] = even[panel + arrow:].astype(F32)
    m_tile[ODD] = odd_far[c, panel:panel + arrow].astype(F32)
    q_tile[ODD] = odd_far[c, panel + arrow:].astype(F32)
    even_cols.wait()
    odd_panel.wait()
    new_map(lambda k: odd_far[k, :panel + arrow], EVEN, PAIR)
    fan = take(8)

    def fan_copy(d, diag):
        src = q_send.at[PAIR] if diag else tile.at[PAIR]
        dst = far_diag.at[0, c] if diag else far_map.at[0, c]
        return copy(src, dst, fan + 4 * diag + d, dev(dcore=1, dc=d))

    def fan_wait(diag):
        for d in range(SIDE):
            at = c_at[-d]
            src = q_send.at[PAIR] if diag else tile.at[PAIR]
            dst = far_diag.at[0, at] if diag else far_map.at[0, at]
            copy(src, dst, fan + 4 * diag + d, dev(dcore=1, dc=d)).wait_recv()

    @pl.when(core == 1)
    def _():
        for d in FAN:
            fan_copy(d, 0).start()

    pair_cols, pair_rows = get_cols(PAIR), get_rows(PAIR)
    pair = Congruence(0)

    @pl.when(is_first)
    def _():
        pair_cols.start()

    odd_diags.wait()
    even_rows.wait()
    pair.start(lambda k: odd_far[k, panel + arrow:], EVEN)

    @pl.when(is_first)
    def _():
        pair_rows.start()

    for k in range(SIDE):
        rows[ODD, k] = odd_far[k, :panel]

    z_base = take(6)

    def z_map(n):
        steps = (1, 1, 2)[n]
        src = tile.at[TWO if n else PLANE]
        return steps, copy(src, far_map.at[n + 1, c], z_base + n, dev(dz=-steps))

    def z_diag(n):
        return n, copy(q_send.at[PLANE], far_diag.at[n, c], z_base + 2 + n, dev(dz=-n))

    def z_each(copies, do):
        for steps, move in copies:
            @pl.when(z >= steps)
            def _():
                do(move)

    last_base = take(8)

    def last_copy(far, to_core, diag):
        if far:
            src = q_send.at[FOUR] if diag else tile.at[FOUR, pl.ds(panel, arrow)]
            dst = b_diag.at[c] if diag else b_arrow.at[c]
        else:
            src = q_send.at[FOUR] if diag else tile.at[FOUR]
            dst = a_diag.at[c] if diag else a_map.at[c]
        return copy(src, dst, last_base + 4 * far + 2 * to_core + diag, dev(dz=-5 if far else -1, dcore=to_core))

    def last_each(diag, do):
        for far, steps in ((0, 1), (1, 5)):
            @pl.when(z >= steps)
            def _():
                for k in range(2):
                    do(last_copy(far, k, diag))

    def last_wait(far, diag):
        for k in range(2):
            @pl.when(core == k)
            def _():
                last_copy(far, k, diag).wait_recv()

    far_maps = [None] + [Gather(lambda i, n=n: far_map.at[n, i], True, is_first & has[m]) for n, m in ((1, 1), (2, 3), (3, 2))]
    far_diags = [None] + [Gather(lambda i, n=n: far_diag.at[n, i], True, is_first & has[n]) for n in (1, 2, 3)]
    triple_cols, triple_rows = get_cols(TRIPLE, is_first), get_rows(TRIPLE, is_first)
    near = (None, PLANE, TWO, THREE)
    scan_when = (None, is_first, is_first & has[2], is_first & has[3])
    scan_cols = [None] + [get_cols(near[n], scan_when[n]) for n in (1, 2, 3)]
    scan_rows = [None] + [get_rows(near[n], scan_when[n]) for n in (1, 2, 3)]
    plane, triple, scan = Congruence(2, is_first), Congruence(1, is_first), Congruence(3, is_first & has_a)
    get_am = Gather(lambda i: a_map.at[i], True, has_a)
    get_bm = Gather(lambda i: b_arrow.at[i], True, has_b)
    get_aq = Gather(lambda i: a_diag.at[i], True, has_a)
    get_bq = Gather(lambda i: b_diag.at[i], True, has_b)
    long_cols, long_rows = [get_cols(LONG + j, has_b) for j in range(2)], [get_rows(LONG + j, has_b) for j in range(2)]
    finals = (jnp.where(core == 0, PLANE, PAIR), jnp.where(core == 0, TRIPLE, ODD))

    @pl.when(core == 1)
    def _():
        pair.finish(EVEN, PAIR)
        for d in FAN:
            fan_copy(d, 1).start()
        pair_cols.start()
        odd_cols.start()
        pair_rows.start()
        pair_cols.wait()
        pair_rows.wait()
        odd_cols.wait()

    @pl.when(core == 0)
    def _():
        fan_wait(0)
        pair_cols.wait()
        new_map(lambda k: far_map[0, k], PAIR, PLANE)
        z_each([z_map(0)], lambda move: move.start())
        scan_cols[1].start()
        pair.finish(EVEN, PAIR)

        @pl.when(has[1])
        def _():
            z_map(0)[1].wait_recv()
            far_maps[1].start()

        scan_rows[1].start()
        pair_rows.wait()
        fan_wait(1)
        plane.start(lambda k: far_diag[0, k], PAIR)
        scan_cols[1].wait()

        @pl.when(has[1])
        def _():
            far_maps[1].wait()
            new_map(lambda k: far_map[1, k], PLANE, TWO)

        @pl.when(z + 1 == planes)
        def _():
            tile[TWO] = tile[PLANE]

        z_each([z_map(1), z_map(2)], lambda move: move.start())

        @pl.when(has[2])
        def _():
            scan_cols[2].start()

        odd_cols.start()
        plane.finish(PAIR, PLANE)
        z_each([z_diag(n) for n in (1, 2, 3)], lambda move: move.start())

        @pl.when(has[2])
        def _():
            scan_rows[2].start()

        odd_cols.wait()
        new_map(lambda k: far_map[0, k], ODD, TRIPLE)
        triple_cols.start()

        @pl.when(has[1])
        def _():
            z_map(1)[1].wait_recv()

        @pl.when(has[3])
        def _():
            far_maps[2].start()

        @pl.when(has[2])
        def _():
            z_map(2)[1].wait_recv()
            far_maps[3].start()

        triple.start(lambda k: far_diag[0, k], ODD)

        for n in (1, 2, 3):
            @pl.when(has[n])
            def _():
                z_diag(n)[1].wait_recv()
                far_diags[n].start()

        @pl.when(has[2])
        def _():
            scan_cols[2].wait()
            far_maps[3].wait()
            new_map(lambda k: far_map[3, k], TWO, FOUR, False)

        @pl.when(z + 2 >= planes)
        def _():
            tile[FOUR] = tile[TWO]

        last_each(0, lambda move: move.start())

        @pl.when(has[3])
        def _():
            far_maps[2].wait()
            new_map(lambda k: far_map[2, k], PLANE, THREE)
            scan_cols[3].start()
            scan_rows[3].start()

        triple_rows.start()
        scan_rows[1].wait()

        @pl.when(has[1])
        def _():
            far_diags[1].wait()
            scan.add(lambda k: far_diag[1, k], PLANE, True)

        @pl.when(has[2])
        def _():
            scan_rows[2].wait()
            far_diags[2].wait()
            scan.add(lambda k: far_diag[2, k], TWO, False)

        triple_cols.wait()

    @pl.when(has_a)
    def _():
        last_wait(0, 0)
        get_am.start()

    @pl.when(has_b)
    def _():
        last_wait(1, 0)
        get_bm.start()

    @pl.when((core == 0) & has_a)
    def _():
        @pl.when(has[3])
        def _():
            far_diags[3].wait()
            scan_cols[3].wait()
            scan_rows[3].wait()
            scan.add(lambda k: far_diag[3, k], THREE, False)
        scan.send()

    @pl.when((core == 0) & (z + 1 == planes))
    def _():
        q_send[FOUR] = q_send[PLANE]
        last_each(1, lambda move: move.start())

    @pl.when(has_a)
    def _():
        get_am.wait()
        for j in range(2):
            total = product(lambda k: a_map[k], finals[j])
            m_total[j] = total[panel:] + m_tile[finals[j]]

            @pl.when(has_b)
            def _():
                cols[LONG + j, r] = total[:panel].astype(BF)
                rows[LONG + j, c] = total[:panel].astype(BF)
                long_cols[j].start()

        @pl.when(has_b)
        def _():
            for j in range(2):
                long_rows[j].start()

    @pl.when(z + 1 == planes)
    def _():
        for j in range(2):
            m_total[j] = m_tile[finals[j]]

    @pl.when(core == 0)
    def _():
        @pl.when(has_a)
        def _():
            scan.finish(PLANE, FOUR)
            last_each(1, lambda move: move.start())
        triple.finish(ODD, TRIPLE)
        triple_rows.wait()

    @pl.when(has_a)
    def _():
        last_wait(0, 1)
        get_aq.start()

    @pl.when(has_b)
    def _():
        last_wait(1, 1)
        get_bq.start()

    @pl.when(has_b)
    def _():
        get_bm.wait()
        for j in range(2):
            long_cols[j].wait()
            m_total[j] += product(lambda k: b_arrow[k], LONG + j)

    get_mr, get_mc = [], []
    for j in range(2):
        m_row[j, c] = m_total[j].astype(BF)
        m_col[j, r] = m_total[j].astype(BF)
        get_mr.append(Gather(lambda i, j=j: m_row.at[j, i], True))
        get_mc.append(Gather(lambda i, j=j: m_col.at[j, i], False))
        get_mr[j].start()
        get_mc[j].start()

    @pl.when(has_a)
    def _():
        get_aq.wait()
        for j in range(2):
            weight[j] = product(lambda k: a_diag[k], finals[j]).astype(BF)

    x_base = take(2 * SIDE)

    def x_out(j, do):
        for sub in range(SIDE):
            @pl.when((r != y) | (x != sub))
            def _():
                do(pltpu.make_async_remote_copy(
                    src_ref=x_send.at[j, own_arrow * sub:own_arrow * (sub + 1)], dst_ref=x_in.at[j, c],
                    send_sem=send_sem.at[x_base + SIDE * j + sub], recv_sem=recv_sem.at[x_base + SIDE * j + c],
                    device_id=(chain, r * SIDE + sub), device_id_type=MESH))

    def x_wait(j):
        for i in range(SIDE):
            @pl.when((r != y) | (c != i))
            def _():
                copy(x_send.at[j, :own_arrow], x_in.at[j, i], x_base + SIDE * j + i, c_dev[1]).wait_recv()

    sigma_rows = sigma[pl.ds(pl.multiple_of(r * arrow, 8), arrow)]
    for j in range(2):
        get_mr[j].wait()
        get_mc[j].wait()
        x_send[j] = lax.dot_general(
            sigma_rows, m_col[j].reshape(SIDE * arrow, panel).astype(F32), (((1,), (0,)), ((), ())),
            precision=lax.Precision.HIGHEST, preferred_element_type=F32)

        @pl.when(r == y)
        def _():
            x_in[j, c] = x_send[j, pl.ds(pl.multiple_of(x * own_arrow, 8), own_arrow)]
        x_out(j, lambda move: move.start())

    @pl.when(has_b)
    def _():
        get_bq.wait()
        for j in range(2):
            long_rows[j].wait()
            weight[2 + j] = product(lambda k: b_diag[k], LONG + j).astype(BF)

    out_base = take(2 * len(OFFSETS))

    def out_each(j, arriving):
        for n, (dy, dx) in enumerate(OFFSETS):
            ty, tx = lax.rem(y + dy, SIDE), lax.rem(x + dx, SIDE)
            sy, sx = lax.rem(y + SIDE - dy, SIDE), lax.rem(x + SIDE - dx, SIDE)
            at = (jnp.where(core == 0, sy, sx), jnp.where(core == 0, sx, sy)) if arriving else (r, c)
            src = out_send.at[j, ty, pl.ds(pl.multiple_of(tx * row, 16), row)]
            yield copy(src, out_in.at[j, at[0], at[1]], out_base + len(OFFSETS) * j + n, near_by(dy, dx))

    for j in range(2):
        arrows = x_send[j].astype(BF)
        for s in range(SIDE):
            part_own[5] = tdot(m_row[j, s], arrows)

            @pl.when(has_a)
            def _():
                part_own[5] += tdot(rows[finals[j], s], weight[j])

            @pl.when(has_b)
            def _():
                part_own[5] += tdot(rows[LONG + j, s], weight[2 + j])

            @pl.when(r == s)
            def _():
                part_own[5] += q_tile[finals[j]]
            out_send[j, s] = part_own[5].astype(BF)
        out_in[j, r, c] = out_send[j, y, pl.ds(pl.multiple_of(x * row, 16), row)]
        for move in out_each(j, False):
            move.start()
    groups = {}
    for when, sender in late:
        groups.setdefault(id(when), (when, []))[1].append(sender)

    def all_sent(senders):
        for sender in senders:
            for move in sender.each(False):
                move.wait_send()

    for when, senders in groups.values():
        if when is None:
            all_sent(senders)
        else:
            pl.when(when)(lambda senders=senders: all_sent(senders))
    spread(lambda move: move.wait_send())

    @pl.when(mine)
    def _():
        for n in range(3):
            tile_send(0, n).wait_send()

    @pl.when(core == 1)
    def _():
        for d in FAN:
            fan_copy(d, 0).wait_send()
            fan_copy(d, 1).wait_send()

    @pl.when(core == 0)
    def _():
        z_each([z_map(n) for n in range(3)] + [z_diag(n) for n in (1, 2, 3)], lambda move: move.wait_send())
        last_each(0, lambda move: move.wait_send())
        last_each(1, lambda move: move.wait_send())

    for j in range(2):
        x_wait(j)
        for i in range(SIDE):
            arrow_ref[j, :, panel * i:panel * (i + 1)] = x_in[j, i]
        x_out(j, lambda move: move.wait_send())
    for j in range(2):
        for move in out_each(j, True):
            move.wait_recv()
        for i in range(SIDE):
            total = out_in[j, 0, i].astype(F32)
            for k in range(1, SIDE):
                total += out_in[j, k, i].astype(F32)
            diag_ref[j, :, panel * i:panel * (i + 1)] = total
    for j in range(2):
        for move in out_each(j, False):
            move.wait_send()


def solution(mesh):
    planes = mesh.shape["chain"] // 2

    def on_device(inverse_diag, sub_diag, arrow_rows, arrow_inverse):
        count, row, node = inverse_diag.shape
        own_arrow = arrow_rows.shape[1]
        panel, arrow = row * SIDE, own_arrow * SIDE
        vm = pltpu.VMEM
        scratch = [
            vm(inverse_diag.shape, BF), vm(sub_diag.shape, BF), vm(arrow_rows.shape, BF), vm(arrow_inverse.shape, BF),
            vm((node, node), BF), vm((panel, node), BF), vm((SIDE, 2 * own_arrow, node), BF), vm((2 * own_arrow, node), BF),
            vm((panel + arrow, node), F32), vm((panel, node), F32), vm((2 * arrow, node), F32),
            vm((SIDE, 2 * panel + arrow, panel), BF), vm((2 * panel + arrow, panel), BF),
            vm((SIDE, 2 * panel + arrow, panel), BF),
            vm((9, SIDE, panel, panel), BF), vm((9, SIDE, panel, panel), BF),
            vm((8, panel + arrow, panel), BF), vm((8, panel, panel), F32), vm((8, arrow, panel), F32),
            vm((4, SIDE, panel + arrow, panel), BF), vm((4, SIDE, panel, panel), BF),
            vm((5, SIDE, panel, panel), BF), vm((5, SIDE, panel, panel), BF), vm((6, panel, panel), F32),
            vm((SIDE, panel, panel), F32),
            vm((8, panel, panel), BF),
            vm((SIDE, panel + arrow, panel), BF), vm((SIDE, panel, panel), BF),
            vm((SIDE, arrow, panel), BF), vm((SIDE, panel, panel), BF),
            vm((2, SIDE, arrow, panel), BF), vm((2, SIDE, arrow, panel), BF), vm((2, arrow, panel), F32),
            vm((2, arrow, panel), F32), vm((2, SIDE, own_arrow, panel), F32),
            vm((4, panel, panel), BF), vm((2, SIDE, panel, panel), BF), vm((2, SIDE, SIDE, row, panel), BF),
            vm(arrow_inverse.shape, F32),
            pltpu.SemaphoreType.DMA((200,)), pltpu.SemaphoreType.DMA((200,)),
            pltpu.SemaphoreType.DMA((2, 6)), pltpu.SemaphoreType.DMA((26,)), pltpu.SemaphoreType.DMA((4,)),
        ]
        return pl.pallas_call(
            functools.partial(kernel, planes, (row, node, panel, own_arrow)),
            out_shape=(
                jax.ShapeDtypeStruct(inverse_diag.shape, F32),
                jax.ShapeDtypeStruct(arrow_rows.shape, F32),
            ),
            in_specs=[pl.BlockSpec(memory_space=pl.ANY)] * 4,
            out_specs=(pl.BlockSpec(memory_space=vm),) * 2,
            scratch_shapes=scratch,
            compiler_params=pltpu.CompilerParams(
                collective_id=0, has_side_effects=True, vmem_limit_bytes=62 << 20),
            name="selected_inverse",
        )(inverse_diag, sub_diag, arrow_rows, arrow_inverse)

    placed = P("chain", "tile", None)
    return jax.shard_map(
        on_device, mesh=mesh, in_specs=(placed, placed, placed, P()), out_specs=(placed, placed), check_vma=False)
```

```python
import functools
import jax
import jax.numpy as jnp
from jax import lax
from jax.experimental import pallas as pl
from jax.experimental.pallas import tpu as pltpu
from jax.sharding import PartitionSpec as P

MESH = pl.DeviceIdType.MESH
BF, F32 = jnp.bfloat16, jnp.float32
SIDE = 4
ODD, PAIR, PLANE, TRIPLE, EVEN, TWO, THREE, FOUR = range(8)
LONG = 7
OFFSETS = [(dy, dx) for dy in range(SIDE) for dx in range(SIDE) if dy or dx]
OFFSETS.sort(key=lambda o: min(o[0], 4 - o[0]) + min(o[1], 4 - o[1]))
RING = (1, 3, 2)
FAN = (2, 1, 3, 0)


def tdot(a, b):
    return lax.dot_general(a, b, (((0,), (0,)), ((), ())), preferred_element_type=F32)


def dot(a, b):
    return jnp.dot(a, b, preferred_element_type=F32)


def kernel(
    planes, sizes,
    l_in, b_in, a_in, z_in, diag_ref, arrow_ref,
    l_ref, b_ref, a_ref, z_ref, full_l, full_b, full_a, both_a, wide, wide_d, arrows_all, own_tiles, even, odd_far,
    cols, rows, tile, q_tile, m_tile, far_map, far_diag, part_out, part_in, part_own, part_sum, q_send,
    a_map, a_diag, b_arrow, b_diag, m_row, m_col, m_total, x_send, x_in, weight, last_sum, out_send, out_in, sigma,
    send_sem, recv_sem, l_send, l_recv, load_sem,
):
    row, node, panel, own_arrow = sizes
    arrow = own_arrow * SIDE
    chain = lax.axis_index("chain")
    t = lax.axis_index("tile")
    z, core = chain // 2, chain % 2
    y, x = t // SIDE, t % SIDE
    r, c = jnp.where(core == 0, y, x), jnp.where(core == 0, x, y)
    widths = [min(node, -(-panel * (i + 1) // 128) * 128) for i in range(SIDE)]
    loads = [pltpu.make_async_copy(src, dst, load_sem.at[n]) for n, (src, dst) in enumerate(
        ((l_in, l_ref), (b_in, b_ref), (a_in, a_ref), (z_in, z_ref)))]
    for load in loads:
        load.start()

    def place(core, r, c):
        return jnp.where(core == 0, r * SIDE + c, c * SIDE + r)

    def dev(dz=0, dcore=0, dr=0, dc=0):
        zz = lax.rem(z + dz + planes, planes)
        cc = lax.rem(core + dcore, 2)
        return (zz * 2 + cc, place(cc, lax.rem(r + dr, SIDE), lax.rem(c + dc, SIDE)))

    def near_by(dy, dx):
        return (chain, lax.rem(y + dy, SIDE) * SIDE + lax.rem(x + dx, SIDE))

    r_at, c_at = [lax.rem(r + d, SIDE) for d in range(SIDE)], [lax.rem(c + d, SIDE) for d in range(SIDE)]
    r_dev, c_dev = [dev(dr=d) for d in range(SIDE)], [dev(dc=d) for d in range(SIDE)]
    is_first = core == 0
    has = [None] + [z + n < planes for n in (1, 2, 3)]
    has_a, has_b = has[1], z + 5 < planes
    late = []

    used = [0]

    def take(n):
        used[0] += n
        assert used[0] <= send_sem.shape[0]
        return used[0] - n

    def copy(src, dst, sem, where):
        return pltpu.make_async_remote_copy(
            src_ref=src, dst_ref=dst, send_sem=send_sem.at[sem], recv_sem=recv_sem.at[sem],
            device_id=where, device_id_type=MESH)

    class Gather:
        def __init__(self, buf, along_c, when=None):
            self.buf, self.along_c, self.base = buf, along_c, take(3)
            late.append((when, self))

        def each(self, arriving):
            at, where = (c_at, c_dev) if self.along_c else (r_at, r_dev)
            for n, d in enumerate(RING):
                to = at[SIDE - d] if arriving else at[0]
                yield copy(self.buf(at[0]), self.buf(to), self.base + n, where[d])

        def start(self):
            for move in self.each(False):
                move.start()

        def wait(self):
            for move in self.each(True):
                move.wait_recv()

    barrier = pltpu.get_barrier_semaphore()
    group = [near_by(dy, dx) for dy, dx in OFFSETS]
    first = [dev(dcore=1, dc=d) for d in range(SIDE)] + [dev(dz=d) for d in (1, 2, 3, -3)]
    second = [dev(dz=d, dcore=1) for d in (1, -3)]
    for peer in group:
        pl.semaphore_signal(barrier, inc=1, device_id=peer, device_id_type=MESH)
    for k, others in enumerate((first, second)):
        @pl.when(core == k)
        def _():
            for peer in others:
                pl.semaphore_signal(barrier, inc=1, device_id=peer, device_id_type=MESH)

    my_rows = pl.ds(pl.multiple_of(t * row, 16), row)
    panel_rows = pl.ds(pl.multiple_of(x * row, 16), row)
    mine = c // 2 == core
    block = lax.rem(c, 2)
    for i in range(SIDE - 1):
        if widths[i] < node:
            full_l[panel * i:panel * (i + 1), widths[i]:] = jnp.zeros((panel, node - widths[i]), BF)
    for load in loads:
        load.wait()
    both_a[...] = jnp.concatenate([a_ref[0].astype(F32), a_ref[1].astype(F32)], axis=0).astype(BF)
    for k, extra in enumerate((6, SIDE)):
        @pl.when(core == k)
        def _():
            pl.semaphore_wait(barrier, len(group) + extra)

    def to_column(b, row):
        return (chain, place(core, row, 2 * core + b))

    def l_copy(b, dr, w):
        return pltpu.make_async_remote_copy(
            src_ref=l_ref.at[b, :, :w], dst_ref=full_l.at[my_rows, :w], send_sem=l_send.at[b, dr],
            recv_sem=l_recv.at[t], device_id=to_column(b, lax.rem(r + dr, SIDE)), device_id_type=MESH)

    def b_copy(b):
        return pltpu.make_async_remote_copy(
            src_ref=b_ref.at[b], dst_ref=full_b.at[panel_rows], send_sem=l_send.at[b, 4],
            recv_sem=l_recv.at[16 + x], device_id=to_column(b, y), device_id_type=MESH)

    def a_copy(b):
        return pltpu.make_async_remote_copy(
            src_ref=both_a, dst_ref=full_a.at[x], send_sem=l_send.at[b, 5],
            recv_sem=l_recv.at[20 + x], device_id=to_column(b, y), device_id_type=MESH)

    def spread(do):
        for b in range(2):
            for i in range(SIDE):
                @pl.when(y == i)
                def _():
                    for dr in (1, 3, 2):
                        do(l_copy(b, dr, widths[i]))

            @pl.when(c != 2 * core + b)
            def _():
                for i in range(SIDE):
                    @pl.when(y == i)
                    def _():
                        do(l_copy(b, 0, widths[i]))

            @pl.when((c != 2 * core + b) | (r != y))
            def _():
                do(b_copy(b))
                do(a_copy(b))

    spread(lambda move: move.start())
    sigma[...] = tdot(z_ref[...], z_ref[...])
    tile_base = take(3)

    def tile_send(b, n):
        to = c_at[RING[n]]
        dst = odd_far.at[to] if b else even
        return pltpu.make_async_remote_copy(
            src_ref=own_tiles.at[to], dst_ref=dst, send_sem=send_sem.at[tile_base + n],
            recv_sem=l_recv.at[24 + b], device_id=c_dev[RING[n]], device_id_type=MESH)

    @pl.when(mine)
    def _():
        for b in range(2):
            @pl.when(block == b)
            def _():
                full_l[my_rows, :] = l_ref[b]

                @pl.when(r == y)
                def _():
                    full_b[panel_rows, :] = b_ref[b]
                    full_a[x] = both_a[...]
        for s in range(SIDE * SIDE):
            @pl.when(t != s)
            def _():
                w = widths[s // SIDE]
                pltpu.make_async_remote_copy(
                    src_ref=l_ref.at[0, :, :w], dst_ref=full_l.at[pl.ds(s * row, row), :w],
                    send_sem=l_send.at[0, 0], recv_sem=l_recv.at[s], device_id=c_dev[1], device_id_type=MESH,
                ).wait_recv()
        for s in range(SIDE):
            @pl.when((x != s) | (r != y))
            def _():
                pltpu.make_async_remote_copy(
                    src_ref=b_ref.at[0], dst_ref=full_b.at[pl.ds(s * row, row)], send_sem=l_send.at[0, 4],
                    recv_sem=l_recv.at[16 + s], device_id=c_dev[1], device_id_type=MESH).wait_recv()
                pltpu.make_async_remote_copy(
                    src_ref=both_a, dst_ref=full_a.at[s], send_sem=l_send.at[0, 5],
                    recv_sem=l_recv.at[20 + s], device_id=c_dev[1], device_id_type=MESH).wait_recv()
        for j in range(0, node, 256):
            wide[:panel, j:j + 256] = -dot(full_b[:, j:], full_l[j:, j:j + 256])
            arrows_all[:, j:j + 256] = -dot(full_a[...].reshape(SIDE * 2 * own_arrow, node)[:, j:], full_l[j:, j:j + 256])
        for i in range(SIDE):
            lo = pl.multiple_of(2 * own_arrow * i + own_arrow * block, 8)
            wide[panel + own_arrow * i:panel + own_arrow * (i + 1)] = arrows_all[pl.ds(lo, own_arrow)]
        for i in range(SIDE):
            @pl.when(r == i)
            def _():
                lo = panel * i
                wide_d[...] = tdot(full_l[lo:, lo:lo + panel], full_l[lo:, :])
        for i in range(SIDE):
            own_tiles[i, :panel + arrow] = wide[:, panel * i:panel * (i + 1)].astype(BF)
            own_tiles[i, panel + arrow:] = wide_d[:, panel * i:panel * (i + 1)].astype(BF)
        for b in range(2):
            @pl.when(block == b)
            def _():
                for n in range(3):
                    tile_send(b, n).start()
                if b:
                    odd_far[c] = own_tiles[c]
                else:
                    even[...] = own_tiles[c]

    def get_cols(slot, when=None):
        return Gather(lambda i: cols.at[slot, i], False, when)

    def get_rows(slot, when=None):
        return Gather(lambda i: rows.at[slot, i], True, when)

    def product(left, slot):
        total = dot(left(0), cols[slot, 0])
        for k in range(1, SIDE):
            total += dot(left(k), cols[slot, k])
        return total

    def new_map(left, near, to, spread=True):
        total = product(left, near)
        arrows = total[panel:] + m_tile[near]
        m_tile[to] = arrows
        tile[to, :panel] = total[:panel].astype(BF)
        tile[to, panel:] = arrows.astype(BF)
        if spread:
            cols[to, r] = total[:panel].astype(BF)
            rows[to, c] = total[:panel].astype(BF)

    class Congruence:
        def __init__(self, index, when=None):
            self.index, self.base = index, take(3)
            late.append((when, self))

        def each(self, arriving):
            for n, d in enumerate(RING):
                at = r_at[SIDE - d] if arriving else r
                yield copy(part_out.at[self.index, r_at[d]], part_in.at[self.index, at], self.base + n, r_dev[d])

        def add(self, left, near, first):
            right = product(left, near).astype(BF)
            for s in range(SIDE):
                piece = tdot(rows[near, s], right)
                part_sum[s] = piece if first else part_sum[s] + piece

        def send(self):
            for s in range(SIDE):
                part_out[self.index, s] = part_sum[s].astype(BF)
            for move in self.each(False):
                move.start()
            part_own[self.index] = part_sum[r]

        def start(self, left, near):
            self.add(left, near, True)
            self.send()

        def finish(self, near, to):
            total = part_own[self.index] + q_tile[near]
            for move in self.each(True):
                move.wait_recv()
            for d in RING:
                total += part_in[self.index, r_at[d]].astype(F32)
            q_tile[to] = total
            q_send[to] = total.astype(BF)

    for b in (1, 0):
        @pl.when(c != 2 * core + b)
        def _():
            pltpu.make_async_remote_copy(
                src_ref=own_tiles.at[0], dst_ref=odd_far.at[c] if b else even, send_sem=send_sem.at[tile_base],
                recv_sem=l_recv.at[24 + b], device_id=c_dev[1], device_id_type=MESH).wait_recv()
    cols[EVEN, r] = even[:panel]
    rows[EVEN, c] = even[:panel]
    even_cols, even_rows, odd_cols = get_cols(EVEN), get_rows(EVEN), get_cols(ODD)
    odd_panel = Gather(lambda i: odd_far.at[i, pl.ds(0, panel + arrow)], True)
    odd_diags = Gather(lambda i: odd_far.at[i, pl.ds(panel + arrow, panel)], True)
    even_cols.start()
    odd_panel.start()
    odd_diags.start()
    even_rows.start()
    cols[ODD, r] = odd_far[c, :panel]
    m_tile[EVEN] = even[panel:panel + arrow].astype(F32)
    q_tile[EVEN] = even[panel + arrow:].astype(F32)
    m_tile[ODD] = odd_far[c, panel:panel + arrow].astype(F32)
    q_tile[ODD] = odd_far[c, panel + arrow:].astype(F32)
    even_cols.wait()
    odd_panel.wait()
    new_map(lambda k: odd_far[k, :panel + arrow], EVEN, PAIR)
    fan = take(8)

    def fan_copy(d, diag):
        src = q_send.at[PAIR] if diag else tile.at[PAIR]
        dst = far_diag.at[0, c] if diag else far_map.at[0, c]
        return copy(src, dst, fan + 4 * diag + d, dev(dcore=1, dc=d))

    def fan_wait(diag):
        for d in range(SIDE):
            at = c_at[-d]
            src = q_send.at[PAIR] if diag else tile.at[PAIR]
            dst = far_diag.at[0, at] if diag else far_map.at[0, at]
            copy(src, dst, fan + 4 * diag + d, dev(dcore=1, dc=d)).wait_recv()

    @pl.when(core == 1)
    def _():
        for d in FAN:
            fan_copy(d, 0).start()

    pair_cols, pair_rows = get_cols(PAIR), get_rows(PAIR)
    pair = Congruence(0)

    @pl.when(is_first)
    def _():
        pair_cols.start()

    odd_diags.wait()
    even_rows.wait()
    pair.start(lambda k: odd_far[k, panel + arrow:], EVEN)

    @pl.when(is_first)
    def _():
        pair_rows.start()

    for k in range(SIDE):
        rows[ODD, k] = odd_far[k, :panel]

    z_base = take(6)

    def z_map(n):
        steps = (1, 1, 2)[n]
        src = tile.at[TWO if n else PLANE]
        return steps, copy(src, far_map.at[n + 1, c], z_base + n, dev(dz=-steps))

    def z_diag(n):
        return n, copy(q_send.at[PLANE], far_diag.at[n, c], z_base + 2 + n, dev(dz=-n))

    def z_each(copies, do):
        for steps, move in copies:
            @pl.when(z >= steps)
            def _():
                do(move)

    last_base = take(8)

    def last_copy(far, to_core, diag):
        if far:
            src = q_send.at[FOUR] if diag else tile.at[FOUR, pl.ds(panel, arrow)]
            dst = b_diag.at[c] if diag else b_arrow.at[c]
        else:
            src = q_send.at[FOUR] if diag else tile.at[FOUR]
            dst = a_diag.at[c] if diag else a_map.at[c]
        return copy(src, dst, last_base + 4 * far + 2 * to_core + diag, dev(dz=-5 if far else -1, dcore=to_core))

    def last_each(diag, do):
        for far, steps in ((0, 1), (1, 5)):
            @pl.when(z >= steps)
            def _():
                for k in range(2):
                    do(last_copy(far, k, diag))

    def last_wait(far, diag):
        for k in range(2):
            @pl.when(core == k)
            def _():
                last_copy(far, k, diag).wait_recv()

    far_maps = [None] + [Gather(lambda i, n=n: far_map.at[n, i], True, is_first & has[m]) for n, m in ((1, 1), (2, 3), (3, 2))]
    far_diags = [None] + [Gather(lambda i, n=n: far_diag.at[n, i], True, is_first & has[n]) for n in (1, 2, 3)]
    triple_cols, triple_rows = get_cols(TRIPLE, is_first), get_rows(TRIPLE, is_first)
    near = (None, PLANE, TWO, THREE)
    scan_when = (None, is_first, is_first & has[2], is_first & has[3])
    scan_cols = [None] + [get_cols(near[n], scan_when[n]) for n in (1, 2, 3)]
    scan_rows = [None] + [get_rows(near[n], scan_when[n]) for n in (1, 2, 3)]
    plane, triple, scan = Congruence(2, is_first), Congruence(1, is_first), Congruence(3, is_first & has_a)
    get_am = Gather(lambda i: a_map.at[i], True, has_a)
    get_bm = Gather(lambda i: b_arrow.at[i], True, has_b)
    get_aq = Gather(lambda i: a_diag.at[i], True, has_a)
    get_bq = Gather(lambda i: b_diag.at[i], True, has_b)
    long_cols, long_rows = [get_cols(LONG + j, has_b) for j in range(2)], [get_rows(LONG + j, has_b) for j in range(2)]
    finals = (jnp.where(core == 0, PLANE, PAIR), jnp.where(core == 0, TRIPLE, ODD))

    @pl.when(core == 1)
    def _():
        pair.finish(EVEN, PAIR)
        for d in FAN:
            fan_copy(d, 1).start()
        pair_cols.start()
        odd_cols.start()
        pair_rows.start()
        pair_cols.wait()
        pair_rows.wait()
        odd_cols.wait()

    @pl.when(core == 0)
    def _():
        fan_wait(0)
        pair_cols.wait()
        new_map(lambda k: far_map[0, k], PAIR, PLANE)
        z_each([z_map(0)], lambda move: move.start())
        scan_cols[1].start()
        pair.finish(EVEN, PAIR)

        @pl.when(has[1])
        def _():
            z_map(0)[1].wait_recv()
            far_maps[1].start()

        scan_rows[1].start()
        pair_rows.wait()
        fan_wait(1)
        plane.start(lambda k: far_diag[0, k], PAIR)
        scan_cols[1].wait()

        @pl.when(has[1])
        def _():
            far_maps[1].wait()
            new_map(lambda k: far_map[1, k], PLANE, TWO)

        @pl.when(z + 1 == planes)
        def _():
            tile[TWO] = tile[PLANE]

        z_each([z_map(1), z_map(2)], lambda move: move.start())

        @pl.when(has[2])
        def _():
            scan_cols[2].start()

        odd_cols.start()
        plane.finish(PAIR, PLANE)
        z_each([z_diag(n) for n in (1, 2, 3)], lambda move: move.start())

        @pl.when(has[2])
        def _():
            scan_rows[2].start()

        odd_cols.wait()
        new_map(lambda k: far_map[0, k], ODD, TRIPLE)
        triple_cols.start()

        @pl.when(has[1])
        def _():
            z_map(1)[1].wait_recv()

        @pl.when(has[3])
        def _():
            far_maps[2].start()

        @pl.when(has[2])
        def _():
            z_map(2)[1].wait_recv()
            far_maps[3].start()

        triple.start(lambda k: far_diag[0, k], ODD)

        for n in (1, 2, 3):
            @pl.when(has[n])
            def _():
                z_diag(n)[1].wait_recv()
                far_diags[n].start()

        @pl.when(has[2])
        def _():
            scan_cols[2].wait()
            far_maps[3].wait()
            new_map(lambda k: far_map[3, k], TWO, FOUR, False)

        @pl.when(z + 2 >= planes)
        def _():
            tile[FOUR] = tile[TWO]

        last_each(0, lambda move: move.start())

        @pl.when(has[3])
        def _():
            far_maps[2].wait()
            new_map(lambda k: far_map[2, k], PLANE, THREE)
            scan_cols[3].start()
            scan_rows[3].start()

        triple_rows.start()
        scan_rows[1].wait()

        @pl.when(has[1])
        def _():
            far_diags[1].wait()
            scan.add(lambda k: far_diag[1, k], PLANE, True)

        @pl.when(has[2])
        def _():
            scan_rows[2].wait()
            far_diags[2].wait()
            scan.add(lambda k: far_diag[2, k], TWO, False)

        triple_cols.wait()

    @pl.when(has_a)
    def _():
        last_wait(0, 0)
        get_am.start()

    @pl.when(has_b)
    def _():
        last_wait(1, 0)
        get_bm.start()

    @pl.when((core == 0) & has_a)
    def _():
        @pl.when(has[3])
        def _():
            far_diags[3].wait()
            scan_cols[3].wait()
            scan_rows[3].wait()
            scan.add(lambda k: far_diag[3, k], THREE, False)
        scan.send()

    @pl.when((core == 0) & (z + 1 == planes))
    def _():
        q_send[FOUR] = q_send[PLANE]
        last_each(1, lambda move: move.start())

    @pl.when(has_a)
    def _():
        get_am.wait()
        for j in range(2):
            total = product(lambda k: a_map[k], finals[j])
            m_total[j] = total[panel:] + m_tile[finals[j]]

            @pl.when(has_b)
            def _():
                cols[LONG + j, r] = total[:panel].astype(BF)
                rows[LONG + j, c] = total[:panel].astype(BF)
                long_cols[j].start()

        @pl.when(has_b)
        def _():
            for j in range(2):
                long_rows[j].start()

    @pl.when(z + 1 == planes)
    def _():
        for j in range(2):
            m_total[j] = m_tile[finals[j]]

    @pl.when(core == 0)
    def _():
        @pl.when(has_a)
        def _():
            scan.finish(PLANE, FOUR)
            last_each(1, lambda move: move.start())
        triple.finish(ODD, TRIPLE)
        triple_rows.wait()

    @pl.when(has_a)
    def _():
        last_wait(0, 1)
        get_aq.start()

    @pl.when(has_b)
    def _():
        last_wait(1, 1)
        get_bq.start()

    @pl.when(has_b)
    def _():
        get_bm.wait()
        for j in range(2):
            long_cols[j].wait()
            m_total[j] += product(lambda k: b_arrow[k], LONG + j)

    get_mr, get_mc = [], []
    for j in range(2):
        m_row[j, c] = m_total[j].astype(BF)
        m_col[j, r] = m_total[j].astype(BF)
        get_mr.append(Gather(lambda i, j=j: m_row.at[j, i], True))
        get_mc.append(Gather(lambda i, j=j: m_col.at[j, i], False))
        get_mr[j].start()
        get_mc[j].start()

    x_base = take(2 * SIDE)

    def x_out(j, do):
        for sub in range(SIDE):
            @pl.when((r != y) | (x != sub))
            def _():
                do(pltpu.make_async_remote_copy(
                    src_ref=x_send.at[j, own_arrow * sub:own_arrow * (sub + 1)], dst_ref=x_in.at[j, c],
                    send_sem=send_sem.at[x_base + SIDE * j + sub], recv_sem=recv_sem.at[x_base + SIDE * j + c],
                    device_id=(chain, r * SIDE + sub), device_id_type=MESH))

    def x_wait(j):
        for i in range(SIDE):
            @pl.when((r != y) | (c != i))
            def _():
                copy(x_send.at[j, :own_arrow], x_in.at[j, i], x_base + SIDE * j + i, c_dev[1]).wait_recv()

    for j in range(2):
        @pl.when(has_a)
        def _():
            if j == 0:
                get_aq.wait()
            right = product(lambda k: a_diag[k], finals[j]).astype(BF)
            for s in range(SIDE):
                last_sum[j, s] = tdot(rows[finals[j], s], right)

        @pl.when(z + 1 == planes)
        def _():
            last_sum[j] = jnp.zeros((SIDE, panel, panel), F32)
        last_sum[j, r] += q_tile[finals[j]]

    sigma_rows = sigma[pl.ds(pl.multiple_of(r * arrow, 8), arrow)]
    for j in range(2):
        get_mr[j].wait()
        get_mc[j].wait()
        x_send[j] = lax.dot_general(
            sigma_rows, m_col[j].reshape(SIDE * arrow, panel).astype(F32), (((1,), (0,)), ((), ())),
            precision=lax.Precision.HIGHEST, preferred_element_type=F32)

        @pl.when(r == y)
        def _():
            x_in[j, c] = x_send[j, pl.ds(pl.multiple_of(x * own_arrow, 8), own_arrow)]
        x_out(j, lambda move: move.start())
        arrows = x_send[j].astype(BF)
        for s in range(SIDE):
            last_sum[j, s] += tdot(m_row[j, s], arrows)

    out_base = take(2 * SIDE * SIDE)

    def out_copy(j, i, dx):
        tx = lax.rem(x + dx, SIDE)
        src = out_send.at[j, r_at[i], pl.ds(pl.multiple_of(tx * row, 16), row)]
        sem = out_base + SIDE * SIDE * j
        return pltpu.make_async_remote_copy(
            src_ref=src, dst_ref=out_in.at[j, r, c], send_sem=send_sem.at[sem + SIDE * i + dx],
            recv_sem=recv_sem.at[sem + t], device_id=(chain, r_at[i] * SIDE + tx), device_id_type=MESH)

    def out_each(j, i, do):
        for dx in (1, 3, 2):
            do(out_copy(j, i, dx))

        @pl.when(r_at[i] != y)
        def _():
            do(out_copy(j, i, 0))

    @pl.when(has_b)
    def _():
        get_bq.wait()

    for j in range(2):
        @pl.when(has_b)
        def _():
            long_rows[j].wait()
            weight[...] = product(lambda k: b_diag[k], LONG + j).astype(BF)

        for i in (1, 2, 3, 0):
            s = r_at[i]

            @pl.when(has_b)
            def _():
                out_send[j, s] = (last_sum[j, s] + tdot(rows[LONG + j, s], weight[...])).astype(BF)

            @pl.when(z + 5 >= planes)
            def _():
                out_send[j, s] = last_sum[j, s].astype(BF)
            out_each(j, i, lambda move: move.start())
        out_in[j, r, c] = out_send[j, y, pl.ds(pl.multiple_of(x * row, 16), row)]

    groups = {}
    for when, sender in late:
        groups.setdefault(id(when), (when, []))[1].append(sender)

    def all_sent(senders):
        for sender in senders:
            for move in sender.each(False):
                move.wait_send()

    for when, senders in groups.values():
        if when is None:
            all_sent(senders)
        else:
            pl.when(when)(lambda senders=senders: all_sent(senders))
    spread(lambda move: move.wait_send())

    @pl.when(mine)
    def _():
        for n in range(3):
            tile_send(0, n).wait_send()

    @pl.when(core == 1)
    def _():
        for d in FAN:
            fan_copy(d, 0).wait_send()
            fan_copy(d, 1).wait_send()

    @pl.when(core == 0)
    def _():
        z_each([z_map(n) for n in range(3)] + [z_diag(n) for n in (1, 2, 3)], lambda move: move.wait_send())
        last_each(0, lambda move: move.wait_send())
        last_each(1, lambda move: move.wait_send())

    for j in range(2):
        x_wait(j)
        for i in range(SIDE):
            arrow_ref[j, :, panel * i:panel * (i + 1)] = x_in[j, i]
        x_out(j, lambda move: move.wait_send())
    for j in range(2):
        for sy in range(SIDE):
            for sx in range(SIDE):
                @pl.when(t != SIDE * sy + sx)
                def _():
                    at = (jnp.where(is_first, sy, sx), jnp.where(is_first, sx, sy))
                    copy(out_send.at[j, 0, :row], out_in.at[j, at[0], at[1]],
                         out_base + SIDE * SIDE * j + SIDE * sy + sx, c_dev[1]).wait_recv()
        for i in range(SIDE):
            total = out_in[j, 0, i].astype(F32)
            for k in range(1, SIDE):
                total += out_in[j, k, i].astype(F32)
            diag_ref[j, :, panel * i:panel * (i + 1)] = total
    for j in range(2):
        for i in range(SIDE):
            out_each(j, i, lambda move: move.wait_send())


def solution(mesh):
    planes = mesh.shape["chain"] // 2

    def on_device(inverse_diag, sub_diag, arrow_rows, arrow_inverse):
        count, row, node = inverse_diag.shape
        own_arrow = arrow_rows.shape[1]
        panel, arrow = row * SIDE, own_arrow * SIDE
        vm = pltpu.VMEM
        scratch = [
            vm(inverse_diag.shape, BF), vm(sub_diag.shape, BF), vm(arrow_rows.shape, BF), vm(arrow_inverse.shape, BF),
            vm((node, node), BF), vm((panel, node), BF), vm((SIDE, 2 * own_arrow, node), BF), vm((2 * own_arrow, node), BF),
            vm((panel + arrow, node), F32), vm((panel, node), F32), vm((2 * arrow, node), F32),
            vm((SIDE, 2 * panel + arrow, panel), BF), vm((2 * panel + arrow, panel), BF),
            vm((SIDE, 2 * panel + arrow, panel), BF),
            vm((9, SIDE, panel, panel), BF), vm((9, SIDE, panel, panel), BF),
            vm((8, panel + arrow, panel), BF), vm((8, panel, panel), F32), vm((8, arrow, panel), F32),
            vm((4, SIDE, panel + arrow, panel), BF), vm((4, SIDE, panel, panel), BF),
            vm((5, SIDE, panel, panel), BF), vm((5, SIDE, panel, panel), BF), vm((6, panel, panel), F32),
            vm((SIDE, panel, panel), F32),
            vm((8, panel, panel), BF),
            vm((SIDE, panel + arrow, panel), BF), vm((SIDE, panel, panel), BF),
            vm((SIDE, arrow, panel), BF), vm((SIDE, panel, panel), BF),
            vm((2, SIDE, arrow, panel), BF), vm((2, SIDE, arrow, panel), BF), vm((2, arrow, panel), F32),
            vm((2, arrow, panel), F32), vm((2, SIDE, own_arrow, panel), F32),
            vm((panel, panel), BF), vm((2, SIDE, panel, panel), F32), vm((2, SIDE, panel, panel), BF), vm((2, SIDE, SIDE, row, panel), BF),
            vm(arrow_inverse.shape, F32),
            pltpu.SemaphoreType.DMA((210,)), pltpu.SemaphoreType.DMA((210,)),
            pltpu.SemaphoreType.DMA((2, 6)), pltpu.SemaphoreType.DMA((26,)), pltpu.SemaphoreType.DMA((4,)),
        ]
        return pl.pallas_call(
            functools.partial(kernel, planes, (row, node, panel, own_arrow)),
            out_shape=(
                jax.ShapeDtypeStruct(inverse_diag.shape, F32),
                jax.ShapeDtypeStruct(arrow_rows.shape, F32),
            ),
            in_specs=[pl.BlockSpec(memory_space=pl.ANY)] * 4,
            out_specs=(pl.BlockSpec(memory_space=vm),) * 2,
            scratch_shapes=scratch,
            compiler_params=pltpu.CompilerParams(
                collective_id=0, has_side_effects=True, vmem_limit_bytes=62 << 20),
            name="selected_inverse",
        )(inverse_diag, sub_diag, arrow_rows, arrow_inverse)

    placed = P("chain", "tile", None)
    return jax.shard_map(
        on_device, mesh=mesh, in_specs=(placed, placed, placed, P()), out_specs=(placed, placed), check_vma=False)
```

```python
import functools
import jax
import jax.numpy as jnp
from jax import lax
from jax.experimental import pallas as pl
from jax.experimental.pallas import tpu as pltpu
from jax.sharding import PartitionSpec as P

MESH = pl.DeviceIdType.MESH
BF, F32 = jnp.bfloat16, jnp.float32
SIDE = 4
ODD, PAIR, PLANE, TRIPLE, EVEN, TWO, THREE, FOUR = range(8)
LONG = 7
OFFSETS = [(dy, dx) for dy in range(SIDE) for dx in range(SIDE) if dy or dx]
OFFSETS.sort(key=lambda o: min(o[0], 4 - o[0]) + min(o[1], 4 - o[1]))
RING = (2, 1, 3)
FAN = (2, 1, 3, 0)


def tdot(a, b):
    return lax.dot_general(a, b, (((0,), (0,)), ((), ())), preferred_element_type=F32)


def dot(a, b):
    return jnp.dot(a, b, preferred_element_type=F32)


def kernel(
    planes, sizes,
    l_in, b_in, a_in, z_in, diag_ref, arrow_ref,
    l_ref, b_ref, a_ref, z_ref, full_l, full_b, full_a, both_a, wide, wide_d, arrows_all, own_tiles, even, odd_far,
    cols, rows, tile, q_tile, m_tile, far_map, far_diag, part_out, part_in, part_own, part_sum, q_send,
    a_map, a_diag, b_arrow, b_diag, m_row, m_col, m_total, x_send, x_in, weight, last_sum, out_send, out_in, sigma,
    send_sem, recv_sem, l_send, l_recv, load_sem,
):
    row, node, panel, own_arrow = sizes
    arrow = own_arrow * SIDE
    chain = lax.axis_index("chain")
    t = lax.axis_index("tile")
    z, core = chain // 2, chain % 2
    y, x = t // SIDE, t % SIDE
    r, c = jnp.where(core == 0, y, x), jnp.where(core == 0, x, y)
    widths = [min(node, -(-panel * (i + 1) // 128) * 128) for i in range(SIDE)]
    loads = [pltpu.make_async_copy(src, dst, load_sem.at[n]) for n, (src, dst) in enumerate(
        ((l_in, l_ref), (b_in, b_ref), (a_in, a_ref), (z_in, z_ref)))]
    for load in loads:
        load.start()

    def place(core, r, c):
        return jnp.where(core == 0, r * SIDE + c, c * SIDE + r)

    def dev(dz=0, dcore=0, dr=0, dc=0):
        zz = lax.rem(z + dz + planes, planes)
        cc = lax.rem(core + dcore, 2)
        return (zz * 2 + cc, place(cc, lax.rem(r + dr, SIDE), lax.rem(c + dc, SIDE)))

    def near_by(dy, dx):
        return (chain, lax.rem(y + dy, SIDE) * SIDE + lax.rem(x + dx, SIDE))

    r_at, c_at = [lax.rem(r + d, SIDE) for d in range(SIDE)], [lax.rem(c + d, SIDE) for d in range(SIDE)]
    r_dev, c_dev = [dev(dr=d) for d in range(SIDE)], [dev(dc=d) for d in range(SIDE)]
    is_first = core == 0
    has = [None] + [z + n < planes for n in (1, 2, 3)]
    has_a, has_b = has[1], z + 5 < planes
    late = []

    used = [0]

    def take(n):
        used[0] += n
        assert used[0] <= send_sem.shape[0]
        return used[0] - n

    def copy(src, dst, sem, where):
        return pltpu.make_async_remote_copy(
            src_ref=src, dst_ref=dst, send_sem=send_sem.at[sem], recv_sem=recv_sem.at[sem],
            device_id=where, device_id_type=MESH)

    class Gather:
        def __init__(self, buf, along_c, when=None):
            self.buf, self.along_c, self.base = buf, along_c, take(3)
            late.append((when, self))

        def each(self, arriving):
            at, where = (c_at, c_dev) if self.along_c else (r_at, r_dev)
            for n, d in enumerate(RING):
                to = at[SIDE - d] if arriving else at[0]
                yield copy(self.buf(at[0]), self.buf(to), self.base + n, where[d])

        def start(self):
            for move in self.each(False):
                move.start()

        def wait(self):
            for move in self.each(True):
                move.wait_recv()

    barrier = pltpu.get_barrier_semaphore()
    group = [near_by(dy, dx) for dy, dx in OFFSETS]
    first = [dev(dcore=1, dc=d) for d in range(SIDE)] + [dev(dz=d) for d in (1, 2, 3, -3)]
    second = [dev(dz=d, dcore=1) for d in (1, -3)]
    for peer in group:
        pl.semaphore_signal(barrier, inc=1, device_id=peer, device_id_type=MESH)
    for k, others in enumerate((first, second)):
        @pl.when(core == k)
        def _():
            for peer in others:
                pl.semaphore_signal(barrier, inc=1, device_id=peer, device_id_type=MESH)

    my_rows = pl.ds(pl.multiple_of(t * row, 16), row)
    panel_rows = pl.ds(pl.multiple_of(x * row, 16), row)
    mine = c // 2 == core
    block = lax.rem(c, 2)
    for i in range(SIDE - 1):
        if widths[i] < node:
            full_l[panel * i:panel * (i + 1), widths[i]:] = jnp.zeros((panel, node - widths[i]), BF)
    for load in loads:
        load.wait()
    both_a[...] = jnp.concatenate([a_ref[0].astype(F32), a_ref[1].astype(F32)], axis=0).astype(BF)
    for k, extra in enumerate((6, SIDE)):
        @pl.when(core == k)
        def _():
            pl.semaphore_wait(barrier, len(group) + extra)

    def to_column(b, row):
        return (chain, place(core, row, 2 * core + b))

    def l_copy(b, dr, w):
        return pltpu.make_async_remote_copy(
            src_ref=l_ref.at[b, :, :w], dst_ref=full_l.at[my_rows, :w], send_sem=l_send.at[b, dr],
            recv_sem=l_recv.at[t], device_id=to_column(b, lax.rem(r + dr, SIDE)), device_id_type=MESH)

    def b_copy(b):
        return pltpu.make_async_remote_copy(
            src_ref=b_ref.at[b], dst_ref=full_b.at[panel_rows], send_sem=l_send.at[b, 4],
            recv_sem=l_recv.at[16 + x], device_id=to_column(b, y), device_id_type=MESH)

    def a_copy(b):
        return pltpu.make_async_remote_copy(
            src_ref=both_a, dst_ref=full_a.at[x], send_sem=l_send.at[b, 5],
            recv_sem=l_recv.at[20 + x], device_id=to_column(b, y), device_id_type=MESH)

    def spread(do):
        for b in range(2):
            for i in range(SIDE):
                @pl.when(y == i)
                def _():
                    for dr in (2, 1, 3):
                        do(l_copy(b, dr, widths[i]))

            @pl.when(c != 2 * core + b)
            def _():
                for i in range(SIDE):
                    @pl.when(y == i)
                    def _():
                        do(l_copy(b, 0, widths[i]))

            @pl.when((c != 2 * core + b) | (r != y))
            def _():
                do(b_copy(b))
                do(a_copy(b))

    spread(lambda move: move.start())
    sigma[...] = tdot(z_ref[...], z_ref[...])
    tile_base = take(6)
    tile_parts = (pl.ds(0, panel + arrow), pl.ds(panel + arrow, panel))

    def tile_send(b, n, part):
        to, at = c_at[RING[n]], tile_parts[part]
        dst = odd_far.at[to, at] if b else even.at[at]
        return pltpu.make_async_remote_copy(
            src_ref=own_tiles.at[to, at], dst_ref=dst, send_sem=send_sem.at[tile_base + 3 * part + n],
            recv_sem=l_recv.at[24 + 2 * part + b], device_id=c_dev[RING[n]], device_id_type=MESH)

    def tile_start(part):
        at = tile_parts[part]
        for b in range(2):
            @pl.when(block == b)
            def _():
                for n in range(3):
                    tile_send(b, n, part).start()
                if b:
                    odd_far[c, at] = own_tiles[c, at]
                else:
                    even[at] = own_tiles[c, at]

    def tile_wait(part):
        at = tile_parts[part]
        for b in (1, 0):
            @pl.when(c != 2 * core + b)
            def _():
                pltpu.make_async_remote_copy(
                    src_ref=own_tiles.at[0, at], dst_ref=odd_far.at[c, at] if b else even.at[at],
                    send_sem=send_sem.at[tile_base], recv_sem=l_recv.at[24 + 2 * part + b],
                    device_id=c_dev[1], device_id_type=MESH).wait_recv()

    @pl.when(mine)
    def _():
        for b in range(2):
            @pl.when(block == b)
            def _():
                full_l[my_rows, :] = l_ref[b]

                @pl.when(r == y)
                def _():
                    full_b[panel_rows, :] = b_ref[b]
                    full_a[x] = both_a[...]
        for s in range(SIDE * SIDE):
            @pl.when(t != s)
            def _():
                w = widths[s // SIDE]
                pltpu.make_async_remote_copy(
                    src_ref=l_ref.at[0, :, :w], dst_ref=full_l.at[pl.ds(s * row, row), :w],
                    send_sem=l_send.at[0, 0], recv_sem=l_recv.at[s], device_id=c_dev[1], device_id_type=MESH,
                ).wait_recv()
        for s in range(SIDE):
            @pl.when((x != s) | (r != y))
            def _():
                pltpu.make_async_remote_copy(
                    src_ref=b_ref.at[0], dst_ref=full_b.at[pl.ds(s * row, row)], send_sem=l_send.at[0, 4],
                    recv_sem=l_recv.at[16 + s], device_id=c_dev[1], device_id_type=MESH).wait_recv()
                pltpu.make_async_remote_copy(
                    src_ref=both_a, dst_ref=full_a.at[s], send_sem=l_send.at[0, 5],
                    recv_sem=l_recv.at[20 + s], device_id=c_dev[1], device_id_type=MESH).wait_recv()
        for j in range(0, node, 256):
            wide[:panel, j:j + 256] = -dot(full_b[:, j:], full_l[j:, j:j + 256])
            arrows_all[:, j:j + 256] = -dot(full_a[...].reshape(SIDE * 2 * own_arrow, node)[:, j:], full_l[j:, j:j + 256])
        for i in range(SIDE):
            lo = pl.multiple_of(2 * own_arrow * i + own_arrow * block, 8)
            wide[panel + own_arrow * i:panel + own_arrow * (i + 1)] = arrows_all[pl.ds(lo, own_arrow)]
        for i in range(SIDE):
            own_tiles[i, :panel + arrow] = wide[:, panel * i:panel * (i + 1)].astype(BF)
        tile_start(0)
        for i in range(SIDE):
            @pl.when(r == i)
            def _():
                lo = panel * i
                wide_d[...] = tdot(full_l[lo:, lo:lo + panel], full_l[lo:, :])
        for i in range(SIDE):
            own_tiles[i, panel + arrow:] = wide_d[:, panel * i:panel * (i + 1)].astype(BF)
        tile_start(1)

    def get_cols(slot, when=None):
        return Gather(lambda i: cols.at[slot, i], False, when)

    def get_rows(slot, when=None):
        return Gather(lambda i: rows.at[slot, i], True, when)

    def product(left, slot):
        total = dot(left(0), cols[slot, 0])
        for k in range(1, SIDE):
            total += dot(left(k), cols[slot, k])
        return total

    def new_map(left, near, to, spread=True):
        total = product(left, near)
        arrows = total[panel:] + m_tile[near]
        m_tile[to] = arrows
        tile[to, :panel] = total[:panel].astype(BF)
        tile[to, panel:] = arrows.astype(BF)
        if spread:
            cols[to, r] = total[:panel].astype(BF)
            rows[to, c] = total[:panel].astype(BF)

    class Congruence:
        def __init__(self, index, when=None):
            self.index, self.base = index, take(3)
            late.append((when, self))

        def each(self, arriving):
            for n, d in enumerate(RING):
                at = r_at[SIDE - d] if arriving else r
                yield copy(part_out.at[self.index, r_at[d]], part_in.at[self.index, at], self.base + n, r_dev[d])

        def add(self, left, near, first):
            right = product(left, near).astype(BF)
            for s in range(SIDE):
                piece = tdot(rows[near, s], right)
                part_sum[s] = piece if first else part_sum[s] + piece

        def send(self):
            for s in range(SIDE):
                part_out[self.index, s] = part_sum[s].astype(BF)
            for move in self.each(False):
                move.start()
            part_own[self.index] = part_sum[r]

        def start(self, left, near):
            self.add(left, near, True)
            self.send()

        def finish(self, near, to):
            total = part_own[self.index] + q_tile[near]
            for move in self.each(True):
                move.wait_recv()
            for d in RING:
                total += part_in[self.index, r_at[d]].astype(F32)
            q_tile[to] = total
            q_send[to] = total.astype(BF)

    tile_wait(0)
    cols[EVEN, r] = even[:panel]
    even_cols, even_rows, odd_cols = get_cols(EVEN), get_rows(EVEN), get_cols(ODD)
    odd_panel = Gather(lambda i: odd_far.at[i, pl.ds(0, panel + arrow)], True)
    odd_diags = Gather(lambda i: odd_far.at[i, pl.ds(panel + arrow, panel)], True)
    even_cols.start()
    odd_panel.start()
    rows[EVEN, c] = even[:panel]
    tile_wait(1)
    odd_diags.start()
    even_rows.start()
    cols[ODD, r] = odd_far[c, :panel]
    m_tile[EVEN] = even[panel:panel + arrow].astype(F32)
    q_tile[EVEN] = even[panel + arrow:].astype(F32)
    m_tile[ODD] = odd_far[c, panel:panel + arrow].astype(F32)
    q_tile[ODD] = odd_far[c, panel + arrow:].astype(F32)
    odd_cols.start()
    even_cols.wait()
    odd_panel.wait()
    new_map(lambda k: odd_far[k, :panel + arrow], EVEN, PAIR)
    fan = take(8)

    def fan_copy(d, diag):
        src = q_send.at[PAIR] if diag else tile.at[PAIR]
        dst = far_diag.at[0, c] if diag else far_map.at[0, c]
        return copy(src, dst, fan + 4 * diag + d, dev(dcore=1, dc=d))

    def fan_wait(diag):
        for d in range(SIDE):
            at = c_at[-d]
            src = q_send.at[PAIR] if diag else tile.at[PAIR]
            dst = far_diag.at[0, at] if diag else far_map.at[0, at]
            copy(src, dst, fan + 4 * diag + d, dev(dcore=1, dc=d)).wait_recv()

    @pl.when(core == 1)
    def _():
        for d in FAN:
            fan_copy(d, 0).start()

    pair_cols, pair_rows = get_cols(PAIR), get_rows(PAIR)
    pair = Congruence(0)

    @pl.when(is_first)
    def _():
        pair_cols.start()

    odd_diags.wait()
    even_rows.wait()
    pair.start(lambda k: odd_far[k, panel + arrow:], EVEN)

    @pl.when(is_first)
    def _():
        pair_rows.start()

    for k in range(SIDE):
        rows[ODD, k] = odd_far[k, :panel]

    z_base = take(6)

    def z_map(n):
        steps = (1, 1, 2)[n]
        src = tile.at[TWO if n else PLANE]
        return steps, copy(src, far_map.at[n + 1, c], z_base + n, dev(dz=-steps))

    def z_diag(n):
        return n, copy(q_send.at[PLANE], far_diag.at[n, c], z_base + 2 + n, dev(dz=-n))

    def z_each(copies, do):
        for steps, move in copies:
            @pl.when(z >= steps)
            def _():
                do(move)

    last_base = take(8)

    def last_copy(far, to_core, diag):
        if far:
            src = q_send.at[FOUR] if diag else tile.at[FOUR, pl.ds(panel, arrow)]
            dst = b_diag.at[c] if diag else b_arrow.at[c]
        else:
            src = q_send.at[FOUR] if diag else tile.at[FOUR]
            dst = a_diag.at[c] if diag else a_map.at[c]
        return copy(src, dst, last_base + 4 * far + 2 * to_core + diag, dev(dz=-5 if far else -1, dcore=to_core))

    def last_each(diag, do):
        for far, steps in ((1, 5), (0, 1)):
            @pl.when(z >= steps)
            def _():
                for k in range(2):
                    do(last_copy(far, k, diag))

    def last_wait(far, diag):
        for k in range(2):
            @pl.when(core == k)
            def _():
                last_copy(far, k, diag).wait_recv()

    far_maps = [None] + [Gather(lambda i, n=n: far_map.at[n, i], True, is_first & has[m]) for n, m in ((1, 1), (2, 3), (3, 2))]
    far_diags = [None] + [Gather(lambda i, n=n: far_diag.at[n, i], True, is_first & has[n]) for n in (1, 2, 3)]
    triple_cols, triple_rows = get_cols(TRIPLE, is_first), get_rows(TRIPLE, is_first)
    near = (None, PLANE, TWO, THREE)
    scan_when = (None, is_first, is_first & has[2], is_first & has[3])
    scan_cols = [None] + [get_cols(near[n], scan_when[n]) for n in (1, 2, 3)]
    scan_rows = [None] + [get_rows(near[n], scan_when[n]) for n in (1, 2, 3)]
    plane, triple, scan = Congruence(2, is_first), Congruence(1, is_first), Congruence(3, is_first & has_a)
    get_am = Gather(lambda i: a_map.at[i], True, has_a)
    get_bm = Gather(lambda i: b_arrow.at[i], True, has_b)
    get_aq = Gather(lambda i: a_diag.at[i], True, has_a)
    get_bq = Gather(lambda i: b_diag.at[i], True, has_b)
    long_cols, long_rows = [get_cols(LONG + j, has_b) for j in range(2)], [get_rows(LONG + j, has_b) for j in range(2)]
    finals = (jnp.where(core == 0, PLANE, PAIR), jnp.where(core == 0, TRIPLE, ODD))

    @pl.when(core == 1)
    def _():
        pair.finish(EVEN, PAIR)
        for d in FAN:
            fan_copy(d, 1).start()
        pair_cols.start()
        pair_rows.start()
        pair_cols.wait()
        pair_rows.wait()
        odd_cols.wait()

    @pl.when(core == 0)
    def _():
        fan_wait(0)
        pair_cols.wait()
        new_map(lambda k: far_map[0, k], PAIR, PLANE)
        z_each([z_map(0)], lambda move: move.start())
        scan_cols[1].start()
        pair.finish(EVEN, PAIR)

        @pl.when(has[1])
        def _():
            z_map(0)[1].wait_recv()
            far_maps[1].start()

        scan_rows[1].start()
        pair_rows.wait()
        fan_wait(1)
        plane.start(lambda k: far_diag[0, k], PAIR)
        scan_cols[1].wait()

        @pl.when(has[1])
        def _():
            far_maps[1].wait()
            new_map(lambda k: far_map[1, k], PLANE, TWO)

        @pl.when(z + 1 == planes)
        def _():
            tile[TWO] = tile[PLANE]

        z_each([z_map(2), z_map(1)], lambda move: move.start())

        @pl.when(has[2])
        def _():
            scan_cols[2].start()

        plane.finish(PAIR, PLANE)
        z_each([z_diag(n) for n in (3, 2, 1)], lambda move: move.start())

        @pl.when(has[2])
        def _():
            scan_rows[2].start()

        odd_cols.wait()
        new_map(lambda k: far_map[0, k], ODD, TRIPLE)
        triple_cols.start()

        @pl.when(has[1])
        def _():
            z_map(1)[1].wait_recv()

        @pl.when(has[3])
        def _():
            far_maps[2].start()

        @pl.when(has[2])
        def _():
            z_map(2)[1].wait_recv()
            far_maps[3].start()

        triple.start(lambda k: far_diag[0, k], ODD)

        for n in (1, 2, 3):
            @pl.when(has[n])
            def _():
                z_diag(n)[1].wait_recv()
                far_diags[n].start()

        @pl.when(has[2])
        def _():
            scan_cols[2].wait()
            far_maps[3].wait()
            new_map(lambda k: far_map[3, k], TWO, FOUR, False)

        @pl.when(z + 2 >= planes)
        def _():
            tile[FOUR] = tile[TWO]

        last_each(0, lambda move: move.start())

        @pl.when(has[3])
        def _():
            far_maps[2].wait()
            new_map(lambda k: far_map[2, k], PLANE, THREE)
            scan_cols[3].start()
            scan_rows[3].start()

        triple_rows.start()
        scan_rows[1].wait()

        @pl.when(has[1])
        def _():
            far_diags[1].wait()
            scan.add(lambda k: far_diag[1, k], PLANE, True)

        @pl.when(has[2])
        def _():
            scan_rows[2].wait()
            far_diags[2].wait()
            scan.add(lambda k: far_diag[2, k], TWO, False)

        triple_cols.wait()

    @pl.when(has_a)
    def _():
        last_wait(0, 0)
        get_am.start()

    @pl.when(has_b)
    def _():
        last_wait(1, 0)
        get_bm.start()

    @pl.when((core == 0) & has_a)
    def _():
        @pl.when(has[3])
        def _():
            far_diags[3].wait()
            scan_cols[3].wait()
            scan_rows[3].wait()
            scan.add(lambda k: far_diag[3, k], THREE, False)
        scan.send()

    @pl.when((core == 0) & (z + 1 == planes))
    def _():
        q_send[FOUR] = q_send[PLANE]
        last_each(1, lambda move: move.start())

    @pl.when(has_a)
    def _():
        get_am.wait()
        for j in range(2):
            total = product(lambda k: a_map[k], finals[j])
            m_total[j] = total[panel:] + m_tile[finals[j]]

            @pl.when(has_b)
            def _():
                cols[LONG + j, r] = total[:panel].astype(BF)
                rows[LONG + j, c] = total[:panel].astype(BF)
                long_cols[j].start()

        @pl.when(has_b)
        def _():
            for j in range(2):
                long_rows[j].start()

    @pl.when(z + 1 == planes)
    def _():
        for j in range(2):
            m_total[j] = m_tile[finals[j]]

    @pl.when(core == 0)
    def _():
        @pl.when(has_a)
        def _():
            scan.finish(PLANE, FOUR)
            last_each(1, lambda move: move.start())
        triple.finish(ODD, TRIPLE)
        triple_rows.wait()

    @pl.when(has_a)
    def _():
        last_wait(0, 1)
        get_aq.start()

    @pl.when(has_b)
    def _():
        last_wait(1, 1)
        get_bq.start()

    @pl.when(has_b)
    def _():
        get_bm.wait()
        for j in range(2):
            long_cols[j].wait()
            m_total[j] += product(lambda k: b_arrow[k], LONG + j)

    get_mr, get_mc = [], []
    for j in range(2):
        m_row[j, c] = m_total[j].astype(BF)
        m_col[j, r] = m_total[j].astype(BF)
        get_mr.append(Gather(lambda i, j=j: m_row.at[j, i], True))
        get_mc.append(Gather(lambda i, j=j: m_col.at[j, i], False))
        get_mr[j].start()
        get_mc[j].start()

    x_base = take(2 * SIDE)

    def x_out(j, do):
        for sub in range(SIDE):
            @pl.when((r != y) | (x != sub))
            def _():
                do(pltpu.make_async_remote_copy(
                    src_ref=x_send.at[j, own_arrow * sub:own_arrow * (sub + 1)], dst_ref=x_in.at[j, c],
                    send_sem=send_sem.at[x_base + SIDE * j + sub], recv_sem=recv_sem.at[x_base + SIDE * j + c],
                    device_id=(chain, r * SIDE + sub), device_id_type=MESH))

    def x_wait(j):
        for i in range(SIDE):
            @pl.when((r != y) | (c != i))
            def _():
                copy(x_send.at[j, :own_arrow], x_in.at[j, i], x_base + SIDE * j + i, c_dev[1]).wait_recv()

    for j in range(2):
        @pl.when(has_a)
        def _():
            if j == 0:
                get_aq.wait()
            right = product(lambda k: a_diag[k], finals[j]).astype(BF)
            for s in range(SIDE):
                last_sum[j, s] = tdot(rows[finals[j], s], right)

        @pl.when(z + 1 == planes)
        def _():
            last_sum[j] = jnp.zeros((SIDE, panel, panel), F32)
        last_sum[j, r] += q_tile[finals[j]]

    sigma_rows = sigma[pl.ds(pl.multiple_of(r * arrow, 8), arrow)]
    for j in range(2):
        get_mr[j].wait()
        get_mc[j].wait()
        x_send[j] = lax.dot_general(
            sigma_rows, m_col[j].reshape(SIDE * arrow, panel).astype(F32), (((1,), (0,)), ((), ())),
            precision=lax.Precision.HIGHEST, preferred_element_type=F32)

        @pl.when(r == y)
        def _():
            x_in[j, c] = x_send[j, pl.ds(pl.multiple_of(x * own_arrow, 8), own_arrow)]
        x_out(j, lambda move: move.start())
        arrows = x_send[j].astype(BF)
        for s in range(SIDE):
            last_sum[j, s] += tdot(m_row[j, s], arrows)

    out_base = take(2 * SIDE * SIDE)

    def out_copy(j, i, dx):
        tx = lax.rem(x + dx, SIDE)
        src = out_send.at[j, r_at[i], pl.ds(pl.multiple_of(tx * row, 16), row)]
        sem = out_base + SIDE * SIDE * j
        return pltpu.make_async_remote_copy(
            src_ref=src, dst_ref=out_in.at[j, r, c], send_sem=send_sem.at[sem + SIDE * i + dx],
            recv_sem=recv_sem.at[sem + t], device_id=(chain, r_at[i] * SIDE + tx), device_id_type=MESH)

    def out_each(j, i, do):
        for dx in (2, 1, 3):
            do(out_copy(j, i, dx))

        @pl.when(r_at[i] != y)
        def _():
            do(out_copy(j, i, 0))

    @pl.when(has_b)
    def _():
        get_bq.wait()

    for j in range(2):
        @pl.when(has_b)
        def _():
            long_rows[j].wait()
            weight[...] = product(lambda k: b_diag[k], LONG + j).astype(BF)

        for i in (2, 1, 3, 0):
            s = r_at[i]

            @pl.when(has_b)
            def _():
                out_send[j, s] = (last_sum[j, s] + tdot(rows[LONG + j, s], weight[...])).astype(BF)

            @pl.when(z + 5 >= planes)
            def _():
                out_send[j, s] = last_sum[j, s].astype(BF)
            out_each(j, i, lambda move: move.start())
        out_in[j, r, c] = out_send[j, y, pl.ds(pl.multiple_of(x * row, 16), row)]

    groups = {}
    for when, sender in late:
        groups.setdefault(id(when), (when, []))[1].append(sender)

    def all_sent(senders):
        for sender in senders:
            for move in sender.each(False):
                move.wait_send()

    for when, senders in groups.values():
        if when is None:
            all_sent(senders)
        else:
            pl.when(when)(lambda senders=senders: all_sent(senders))
    spread(lambda move: move.wait_send())

    @pl.when(mine)
    def _():
        for n in range(3):
            tile_send(0, n, 0).wait_send()
            tile_send(0, n, 1).wait_send()

    @pl.when(core == 1)
    def _():
        for d in FAN:
            fan_copy(d, 0).wait_send()
            fan_copy(d, 1).wait_send()

    @pl.when(core == 0)
    def _():
        z_each([z_map(n) for n in range(3)] + [z_diag(n) for n in (1, 2, 3)], lambda move: move.wait_send())
        last_each(0, lambda move: move.wait_send())
        last_each(1, lambda move: move.wait_send())

    for j in range(2):
        x_wait(j)
        for i in range(SIDE):
            arrow_ref[j, :, panel * i:panel * (i + 1)] = x_in[j, i]
        x_out(j, lambda move: move.wait_send())
    for j in range(2):
        for sy in range(SIDE):
            for sx in range(SIDE):
                @pl.when(t != SIDE * sy + sx)
                def _():
                    at = (jnp.where(is_first, sy, sx), jnp.where(is_first, sx, sy))
                    copy(out_send.at[j, 0, :row], out_in.at[j, at[0], at[1]],
                         out_base + SIDE * SIDE * j + SIDE * sy + sx, c_dev[1]).wait_recv()
        for i in range(SIDE):
            total = out_in[j, 0, i].astype(F32)
            for k in range(1, SIDE):
                total += out_in[j, k, i].astype(F32)
            diag_ref[j, :, panel * i:panel * (i + 1)] = total
    for j in range(2):
        for i in range(SIDE):
            out_each(j, i, lambda move: move.wait_send())


def solution(mesh):
    planes = mesh.shape["chain"] // 2

    def on_device(inverse_diag, sub_diag, arrow_rows, arrow_inverse):
        count, row, node = inverse_diag.shape
        own_arrow = arrow_rows.shape[1]
        panel, arrow = row * SIDE, own_arrow * SIDE
        vm = pltpu.VMEM
        scratch = [
            vm(inverse_diag.shape, BF), vm(sub_diag.shape, BF), vm(arrow_rows.shape, BF), vm(arrow_inverse.shape, BF),
            vm((node, node), BF), vm((panel, node), BF), vm((SIDE, 2 * own_arrow, node), BF), vm((2 * own_arrow, node), BF),
            vm((panel + arrow, node), F32), vm((panel, node), F32), vm((2 * arrow, node), F32),
            vm((SIDE, 2 * panel + arrow, panel), BF), vm((2 * panel + arrow, panel), BF),
            vm((SIDE, 2 * panel + arrow, panel), BF),
            vm((9, SIDE, panel, panel), BF), vm((9, SIDE, panel, panel), BF),
            vm((8, panel + arrow, panel), BF), vm((8, panel, panel), F32), vm((8, arrow, panel), F32),
            vm((4, SIDE, panel + arrow, panel), BF), vm((4, SIDE, panel, panel), BF),
            vm((5, SIDE, panel, panel), BF), vm((5, SIDE, panel, panel), BF), vm((6, panel, panel), F32),
            vm((SIDE, panel, panel), F32),
            vm((8, panel, panel), BF),
            vm((SIDE, panel + arrow, panel), BF), vm((SIDE, panel, panel), BF),
            vm((SIDE, arrow, panel), BF), vm((SIDE, panel, panel), BF),
            vm((2, SIDE, arrow, panel), BF), vm((2, SIDE, arrow, panel), BF), vm((2, arrow, panel), F32),
            vm((2, arrow, panel), F32), vm((2, SIDE, own_arrow, panel), F32),
            vm((panel, panel), BF), vm((2, SIDE, panel, panel), F32), vm((2, SIDE, panel, panel), BF), vm((2, SIDE, SIDE, row, panel), BF),
            vm(arrow_inverse.shape, F32),
            pltpu.SemaphoreType.DMA((210,)), pltpu.SemaphoreType.DMA((210,)),
            pltpu.SemaphoreType.DMA((2, 6)), pltpu.SemaphoreType.DMA((28,)), pltpu.SemaphoreType.DMA((4,)),
        ]
        return pl.pallas_call(
            functools.partial(kernel, planes, (row, node, panel, own_arrow)),
            out_shape=(
                jax.ShapeDtypeStruct(inverse_diag.shape, F32),
                jax.ShapeDtypeStruct(arrow_rows.shape, F32),
            ),
            in_specs=[pl.BlockSpec(memory_space=pl.ANY)] * 4,
            out_specs=(pl.BlockSpec(memory_space=vm),) * 2,
            scratch_shapes=scratch,
            compiler_params=pltpu.CompilerParams(
                collective_id=0, has_side_effects=True, vmem_limit_bytes=62 << 20),
            name="selected_inverse",
        )(inverse_diag, sub_diag, arrow_rows, arrow_inverse)

    placed = P("chain", "tile", None)
    return jax.shard_map(
        on_device, mesh=mesh, in_specs=(placed, placed, placed, P()), out_specs=(placed, placed), check_vma=False)
```

```python
import functools
import jax
import jax.numpy as jnp
from jax import lax
from jax.experimental import pallas as pl
from jax.experimental.pallas import tpu as pltpu
from jax.sharding import PartitionSpec as P

MESH = pl.DeviceIdType.MESH
BF, F32 = jnp.bfloat16, jnp.float32
SIDE = 4
ODD, PAIR, PLANE, TRIPLE, EVEN, TWO, THREE, FOUR = range(8)
LONG = 7
OFFSETS = [(dy, dx) for dy in range(SIDE) for dx in range(SIDE) if dy or dx]
OFFSETS.sort(key=lambda o: min(o[0], 4 - o[0]) + min(o[1], 4 - o[1]))
RING = (2, 1, 3)
FAN = (2, 1, 3, 0)


def tdot(a, b):
    return lax.dot_general(a, b, (((0,), (0,)), ((), ())), preferred_element_type=F32)


def dot(a, b):
    return jnp.dot(a, b, preferred_element_type=F32)


def kernel(
    planes, sizes,
    l_in, b_in, a_in, z_in, diag_ref, arrow_ref,
    l_ref, b_ref, a_ref, z_ref, full_l, full_b, full_a, both_a, wide, wide_d, arrows_all, own_tiles, even, odd_far,
    cols, rows, tile, q_tile, m_tile, far_map, far_diag, part_out, part_in, part_own, part_sum, q_send,
    a_map, a_diag, b_arrow, b_diag, m_row, m_col, m_total, x_send, x_in, weight, last_sum, out_send, out_in, sigma,
    send_sem, recv_sem, l_send, l_recv, load_sem,
):
    row, node, panel, own_arrow = sizes
    arrow = own_arrow * SIDE
    chain = lax.axis_index("chain")
    t = lax.axis_index("tile")
    z, core = chain // 2, chain % 2
    y, x = t // SIDE, t % SIDE
    r, c = jnp.where(core == 0, y, x), jnp.where(core == 0, x, y)
    widths = [min(node, -(-panel * (i + 1) // 128) * 128) for i in range(SIDE)]
    loads = [pltpu.make_async_copy(src, dst, load_sem.at[n]) for n, (src, dst) in enumerate(
        ((l_in, l_ref), (b_in, b_ref), (a_in, a_ref), (z_in, z_ref)))]
    for load in loads:
        load.start()

    def place(core, r, c):
        return jnp.where(core == 0, r * SIDE + c, c * SIDE + r)

    def dev(dz=0, dcore=0, dr=0, dc=0):
        zz = lax.rem(z + dz + planes, planes)
        cc = lax.rem(core + dcore, 2)
        return (zz * 2 + cc, place(cc, lax.rem(r + dr, SIDE), lax.rem(c + dc, SIDE)))

    def near_by(dy, dx):
        return (chain, lax.rem(y + dy, SIDE) * SIDE + lax.rem(x + dx, SIDE))

    r_at, c_at = [lax.rem(r + d, SIDE) for d in range(SIDE)], [lax.rem(c + d, SIDE) for d in range(SIDE)]
    r_dev, c_dev = [dev(dr=d) for d in range(SIDE)], [dev(dc=d) for d in range(SIDE)]
    is_first = core == 0
    has = [None] + [z + n < planes for n in (1, 2, 3)]
    has_a, has_b = has[1], z + 5 < planes
    late = []

    used = [0]

    def take(n):
        used[0] += n
        assert used[0] <= send_sem.shape[0]
        return used[0] - n

    def copy(src, dst, sem, where):
        return pltpu.make_async_remote_copy(
            src_ref=src, dst_ref=dst, send_sem=send_sem.at[sem], recv_sem=recv_sem.at[sem],
            device_id=where, device_id_type=MESH)

    class Gather:
        def __init__(self, buf, along_c, when=None):
            self.buf, self.along_c, self.base = buf, along_c, take(3)
            late.append((when, self))

        def each(self, arriving):
            at, where = (c_at, c_dev) if self.along_c else (r_at, r_dev)
            for n, d in enumerate(RING):
                to = at[SIDE - d] if arriving else at[0]
                yield copy(self.buf(at[0]), self.buf(to), self.base + n, where[d])

        def start(self):
            for move in self.each(False):
                move.start()

        def wait(self):
            for move in self.each(True):
                move.wait_recv()

    barrier = pltpu.get_barrier_semaphore()
    group = [near_by(dy, dx) for dy, dx in OFFSETS]
    first = [dev(dcore=1, dc=d) for d in range(SIDE)] + [dev(dz=d) for d in (1, 2, 3, -3)]
    second = [dev(dz=d, dcore=1) for d in (1, -3)]
    for peer in group:
        pl.semaphore_signal(barrier, inc=1, device_id=peer, device_id_type=MESH)
    for k, others in enumerate((first, second)):
        @pl.when(core == k)
        def _():
            for peer in others:
                pl.semaphore_signal(barrier, inc=1, device_id=peer, device_id_type=MESH)

    my_rows = pl.ds(pl.multiple_of(t * row, 16), row)
    panel_rows = pl.ds(pl.multiple_of(x * row, 16), row)
    mine = c // 2 == core
    block = lax.rem(c, 2)
    for i in range(SIDE - 1):
        if widths[i] < node:
            full_l[panel * i:panel * (i + 1), widths[i]:] = jnp.zeros((panel, node - widths[i]), BF)
    for load in loads:
        load.wait()
    both_a[...] = jnp.concatenate([a_ref[0].astype(F32), a_ref[1].astype(F32)], axis=0).astype(BF)
    for k, extra in enumerate((6, SIDE)):
        @pl.when(core == k)
        def _():
            pl.semaphore_wait(barrier, len(group) + extra)

    def to_column(b, row):
        return (chain, place(core, row, 2 * core + b))

    def l_copy(b, dr, w):
        return pltpu.make_async_remote_copy(
            src_ref=l_ref.at[b, :, :w], dst_ref=full_l.at[my_rows, :w], send_sem=l_send.at[b, dr],
            recv_sem=l_recv.at[t], device_id=to_column(b, lax.rem(r + dr, SIDE)), device_id_type=MESH)

    def b_copy(b):
        return pltpu.make_async_remote_copy(
            src_ref=b_ref.at[b], dst_ref=full_b.at[panel_rows], send_sem=l_send.at[b, 4],
            recv_sem=l_recv.at[16 + x], device_id=to_column(b, y), device_id_type=MESH)

    def a_copy(b):
        return pltpu.make_async_remote_copy(
            src_ref=both_a, dst_ref=full_a.at[x], send_sem=l_send.at[b, 5],
            recv_sem=l_recv.at[20 + x], device_id=to_column(b, y), device_id_type=MESH)

    def spread(do):
        for b in range(2):
            for i in range(SIDE):
                @pl.when(y == i)
                def _():
                    for dr in (2, 1, 3):
                        do(l_copy(b, dr, widths[i]))

            @pl.when(c != 2 * core + b)
            def _():
                for i in range(SIDE):
                    @pl.when(y == i)
                    def _():
                        do(l_copy(b, 0, widths[i]))

            @pl.when((c != 2 * core + b) | (r != y))
            def _():
                do(b_copy(b))
                do(a_copy(b))

    spread(lambda move: move.start())
    sigma[...] = tdot(z_ref[...], z_ref[...])
    tile_base = take(6)
    tile_parts = (pl.ds(0, panel + arrow), pl.ds(panel + arrow, panel))

    def tile_send(b, n, part):
        to, at = c_at[RING[n]], tile_parts[part]
        dst = odd_far.at[to, at] if b else even.at[at]
        return pltpu.make_async_remote_copy(
            src_ref=own_tiles.at[to, at], dst_ref=dst, send_sem=send_sem.at[tile_base + 3 * part + n],
            recv_sem=l_recv.at[24 + 2 * part + b], device_id=c_dev[RING[n]], device_id_type=MESH)

    def tile_start(part):
        at = tile_parts[part]
        for b in range(2):
            @pl.when(block == b)
            def _():
                for n in range(3):
                    tile_send(b, n, part).start()
                if b:
                    odd_far[c, at] = own_tiles[c, at]
                else:
                    even[at] = own_tiles[c, at]

    def tile_wait(part):
        at = tile_parts[part]
        for b in (1, 0):
            @pl.when(c != 2 * core + b)
            def _():
                pltpu.make_async_remote_copy(
                    src_ref=own_tiles.at[0, at], dst_ref=odd_far.at[c, at] if b else even.at[at],
                    send_sem=send_sem.at[tile_base], recv_sem=l_recv.at[24 + 2 * part + b],
                    device_id=c_dev[1], device_id_type=MESH).wait_recv()

    @pl.when(mine)
    def _():
        for b in range(2):
            @pl.when(block == b)
            def _():
                full_l[my_rows, :] = l_ref[b]

                @pl.when(r == y)
                def _():
                    full_b[panel_rows, :] = b_ref[b]
                    full_a[x] = both_a[...]
        for s in range(SIDE * SIDE):
            @pl.when(t != s)
            def _():
                w = widths[s // SIDE]
                pltpu.make_async_remote_copy(
                    src_ref=l_ref.at[0, :, :w], dst_ref=full_l.at[pl.ds(s * row, row), :w],
                    send_sem=l_send.at[0, 0], recv_sem=l_recv.at[s], device_id=c_dev[1], device_id_type=MESH,
                ).wait_recv()
        for s in range(SIDE):
            @pl.when((x != s) | (r != y))
            def _():
                pltpu.make_async_remote_copy(
                    src_ref=b_ref.at[0], dst_ref=full_b.at[pl.ds(s * row, row)], send_sem=l_send.at[0, 4],
                    recv_sem=l_recv.at[16 + s], device_id=c_dev[1], device_id_type=MESH).wait_recv()
                pltpu.make_async_remote_copy(
                    src_ref=both_a, dst_ref=full_a.at[s], send_sem=l_send.at[0, 5],
                    recv_sem=l_recv.at[20 + s], device_id=c_dev[1], device_id_type=MESH).wait_recv()
        for j in range(0, node, 256):
            wide[:panel, j:j + 256] = -dot(full_b[:, j:], full_l[j:, j:j + 256])
            arrows_all[:, j:j + 256] = -dot(full_a[...].reshape(SIDE * 2 * own_arrow, node)[:, j:], full_l[j:, j:j + 256])
        for i in range(SIDE):
            lo = pl.multiple_of(2 * own_arrow * i + own_arrow * block, 8)
            wide[panel + own_arrow * i:panel + own_arrow * (i + 1)] = arrows_all[pl.ds(lo, own_arrow)]
        for i in range(SIDE):
            own_tiles[i, :panel + arrow] = wide[:, panel * i:panel * (i + 1)].astype(BF)
        tile_start(0)
        for i in range(SIDE):
            @pl.when(r == i)
            def _():
                lo = panel * i
                wide_d[...] = tdot(full_l[lo:, lo:lo + panel], full_l[lo:, :])
        for i in range(SIDE):
            own_tiles[i, panel + arrow:] = wide_d[:, panel * i:panel * (i + 1)].astype(BF)
        tile_start(1)

    def get_cols(slot, when=None):
        return Gather(lambda i: cols.at[slot, i], False, when)

    def get_rows(slot, when=None):
        return Gather(lambda i: rows.at[slot, i], True, when)

    def product(left, slot):
        total = dot(left(0), cols[slot, 0])
        for k in range(1, SIDE):
            total += dot(left(k), cols[slot, k])
        return total

    def new_map(left, near, to, spread=True):
        total = product(left, near)
        arrows = total[panel:] + m_tile[near]
        m_tile[to] = arrows
        tile[to, :panel] = total[:panel].astype(BF)
        tile[to, panel:] = arrows.astype(BF)
        if spread:
            cols[to, r] = total[:panel].astype(BF)
            rows[to, c] = total[:panel].astype(BF)

    class Congruence:
        def __init__(self, index, when=None):
            self.index, self.base = index, take(3)
            late.append((when, self))

        def each(self, arriving):
            for n, d in enumerate(RING):
                at = r_at[SIDE - d] if arriving else r
                yield copy(part_out.at[self.index, r_at[d]], part_in.at[self.index, at], self.base + n, r_dev[d])

        def add(self, left, near, first):
            right = product(left, near).astype(BF)
            for s in range(SIDE):
                piece = tdot(rows[near, s], right)
                part_sum[s] = piece if first else part_sum[s] + piece

        def send(self):
            for s in range(SIDE):
                part_out[self.index, s] = part_sum[s].astype(BF)
            for move in self.each(False):
                move.start()
            part_own[self.index] = part_sum[r]

        def start(self, left, near):
            self.add(left, near, True)
            self.send()

        def finish(self, near, to):
            total = part_own[self.index] + q_tile[near]
            for move in self.each(True):
                move.wait_recv()
            for d in RING:
                total += part_in[self.index, r_at[d]].astype(F32)
            q_tile[to] = total
            q_send[to] = total.astype(BF)

    tile_wait(0)
    cols[EVEN, r] = even[:panel]
    even_cols, even_rows, odd_cols = get_cols(EVEN), get_rows(EVEN), get_cols(ODD)
    odd_panel = Gather(lambda i: odd_far.at[i, pl.ds(0, panel + arrow)], True)
    odd_diags = Gather(lambda i: odd_far.at[i, pl.ds(panel + arrow, panel)], True)
    even_cols.start()
    odd_panel.start()
    rows[EVEN, c] = even[:panel]
    tile_wait(1)
    odd_diags.start()
    even_rows.start()
    cols[ODD, r] = odd_far[c, :panel]
    m_tile[EVEN] = even[panel:panel + arrow].astype(F32)
    q_tile[EVEN] = even[panel + arrow:].astype(F32)
    m_tile[ODD] = odd_far[c, panel:panel + arrow].astype(F32)
    q_tile[ODD] = odd_far[c, panel + arrow:].astype(F32)
    even_cols.wait()
    odd_panel.wait()
    new_map(lambda k: odd_far[k, :panel + arrow], EVEN, PAIR)
    fan = take(8)

    def fan_copy(d, diag):
        src = q_send.at[PAIR] if diag else tile.at[PAIR]
        dst = far_diag.at[0, c] if diag else far_map.at[0, c]
        return copy(src, dst, fan + 4 * diag + d, dev(dcore=1, dc=d))

    def fan_wait(diag):
        for d in range(SIDE):
            at = c_at[-d]
            src = q_send.at[PAIR] if diag else tile.at[PAIR]
            dst = far_diag.at[0, at] if diag else far_map.at[0, at]
            copy(src, dst, fan + 4 * diag + d, dev(dcore=1, dc=d)).wait_recv()

    @pl.when(core == 1)
    def _():
        for d in FAN:
            fan_copy(d, 0).start()

    pair_cols, pair_rows = get_cols(PAIR), get_rows(PAIR)
    pair = Congruence(0)

    @pl.when(is_first)
    def _():
        pair_cols.start()

    odd_diags.wait()
    even_rows.wait()
    pair.start(lambda k: odd_far[k, panel + arrow:], EVEN)

    @pl.when(is_first)
    def _():
        pair_rows.start()

    for k in range(SIDE):
        rows[ODD, k] = odd_far[k, :panel]

    z_base = take(6)

    def z_map(n):
        steps = (1, 1, 2)[n]
        src = tile.at[TWO if n else PLANE]
        return steps, copy(src, far_map.at[n + 1, c], z_base + n, dev(dz=-steps))

    def z_diag(n):
        return n, copy(q_send.at[PLANE], far_diag.at[n, c], z_base + 2 + n, dev(dz=-n))

    def z_each(copies, do):
        for steps, move in copies:
            @pl.when(z >= steps)
            def _():
                do(move)

    last_base = take(8)

    def last_copy(far, to_core, diag):
        if far:
            src = q_send.at[FOUR] if diag else tile.at[FOUR, pl.ds(panel, arrow)]
            dst = b_diag.at[c] if diag else b_arrow.at[c]
        else:
            src = q_send.at[FOUR] if diag else tile.at[FOUR]
            dst = a_diag.at[c] if diag else a_map.at[c]
        return copy(src, dst, last_base + 4 * far + 2 * to_core + diag, dev(dz=-5 if far else -1, dcore=to_core))

    def last_each(diag, do):
        for far, steps in ((1, 5), (0, 1)):
            @pl.when(z >= steps)
            def _():
                for k in range(2):
                    do(last_copy(far, k, diag))

    def last_wait(far, diag):
        for k in range(2):
            @pl.when(core == k)
            def _():
                last_copy(far, k, diag).wait_recv()

    far_maps = [None] + [Gather(lambda i, n=n: far_map.at[n, i], True, is_first & has[m]) for n, m in ((1, 1), (2, 3), (3, 2))]
    far_diags = [None] + [Gather(lambda i, n=n: far_diag.at[n, i], True, is_first & has[n]) for n in (1, 2, 3)]
    triple_cols, triple_rows = get_cols(TRIPLE, is_first), get_rows(TRIPLE, is_first)
    near = (None, PLANE, TWO, THREE)
    scan_when = (None, is_first, is_first & has[2], is_first & has[3])
    scan_cols = [None] + [get_cols(near[n], scan_when[n]) for n in (1, 2, 3)]
    scan_rows = [None] + [get_rows(near[n], scan_when[n]) for n in (1, 2, 3)]
    plane, triple, scan = Congruence(2, is_first), Congruence(1, is_first), Congruence(3, is_first & has_a)
    get_am = Gather(lambda i: a_map.at[i], True, has_a)
    get_bm = Gather(lambda i: b_arrow.at[i], True, has_b)
    get_aq = Gather(lambda i: a_diag.at[i], True, has_a)
    get_bq = Gather(lambda i: b_diag.at[i], True, has_b)
    long_cols, long_rows = [get_cols(LONG + j, has_b) for j in range(2)], [get_rows(LONG + j, has_b) for j in range(2)]
    finals = (jnp.where(core == 0, PLANE, PAIR), jnp.where(core == 0, TRIPLE, ODD))

    @pl.when(core == 1)
    def _():
        pair.finish(EVEN, PAIR)
        for d in FAN:
            fan_copy(d, 1).start()
        pair_cols.start()
        odd_cols.start()
        pair_rows.start()
        pair_cols.wait()
        pair_rows.wait()
        odd_cols.wait()

    @pl.when(core == 0)
    def _():
        fan_wait(0)
        pair_cols.wait()
        new_map(lambda k: far_map[0, k], PAIR, PLANE)
        z_each([z_map(0)], lambda move: move.start())
        scan_cols[1].start()
        pair.finish(EVEN, PAIR)

        @pl.when(has[1])
        def _():
            z_map(0)[1].wait_recv()
            far_maps[1].start()

        scan_rows[1].start()
        pair_rows.wait()
        fan_wait(1)
        plane.start(lambda k: far_diag[0, k], PAIR)
        scan_cols[1].wait()

        @pl.when(has[1])
        def _():
            far_maps[1].wait()
            new_map(lambda k: far_map[1, k], PLANE, TWO)

        @pl.when(z + 1 == planes)
        def _():
            tile[TWO] = tile[PLANE]

        z_each([z_map(2), z_map(1)], lambda move: move.start())

        @pl.when(has[2])
        def _():
            scan_cols[2].start()

        odd_cols.start()
        plane.finish(PAIR, PLANE)
        z_each([z_diag(n) for n in (3, 2, 1)], lambda move: move.start())

        @pl.when(has[2])
        def _():
            scan_rows[2].start()

        odd_cols.wait()
        new_map(lambda k: far_map[0, k], ODD, TRIPLE)
        triple_cols.start()

        @pl.when(has[1])
        def _():
            z_map(1)[1].wait_recv()

        @pl.when(has[3])
        def _():
            far_maps[2].start()

        @pl.when(has[2])
        def _():
            z_map(2)[1].wait_recv()
            far_maps[3].start()

        triple.start(lambda k: far_diag[0, k], ODD)

        for n in (1, 2, 3):
            @pl.when(has[n])
            def _():
                z_diag(n)[1].wait_recv()
                far_diags[n].start()

        @pl.when(has[2])
        def _():
            scan_cols[2].wait()
            far_maps[3].wait()
            new_map(lambda k: far_map[3, k], TWO, FOUR, False)

        @pl.when(z + 2 >= planes)
        def _():
            tile[FOUR] = tile[TWO]

        last_each(0, lambda move: move.start())

        @pl.when(has[3])
        def _():
            far_maps[2].wait()
            new_map(lambda k: far_map[2, k], PLANE, THREE)
            scan_cols[3].start()
            scan_rows[3].start()

        triple_rows.start()
        scan_rows[1].wait()

        @pl.when(has[1])
        def _():
            far_diags[1].wait()
            scan.add(lambda k: far_diag[1, k], PLANE, True)

        @pl.when(has[2])
        def _():
            scan_rows[2].wait()
            far_diags[2].wait()
            scan.add(lambda k: far_diag[2, k], TWO, False)

        triple_cols.wait()

    @pl.when(has_a)
    def _():
        last_wait(0, 0)
        get_am.start()

    @pl.when(has_b)
    def _():
        last_wait(1, 0)
        get_bm.start()

    @pl.when((core == 0) & has_a)
    def _():
        @pl.when(has[3])
        def _():
            far_diags[3].wait()
            scan_cols[3].wait()
            scan_rows[3].wait()
            scan.add(lambda k: far_diag[3, k], THREE, False)
        scan.send()

    @pl.when((core == 0) & (z + 1 == planes))
    def _():
        q_send[FOUR] = q_send[PLANE]
        last_each(1, lambda move: move.start())

    @pl.when(has_a)
    def _():
        get_am.wait()
        for j in range(2):
            total = product(lambda k: a_map[k], finals[j])
            m_total[j] = total[panel:] + m_tile[finals[j]]

            @pl.when(has_b)
            def _():
                cols[LONG + j, r] = total[:panel].astype(BF)
                rows[LONG + j, c] = total[:panel].astype(BF)
                long_cols[j].start()

        @pl.when(has_b)
        def _():
            for j in range(2):
                long_rows[j].start()

    @pl.when(z + 1 == planes)
    def _():
        for j in range(2):
            m_total[j] = m_tile[finals[j]]

    @pl.when(core == 0)
    def _():
        @pl.when(has_a)
        def _():
            scan.finish(PLANE, FOUR)
            last_each(1, lambda move: move.start())
        triple.finish(ODD, TRIPLE)
        triple_rows.wait()

    @pl.when(has_a)
    def _():
        last_wait(0, 1)
        get_aq.start()

    @pl.when(has_b)
    def _():
        last_wait(1, 1)
        get_bq.start()

    @pl.when(has_b)
    def _():
        get_bm.wait()
        for j in range(2):
            long_cols[j].wait()
            m_total[j] += product(lambda k: b_arrow[k], LONG + j)

    get_mr, get_mc = [], []
    for j in range(2):
        m_row[j, c] = m_total[j].astype(BF)
        m_col[j, r] = m_total[j].astype(BF)
        get_mr.append(Gather(lambda i, j=j: m_row.at[j, i], True))
        get_mc.append(Gather(lambda i, j=j: m_col.at[j, i], False))
        get_mr[j].start()
        get_mc[j].start()

    x_base = take(2 * SIDE)

    def x_out(j, do):
        for sub in range(SIDE):
            @pl.when((r != y) | (x != sub))
            def _():
                do(pltpu.make_async_remote_copy(
                    src_ref=x_send.at[j, own_arrow * sub:own_arrow * (sub + 1)], dst_ref=x_in.at[j, c],
                    send_sem=send_sem.at[x_base + SIDE * j + sub], recv_sem=recv_sem.at[x_base + SIDE * j + c],
                    device_id=(chain, r * SIDE + sub), device_id_type=MESH))

    def x_wait(j):
        for i in range(SIDE):
            @pl.when((r != y) | (c != i))
            def _():
                copy(x_send.at[j, :own_arrow], x_in.at[j, i], x_base + SIDE * j + i, c_dev[1]).wait_recv()

    for j in range(2):
        @pl.when(has_a)
        def _():
            if j == 0:
                get_aq.wait()
            right = product(lambda k: a_diag[k], finals[j]).astype(BF)
            for s in range(SIDE):
                last_sum[j, s] = tdot(rows[finals[j], s], right)

        @pl.when(z + 1 == planes)
        def _():
            last_sum[j] = jnp.zeros((SIDE, panel, panel), F32)
        last_sum[j, r] += q_tile[finals[j]]

    sigma_rows = sigma[pl.ds(pl.multiple_of(r * arrow, 8), arrow)]
    for j in range(2):
        get_mr[j].wait()
        get_mc[j].wait()
        x_send[j] = lax.dot_general(
            sigma_rows, m_col[j].reshape(SIDE * arrow, panel).astype(F32), (((1,), (0,)), ((), ())),
            precision=lax.Precision.HIGHEST, preferred_element_type=F32)

        @pl.when(r == y)
        def _():
            x_in[j, c] = x_send[j, pl.ds(pl.multiple_of(x * own_arrow, 8), own_arrow)]
        x_out(j, lambda move: move.start())
        arrows = x_send[j].astype(BF)
        for s in range(SIDE):
            last_sum[j, s] += tdot(m_row[j, s], arrows)

    out_base = take(2 * SIDE * SIDE)

    def out_copy(j, i, dx):
        tx = lax.rem(x + dx, SIDE)
        src = out_send.at[j, r_at[i], pl.ds(pl.multiple_of(tx * row, 16), row)]
        sem = out_base + SIDE * SIDE * j
        return pltpu.make_async_remote_copy(
            src_ref=src, dst_ref=out_in.at[j, r, c], send_sem=send_sem.at[sem + SIDE * i + dx],
            recv_sem=recv_sem.at[sem + t], device_id=(chain, r_at[i] * SIDE + tx), device_id_type=MESH)

    def out_each(j, i, do):
        for dx in (2, 1, 3):
            do(out_copy(j, i, dx))

        @pl.when(r_at[i] != y)
        def _():
            do(out_copy(j, i, 0))

    @pl.when(has_b)
    def _():
        get_bq.wait()

    for j in range(2):
        @pl.when(has_b)
        def _():
            long_rows[j].wait()
            weight[...] = product(lambda k: b_diag[k], LONG + j).astype(BF)

        for i in (2, 1, 3, 0):
            s = r_at[i]

            @pl.when(has_b)
            def _():
                out_send[j, s] = (last_sum[j, s] + tdot(rows[LONG + j, s], weight[...])).astype(BF)

            @pl.when(z + 5 >= planes)
            def _():
                out_send[j, s] = last_sum[j, s].astype(BF)
            out_each(j, i, lambda move: move.start())
        out_in[j, r, c] = out_send[j, y, pl.ds(pl.multiple_of(x * row, 16), row)]

    groups = {}
    for when, sender in late:
        groups.setdefault(id(when), (when, []))[1].append(sender)

    def all_sent(senders):
        for sender in senders:
            for move in sender.each(False):
                move.wait_send()

    for when, senders in groups.values():
        if when is None:
            all_sent(senders)
        else:
            pl.when(when)(lambda senders=senders: all_sent(senders))
    spread(lambda move: move.wait_send())

    @pl.when(mine)
    def _():
        for n in range(3):
            tile_send(0, n, 0).wait_send()
            tile_send(0, n, 1).wait_send()

    @pl.when(core == 1)
    def _():
        for d in FAN:
            fan_copy(d, 0).wait_send()
            fan_copy(d, 1).wait_send()

    @pl.when(core == 0)
    def _():
        z_each([z_map(n) for n in range(3)] + [z_diag(n) for n in (1, 2, 3)], lambda move: move.wait_send())
        last_each(0, lambda move: move.wait_send())
        last_each(1, lambda move: move.wait_send())

    for j in range(2):
        x_wait(j)
        for i in range(SIDE):
            arrow_ref[j, :, panel * i:panel * (i + 1)] = x_in[j, i]
        x_out(j, lambda move: move.wait_send())
    for j in range(2):
        for sy in range(SIDE):
            for sx in range(SIDE):
                @pl.when(t != SIDE * sy + sx)
                def _():
                    at = (jnp.where(is_first, sy, sx), jnp.where(is_first, sx, sy))
                    copy(out_send.at[j, 0, :row], out_in.at[j, at[0], at[1]],
                         out_base + SIDE * SIDE * j + SIDE * sy + sx, c_dev[1]).wait_recv()
        for i in range(SIDE):
            total = out_in[j, 0, i].astype(F32)
            for k in range(1, SIDE):
                total += out_in[j, k, i].astype(F32)
            diag_ref[j, :, panel * i:panel * (i + 1)] = total
    for j in range(2):
        for i in range(SIDE):
            out_each(j, i, lambda move: move.wait_send())


def solution(mesh):
    planes = mesh.shape["chain"] // 2

    def on_device(inverse_diag, sub_diag, arrow_rows, arrow_inverse):
        count, row, node = inverse_diag.shape
        own_arrow = arrow_rows.shape[1]
        panel, arrow = row * SIDE, own_arrow * SIDE
        vm = pltpu.VMEM
        scratch = [
            vm(inverse_diag.shape, BF), vm(sub_diag.shape, BF), vm(arrow_rows.shape, BF), vm(arrow_inverse.shape, BF),
            vm((node, node), BF), vm((panel, node), BF), vm((SIDE, 2 * own_arrow, node), BF), vm((2 * own_arrow, node), BF),
            vm((panel + arrow, node), F32), vm((panel, node), F32), vm((2 * arrow, node), F32),
            vm((SIDE, 2 * panel + arrow, panel), BF), vm((2 * panel + arrow, panel), BF),
            vm((SIDE, 2 * panel + arrow, panel), BF),
            vm((9, SIDE, panel, panel), BF), vm((9, SIDE, panel, panel), BF),
            vm((8, panel + arrow, panel), BF), vm((8, panel, panel), F32), vm((8, arrow, panel), F32),
            vm((4, SIDE, panel + arrow, panel), BF), vm((4, SIDE, panel, panel), BF),
            vm((5, SIDE, panel, panel), BF), vm((5, SIDE, panel, panel), BF), vm((6, panel, panel), F32),
            vm((SIDE, panel, panel), F32),
            vm((8, panel, panel), BF),
            vm((SIDE, panel + arrow, panel), BF), vm((SIDE, panel, panel), BF),
            vm((SIDE, arrow, panel), BF), vm((SIDE, panel, panel), BF),
            vm((2, SIDE, arrow, panel), BF), vm((2, SIDE, arrow, panel), BF), vm((2, arrow, panel), F32),
            vm((2, arrow, panel), F32), vm((2, SIDE, own_arrow, panel), F32),
            vm((panel, panel), BF), vm((2, SIDE, panel, panel), F32), vm((2, SIDE, panel, panel), BF), vm((2, SIDE, SIDE, row, panel), BF),
            vm(arrow_inverse.shape, F32),
            pltpu.SemaphoreType.DMA((210,)), pltpu.SemaphoreType.DMA((210,)),
            pltpu.SemaphoreType.DMA((2, 6)), pltpu.SemaphoreType.DMA((28,)), pltpu.SemaphoreType.DMA((4,)),
        ]
        return pl.pallas_call(
            functools.partial(kernel, planes, (row, node, panel, own_arrow)),
            out_shape=(
                jax.ShapeDtypeStruct(inverse_diag.shape, F32),
                jax.ShapeDtypeStruct(arrow_rows.shape, F32),
            ),
            in_specs=[pl.BlockSpec(memory_space=pl.ANY)] * 4,
            out_specs=(pl.BlockSpec(memory_space=vm),) * 2,
            scratch_shapes=scratch,
            compiler_params=pltpu.CompilerParams(
                collective_id=0, has_side_effects=True, vmem_limit_bytes=62 << 20),
            name="selected_inverse",
        )(inverse_diag, sub_diag, arrow_rows, arrow_inverse)

    placed = P("chain", "tile", None)
    return jax.shard_map(
        on_device, mesh=mesh, in_specs=(placed, placed, placed, P()), out_specs=(placed, placed), check_vma=False)
```

```python
import functools
import jax
import jax.numpy as jnp
from jax import lax
from jax.experimental import pallas as pl
from jax.experimental.pallas import tpu as pltpu
from jax.sharding import PartitionSpec as P

MESH = pl.DeviceIdType.MESH
BF, F32 = jnp.bfloat16, jnp.float32
SIDE = 4
ODD, PAIR, PLANE, TRIPLE, EVEN, TWO, THREE, FOUR = range(8)
LONG = 7
OFFSETS = [(dy, dx) for dy in range(SIDE) for dx in range(SIDE) if dy or dx]
OFFSETS.sort(key=lambda o: min(o[0], 4 - o[0]) + min(o[1], 4 - o[1]))
RING = (2, 1, 3)
FAN = (2, 1, 3, 0)


def tdot(a, b):
    return lax.dot_general(a, b, (((0,), (0,)), ((), ())), preferred_element_type=F32)


def dot(a, b):
    return jnp.dot(a, b, preferred_element_type=F32)


def kernel(
    planes, sizes,
    l_in, b_in, a_in, z_in, diag_ref, arrow_ref,
    l_ref, b_ref, a_ref, z_ref, full_l, full_b, full_a, both_a, wide, wide_d, arrows_all, own_tiles, even, odd_far,
    cols, rows, tile, q_tile, m_tile, far_map, far_diag, part_out, part_in, part_own, part_sum, q_send,
    a_map, a_diag, b_arrow, b_diag, m_row, m_col, m_total, x_send, x_in, weight, last_sum, out_send, out_in, sigma,
    send_sem, recv_sem, l_send, l_recv, load_sem,
):
    row, node, panel, own_arrow = sizes
    arrow = own_arrow * SIDE
    chain = lax.axis_index("chain")
    t = lax.axis_index("tile")
    z, core = chain // 2, chain % 2
    y, x = t // SIDE, t % SIDE
    r, c = jnp.where(core == 0, y, x), jnp.where(core == 0, x, y)
    widths = [min(node, -(-panel * (i + 1) // 128) * 128) for i in range(SIDE)]
    loads = [pltpu.make_async_copy(src, dst, load_sem.at[n]) for n, (src, dst) in enumerate(
        ((l_in, l_ref), (b_in, b_ref), (a_in, a_ref), (z_in, z_ref)))]
    for load in loads:
        load.start()

    def place(core, r, c):
        return jnp.where(core == 0, r * SIDE + c, c * SIDE + r)

    def dev(dz=0, dcore=0, dr=0, dc=0):
        zz = lax.rem(z + dz + planes, planes)
        cc = lax.rem(core + dcore, 2)
        return (zz * 2 + cc, place(cc, lax.rem(r + dr, SIDE), lax.rem(c + dc, SIDE)))

    def near_by(dy, dx):
        return (chain, lax.rem(y + dy, SIDE) * SIDE + lax.rem(x + dx, SIDE))

    r_at, c_at = [lax.rem(r + d, SIDE) for d in range(SIDE)], [lax.rem(c + d, SIDE) for d in range(SIDE)]
    r_dev, c_dev = [dev(dr=d) for d in range(SIDE)], [dev(dc=d) for d in range(SIDE)]
    is_first = core == 0
    has = [None] + [z + n < planes for n in (1, 2, 3)]
    has_a, has_b = has[1], z + 5 < planes
    late = []

    used = [0]

    def take(n):
        used[0] += n
        assert used[0] <= send_sem.shape[0]
        return used[0] - n

    def copy(src, dst, sem, where):
        return pltpu.make_async_remote_copy(
            src_ref=src, dst_ref=dst, send_sem=send_sem.at[sem], recv_sem=recv_sem.at[sem],
            device_id=where, device_id_type=MESH)

    class Gather:
        def __init__(self, buf, along_c, when=None):
            self.buf, self.along_c, self.base = buf, along_c, take(3)
            late.append((when, self))

        def each(self, arriving):
            at, where = (c_at, c_dev) if self.along_c else (r_at, r_dev)
            for n, d in enumerate(RING):
                to = at[SIDE - d] if arriving else at[0]
                yield copy(self.buf(at[0]), self.buf(to), self.base + n, where[d])

        def start(self):
            for move in self.each(False):
                move.start()

        def wait(self):
            for move in self.each(True):
                move.wait_recv()

    barrier = pltpu.get_barrier_semaphore()
    group = [near_by(dy, dx) for dy, dx in OFFSETS]
    first = [dev(dcore=1, dc=d) for d in range(SIDE)] + [dev(dz=d) for d in (1, 2, 3, -3)]
    second = [dev(dz=d, dcore=1) for d in (1, -3)]
    for peer in group:
        pl.semaphore_signal(barrier, inc=1, device_id=peer, device_id_type=MESH)
    for k, others in enumerate((first, second)):
        @pl.when(core == k)
        def _():
            for peer in others:
                pl.semaphore_signal(barrier, inc=1, device_id=peer, device_id_type=MESH)

    my_rows = pl.ds(pl.multiple_of(t * row, 16), row)
    panel_rows = pl.ds(pl.multiple_of(x * row, 16), row)
    mine = c // 2 == core
    block = lax.rem(c, 2)
    for i in range(SIDE - 1):
        if widths[i] < node:
            full_l[panel * i:panel * (i + 1), widths[i]:] = jnp.zeros((panel, node - widths[i]), BF)
    for load in loads:
        load.wait()
    both_a[...] = jnp.concatenate([a_ref[0].astype(F32), a_ref[1].astype(F32)], axis=0).astype(BF)
    for k, extra in enumerate((6, SIDE)):
        @pl.when(core == k)
        def _():
            pl.semaphore_wait(barrier, len(group) + extra)

    def to_column(b, row):
        return (chain, place(core, row, 2 * core + b))

    def l_copy(b, dr, w):
        return pltpu.make_async_remote_copy(
            src_ref=l_ref.at[b, :, :w], dst_ref=full_l.at[my_rows, :w], send_sem=l_send.at[b, dr],
            recv_sem=l_recv.at[t], device_id=to_column(b, lax.rem(r + dr, SIDE)), device_id_type=MESH)

    def b_copy(b):
        return pltpu.make_async_remote_copy(
            src_ref=b_ref.at[b], dst_ref=full_b.at[panel_rows], send_sem=l_send.at[b, 4],
            recv_sem=l_recv.at[16 + x], device_id=to_column(b, y), device_id_type=MESH)

    def a_copy(b):
        return pltpu.make_async_remote_copy(
            src_ref=both_a, dst_ref=full_a.at[x], send_sem=l_send.at[b, 5],
            recv_sem=l_recv.at[20 + x], device_id=to_column(b, y), device_id_type=MESH)

    def spread(do):
        for b in range(2):
            for i in range(SIDE):
                @pl.when(y == i)
                def _():
                    for dr in (2, 1, 3):
                        do(l_copy(b, dr, widths[i]))

            @pl.when(c != 2 * core + b)
            def _():
                for i in range(SIDE):
                    @pl.when(y == i)
                    def _():
                        do(l_copy(b, 0, widths[i]))

            @pl.when((c != 2 * core + b) | (r != y))
            def _():
                do(b_copy(b))
                do(a_copy(b))

    spread(lambda move: move.start())
    sigma[...] = tdot(z_ref[...], z_ref[...])
    tile_base = take(6)
    tile_parts = (pl.ds(0, panel + arrow), pl.ds(panel + arrow, panel))

    def tile_send(b, n, part):
        to, at = c_at[RING[n]], tile_parts[part]
        dst = odd_far.at[to, at] if b else even.at[at]
        return pltpu.make_async_remote_copy(
            src_ref=own_tiles.at[to, at], dst_ref=dst, send_sem=send_sem.at[tile_base + 3 * part + n],
            recv_sem=l_recv.at[24 + 2 * part + b], device_id=c_dev[RING[n]], device_id_type=MESH)

    def tile_start(part):
        at = tile_parts[part]
        for b in range(2):
            @pl.when(block == b)
            def _():
                for n in range(3):
                    tile_send(b, n, part).start()
                if b:
                    odd_far[c, at] = own_tiles[c, at]
                else:
                    even[at] = own_tiles[c, at]

    def tile_wait(part):
        at = tile_parts[part]
        for b in (1, 0):
            @pl.when(c != 2 * core + b)
            def _():
                pltpu.make_async_remote_copy(
                    src_ref=own_tiles.at[0, at], dst_ref=odd_far.at[c, at] if b else even.at[at],
                    send_sem=send_sem.at[tile_base], recv_sem=l_recv.at[24 + 2 * part + b],
                    device_id=c_dev[1], device_id_type=MESH).wait_recv()

    @pl.when(mine)
    def _():
        for b in range(2):
            @pl.when(block == b)
            def _():
                full_l[my_rows, :] = l_ref[b]

                @pl.when(r == y)
                def _():
                    full_b[panel_rows, :] = b_ref[b]
                    full_a[x] = both_a[...]
        for s in range(SIDE * SIDE):
            @pl.when(t != s)
            def _():
                w = widths[s // SIDE]
                pltpu.make_async_remote_copy(
                    src_ref=l_ref.at[0, :, :w], dst_ref=full_l.at[pl.ds(s * row, row), :w],
                    send_sem=l_send.at[0, 0], recv_sem=l_recv.at[s], device_id=c_dev[1], device_id_type=MESH,
                ).wait_recv()
        for s in range(SIDE):
            @pl.when((x != s) | (r != y))
            def _():
                pltpu.make_async_remote_copy(
                    src_ref=b_ref.at[0], dst_ref=full_b.at[pl.ds(s * row, row)], send_sem=l_send.at[0, 4],
                    recv_sem=l_recv.at[16 + s], device_id=c_dev[1], device_id_type=MESH).wait_recv()
                pltpu.make_async_remote_copy(
                    src_ref=both_a, dst_ref=full_a.at[s], send_sem=l_send.at[0, 5],
                    recv_sem=l_recv.at[20 + s], device_id=c_dev[1], device_id_type=MESH).wait_recv()
        for j in range(0, node, 256):
            wide[:panel, j:j + 256] = -dot(full_b[:, j:], full_l[j:, j:j + 256])
            arrows_all[:, j:j + 256] = -dot(full_a[...].reshape(SIDE * 2 * own_arrow, node)[:, j:], full_l[j:, j:j + 256])
        for i in range(SIDE):
            lo = pl.multiple_of(2 * own_arrow * i + own_arrow * block, 8)
            wide[panel + own_arrow * i:panel + own_arrow * (i + 1)] = arrows_all[pl.ds(lo, own_arrow)]
        for i in range(SIDE):
            own_tiles[i, :panel + arrow] = wide[:, panel * i:panel * (i + 1)].astype(BF)
        tile_start(0)
        for i in range(SIDE):
            @pl.when(r == i)
            def _():
                lo = panel * i
                wide_d[...] = tdot(full_l[lo:, lo:lo + panel], full_l[lo:, :])
        for i in range(SIDE):
            own_tiles[i, panel + arrow:] = wide_d[:, panel * i:panel * (i + 1)].astype(BF)
        tile_start(1)

    def get_cols(slot, when=None):
        return Gather(lambda i: cols.at[slot, i], False, when)

    def get_rows(slot, when=None):
        return Gather(lambda i: rows.at[slot, i], True, when)

    def product(left, slot):
        total = dot(left(0), cols[slot, 0])
        for k in range(1, SIDE):
            total += dot(left(k), cols[slot, k])
        return total

    def new_map(left, near, to, spread=True):
        total = product(left, near)
        arrows = total[panel:] + m_tile[near]
        m_tile[to] = arrows
        tile[to, :panel] = total[:panel].astype(BF)
        tile[to, panel:] = arrows.astype(BF)
        if spread:
            cols[to, r] = total[:panel].astype(BF)
            rows[to, c] = total[:panel].astype(BF)

    class Congruence:
        def __init__(self, index, when=None):
            self.index, self.base = index, take(3)
            late.append((when, self))

        def each(self, arriving):
            for n, d in enumerate(RING):
                at = r_at[SIDE - d] if arriving else r
                yield copy(part_out.at[self.index, r_at[d]], part_in.at[self.index, at], self.base + n, r_dev[d])

        def add(self, left, near, first):
            right = product(left, near).astype(BF)
            for s in range(SIDE):
                piece = tdot(rows[near, s], right)
                part_sum[s] = piece if first else part_sum[s] + piece

        def send(self):
            for s in range(SIDE):
                part_out[self.index, s] = part_sum[s].astype(BF)
            for move in self.each(False):
                move.start()
            part_own[self.index] = part_sum[r]

        def start(self, left, near):
            self.add(left, near, True)
            self.send()

        def finish(self, near, to):
            total = part_own[self.index] + q_tile[near]
            for move in self.each(True):
                move.wait_recv()
            for d in RING:
                total += part_in[self.index, r_at[d]].astype(F32)
            q_tile[to] = total
            q_send[to] = total.astype(BF)

    tile_wait(0)
    cols[EVEN, r] = even[:panel]
    even_cols, even_rows, odd_cols = get_cols(EVEN), get_rows(EVEN), get_cols(ODD)
    odd_panel = Gather(lambda i: odd_far.at[i, pl.ds(0, panel + arrow)], True)
    odd_diags = Gather(lambda i: odd_far.at[i, pl.ds(panel + arrow, panel)], True)
    even_cols.start()
    odd_panel.start()
    rows[EVEN, c] = even[:panel]
    tile_wait(1)
    odd_diags.start()
    even_rows.start()
    cols[ODD, r] = odd_far[c, :panel]
    m_tile[EVEN] = even[panel:panel + arrow].astype(F32)
    q_tile[EVEN] = even[panel + arrow:].astype(F32)
    m_tile[ODD] = odd_far[c, panel:panel + arrow].astype(F32)
    q_tile[ODD] = odd_far[c, panel + arrow:].astype(F32)
    even_cols.wait()
    odd_panel.wait()
    new_map(lambda k: odd_far[k, :panel + arrow], EVEN, PAIR)
    fan = take(8)

    def fan_copy(d, diag):
        src = q_send.at[PAIR] if diag else tile.at[PAIR]
        dst = far_diag.at[0, c] if diag else far_map.at[0, c]
        return copy(src, dst, fan + 4 * diag + d, dev(dcore=1, dc=d))

    def fan_wait(diag):
        for d in range(SIDE):
            at = c_at[-d]
            src = q_send.at[PAIR] if diag else tile.at[PAIR]
            dst = far_diag.at[0, at] if diag else far_map.at[0, at]
            copy(src, dst, fan + 4 * diag + d, dev(dcore=1, dc=d)).wait_recv()

    @pl.when(core == 1)
    def _():
        for d in FAN:
            fan_copy(d, 0).start()

    pair_cols, pair_rows = get_cols(PAIR), get_rows(PAIR)
    pair = Congruence(0)

    @pl.when(is_first)
    def _():
        pair_cols.start()

    odd_diags.wait()
    even_rows.wait()
    pair.start(lambda k: odd_far[k, panel + arrow:], EVEN)

    @pl.when(is_first)
    def _():
        pair_rows.start()

    for k in range(SIDE):
        rows[ODD, k] = odd_far[k, :panel]

    z_base = take(6)

    def z_map(n):
        steps = (1, 1, 2)[n]
        src = tile.at[TWO if n else PLANE]
        return steps, copy(src, far_map.at[n + 1, c], z_base + n, dev(dz=-steps))

    def z_diag(n):
        return n, copy(q_send.at[PLANE], far_diag.at[n, c], z_base + 2 + n, dev(dz=-n))

    def z_each(copies, do):
        for steps, move in copies:
            @pl.when(z >= steps)
            def _():
                do(move)

    last_base = take(8)

    def last_copy(far, to_core, diag):
        if far:
            src = q_send.at[FOUR] if diag else tile.at[FOUR, pl.ds(panel, arrow)]
            dst = b_diag.at[c] if diag else b_arrow.at[c]
        else:
            src = q_send.at[FOUR] if diag else tile.at[FOUR]
            dst = a_diag.at[c] if diag else a_map.at[c]
        return copy(src, dst, last_base + 4 * far + 2 * to_core + diag, dev(dz=-5 if far else -1, dcore=to_core))

    def last_each(diag, do):
        for far, steps in ((1, 5), (0, 1)):
            @pl.when(z >= steps)
            def _():
                for k in range(2):
                    do(last_copy(far, k, diag))

    def last_wait(far, diag):
        for k in range(2):
            @pl.when(core == k)
            def _():
                last_copy(far, k, diag).wait_recv()

    far_maps = [None] + [Gather(lambda i, n=n: far_map.at[n, i], True, is_first & has[m]) for n, m in ((1, 1), (2, 3), (3, 2))]
    far_diags = [None] + [Gather(lambda i, n=n: far_diag.at[n, i], True, is_first & has[n]) for n in (1, 2, 3)]
    triple_cols, triple_rows = get_cols(TRIPLE, is_first), get_rows(TRIPLE, is_first)
    near = (None, PLANE, TWO, THREE)
    scan_when = (None, is_first, is_first & has[2], is_first & has[3])
    scan_cols = [None] + [get_cols(near[n], scan_when[n]) for n in (1, 2, 3)]
    scan_rows = [None] + [get_rows(near[n], scan_when[n]) for n in (1, 2, 3)]
    plane, triple, scan = Congruence(2, is_first), Congruence(1, is_first), Congruence(3, is_first & has_a)
    get_am = Gather(lambda i: a_map.at[i], True, has_a)
    get_bm = Gather(lambda i: b_arrow.at[i], True, has_b)
    get_aq = Gather(lambda i: a_diag.at[i], True, has_a)
    get_bq = Gather(lambda i: b_diag.at[i], True, has_b)
    long_cols, long_rows = [get_cols(LONG + j, has_b) for j in range(2)], [get_rows(LONG + j, has_b) for j in range(2)]
    finals = (jnp.where(core == 0, PLANE, PAIR), jnp.where(core == 0, TRIPLE, ODD))

    @pl.when(core == 1)
    def _():
        pair.finish(EVEN, PAIR)
        for d in FAN:
            fan_copy(d, 1).start()
        pair_cols.start()
        odd_cols.start()
        pair_rows.start()
        pair_cols.wait()
        pair_rows.wait()
        odd_cols.wait()

    @pl.when(core == 0)
    def _():
        fan_wait(0)
        pair_cols.wait()
        new_map(lambda k: far_map[0, k], PAIR, PLANE)
        z_each([z_map(0)], lambda move: move.start())
        scan_cols[1].start()
        scan_rows[1].start()
        pair.finish(EVEN, PAIR)

        @pl.when(has[1])
        def _():
            z_map(0)[1].wait_recv()
            far_maps[1].start()

        pair_rows.wait()
        fan_wait(1)
        plane.start(lambda k: far_diag[0, k], PAIR)
        scan_cols[1].wait()

        @pl.when(has[1])
        def _():
            far_maps[1].wait()
            new_map(lambda k: far_map[1, k], PLANE, TWO)

        @pl.when(z + 1 == planes)
        def _():
            tile[TWO] = tile[PLANE]

        z_each([z_map(2), z_map(1)], lambda move: move.start())

        @pl.when(has[2])
        def _():
            scan_cols[2].start()

        odd_cols.start()
        plane.finish(PAIR, PLANE)
        z_each([z_diag(n) for n in (3, 2, 1)], lambda move: move.start())

        @pl.when(has[2])
        def _():
            scan_rows[2].start()

        odd_cols.wait()
        new_map(lambda k: far_map[0, k], ODD, TRIPLE)
        triple_cols.start()

        @pl.when(has[1])
        def _():
            z_map(1)[1].wait_recv()

        @pl.when(has[3])
        def _():
            far_maps[2].start()

        @pl.when(has[2])
        def _():
            z_map(2)[1].wait_recv()
            far_maps[3].start()

        triple.start(lambda k: far_diag[0, k], ODD)

        for n in (1, 2, 3):
            @pl.when(has[n])
            def _():
                z_diag(n)[1].wait_recv()
                far_diags[n].start()

        @pl.when(has[2])
        def _():
            scan_cols[2].wait()
            far_maps[3].wait()
            new_map(lambda k: far_map[3, k], TWO, FOUR, False)

        @pl.when(z + 2 >= planes)
        def _():
            tile[FOUR] = tile[TWO]

        last_each(0, lambda move: move.start())

        @pl.when(has[3])
        def _():
            far_maps[2].wait()
            new_map(lambda k: far_map[2, k], PLANE, THREE)
            scan_cols[3].start()
            scan_rows[3].start()

        triple_rows.start()
        scan_rows[1].wait()

        @pl.when(has[1])
        def _():
            far_diags[1].wait()
            scan.add(lambda k: far_diag[1, k], PLANE, True)

        @pl.when(has[2])
        def _():
            scan_rows[2].wait()
            far_diags[2].wait()
            scan.add(lambda k: far_diag[2, k], TWO, False)

        triple_cols.wait()

    @pl.when(has_a)
    def _():
        last_wait(0, 0)
        get_am.start()

    @pl.when(has_b)
    def _():
        last_wait(1, 0)
        get_bm.start()

    @pl.when((core == 0) & has_a)
    def _():
        @pl.when(has[3])
        def _():
            far_diags[3].wait()
            scan_cols[3].wait()
            scan_rows[3].wait()
            scan.add(lambda k: far_diag[3, k], THREE, False)
        scan.send()

    @pl.when((core == 0) & (z + 1 == planes))
    def _():
        q_send[FOUR] = q_send[PLANE]
        last_each(1, lambda move: move.start())

    @pl.when(has_a)
    def _():
        get_am.wait()
        for j in range(2):
            total = product(lambda k: a_map[k], finals[j])
            m_total[j] = total[panel:] + m_tile[finals[j]]

            @pl.when(has_b)
            def _():
                cols[LONG + j, r] = total[:panel].astype(BF)
                rows[LONG + j, c] = total[:panel].astype(BF)
                long_cols[j].start()

        @pl.when(has_b)
        def _():
            for j in range(2):
                long_rows[j].start()

    @pl.when(z + 1 == planes)
    def _():
        for j in range(2):
            m_total[j] = m_tile[finals[j]]

    @pl.when(core == 0)
    def _():
        @pl.when(has_a)
        def _():
            scan.finish(PLANE, FOUR)
            last_each(1, lambda move: move.start())
        triple.finish(ODD, TRIPLE)
        triple_rows.wait()

    @pl.when(has_a)
    def _():
        last_wait(0, 1)
        get_aq.start()

    @pl.when(has_b)
    def _():
        last_wait(1, 1)
        get_bq.start()

    @pl.when(has_b)
    def _():
        get_bm.wait()
        for j in range(2):
            long_cols[j].wait()
            m_total[j] += product(lambda k: b_arrow[k], LONG + j)

    get_mr, get_mc = [], []
    for j in range(2):
        m_row[j, c] = m_total[j].astype(BF)
        m_col[j, r] = m_total[j].astype(BF)
        get_mr.append(Gather(lambda i, j=j: m_row.at[j, i], True))
        get_mc.append(Gather(lambda i, j=j: m_col.at[j, i], False))
        get_mr[j].start()
        get_mc[j].start()

    x_base = take(2 * SIDE)

    def x_out(j, do):
        for sub in range(SIDE):
            @pl.when((r != y) | (x != sub))
            def _():
                do(pltpu.make_async_remote_copy(
                    src_ref=x_send.at[j, own_arrow * sub:own_arrow * (sub + 1)], dst_ref=x_in.at[j, c],
                    send_sem=send_sem.at[x_base + SIDE * j + sub], recv_sem=recv_sem.at[x_base + SIDE * j + c],
                    device_id=(chain, r * SIDE + sub), device_id_type=MESH))

    def x_wait(j):
        for i in range(SIDE):
            @pl.when((r != y) | (c != i))
            def _():
                copy(x_send.at[j, :own_arrow], x_in.at[j, i], x_base + SIDE * j + i, c_dev[1]).wait_recv()

    for j in range(2):
        @pl.when(has_a)
        def _():
            if j == 0:
                get_aq.wait()
            right = product(lambda k: a_diag[k], finals[j]).astype(BF)
            for s in range(SIDE):
                last_sum[j, s] = tdot(rows[finals[j], s], right)

        @pl.when(z + 1 == planes)
        def _():
            last_sum[j] = jnp.zeros((SIDE, panel, panel), F32)
        last_sum[j, r] += q_tile[finals[j]]

    sigma_rows = sigma[pl.ds(pl.multiple_of(r * arrow, 8), arrow)]
    for j in range(2):
        get_mr[j].wait()
        get_mc[j].wait()
        x_send[j] = lax.dot_general(
            sigma_rows, m_col[j].reshape(SIDE * arrow, panel).astype(F32), (((1,), (0,)), ((), ())),
            precision=lax.Precision.HIGHEST, preferred_element_type=F32)

        @pl.when(r == y)
        def _():
            x_in[j, c] = x_send[j, pl.ds(pl.multiple_of(x * own_arrow, 8), own_arrow)]
        x_out(j, lambda move: move.start())
        arrows = x_send[j].astype(BF)
        for s in range(SIDE):
            last_sum[j, s] += tdot(m_row[j, s], arrows)

    out_base = take(2 * SIDE * SIDE)

    def out_copy(j, i, dx):
        tx = lax.rem(x + dx, SIDE)
        src = out_send.at[j, r_at[i], pl.ds(pl.multiple_of(tx * row, 16), row)]
        sem = out_base + SIDE * SIDE * j
        return pltpu.make_async_remote_copy(
            src_ref=src, dst_ref=out_in.at[j, r, c], send_sem=send_sem.at[sem + SIDE * i + dx],
            recv_sem=recv_sem.at[sem + t], device_id=(chain, r_at[i] * SIDE + tx), device_id_type=MESH)

    def out_each(j, i, do):
        for dx in (2, 1, 3):
            do(out_copy(j, i, dx))

        @pl.when(r_at[i] != y)
        def _():
            do(out_copy(j, i, 0))

    @pl.when(has_b)
    def _():
        get_bq.wait()

    for j in range(2):
        @pl.when(has_b)
        def _():
            long_rows[j].wait()
            weight[...] = product(lambda k: b_diag[k], LONG + j).astype(BF)

        for i in (2, 1, 3, 0):
            s = r_at[i]

            @pl.when(has_b)
            def _():
                out_send[j, s] = (last_sum[j, s] + tdot(rows[LONG + j, s], weight[...])).astype(BF)

            @pl.when(z + 5 >= planes)
            def _():
                out_send[j, s] = last_sum[j, s].astype(BF)
            out_each(j, i, lambda move: move.start())
        out_in[j, r, c] = out_send[j, y, pl.ds(pl.multiple_of(x * row, 16), row)]

    groups = {}
    for when, sender in late:
        groups.setdefault(id(when), (when, []))[1].append(sender)

    def all_sent(senders):
        for sender in senders:
            for move in sender.each(False):
                move.wait_send()

    for when, senders in groups.values():
        if when is None:
            all_sent(senders)
        else:
            pl.when(when)(lambda senders=senders: all_sent(senders))
    spread(lambda move: move.wait_send())

    @pl.when(mine)
    def _():
        for n in range(3):
            tile_send(0, n, 0).wait_send()
            tile_send(0, n, 1).wait_send()

    @pl.when(core == 1)
    def _():
        for d in FAN:
            fan_copy(d, 0).wait_send()
            fan_copy(d, 1).wait_send()

    @pl.when(core == 0)
    def _():
        z_each([z_map(n) for n in range(3)] + [z_diag(n) for n in (1, 2, 3)], lambda move: move.wait_send())
        last_each(0, lambda move: move.wait_send())
        last_each(1, lambda move: move.wait_send())

    for j in range(2):
        x_wait(j)
        for i in range(SIDE):
            arrow_ref[j, :, panel * i:panel * (i + 1)] = x_in[j, i]
        x_out(j, lambda move: move.wait_send())
    for j in range(2):
        for sy in range(SIDE):
            for sx in range(SIDE):
                @pl.when(t != SIDE * sy + sx)
                def _():
                    at = (jnp.where(is_first, sy, sx), jnp.where(is_first, sx, sy))
                    copy(out_send.at[j, 0, :row], out_in.at[j, at[0], at[1]],
                         out_base + SIDE * SIDE * j + SIDE * sy + sx, c_dev[1]).wait_recv()
        for i in range(SIDE):
            total = out_in[j, 0, i].astype(F32)
            for k in range(1, SIDE):
                total += out_in[j, k, i].astype(F32)
            diag_ref[j, :, panel * i:panel * (i + 1)] = total
    for j in range(2):
        for i in range(SIDE):
            out_each(j, i, lambda move: move.wait_send())


def solution(mesh):
    planes = mesh.shape["chain"] // 2

    def on_device(inverse_diag, sub_diag, arrow_rows, arrow_inverse):
        count, row, node = inverse_diag.shape
        own_arrow = arrow_rows.shape[1]
        panel, arrow = row * SIDE, own_arrow * SIDE
        vm = pltpu.VMEM
        scratch = [
            vm(inverse_diag.shape, BF), vm(sub_diag.shape, BF), vm(arrow_rows.shape, BF), vm(arrow_inverse.shape, BF),
            vm((node, node), BF), vm((panel, node), BF), vm((SIDE, 2 * own_arrow, node), BF), vm((2 * own_arrow, node), BF),
            vm((panel + arrow, node), F32), vm((panel, node), F32), vm((2 * arrow, node), F32),
            vm((SIDE, 2 * panel + arrow, panel), BF), vm((2 * panel + arrow, panel), BF),
            vm((SIDE, 2 * panel + arrow, panel), BF),
            vm((9, SIDE, panel, panel), BF), vm((9, SIDE, panel, panel), BF),
            vm((8, panel + arrow, panel), BF), vm((8, panel, panel), F32), vm((8, arrow, panel), F32),
            vm((4, SIDE, panel + arrow, panel), BF), vm((4, SIDE, panel, panel), BF),
            vm((5, SIDE, panel, panel), BF), vm((5, SIDE, panel, panel), BF), vm((6, panel, panel), F32),
            vm((SIDE, panel, panel), F32),
            vm((8, panel, panel), BF),
            vm((SIDE, panel + arrow, panel), BF), vm((SIDE, panel, panel), BF),
            vm((SIDE, arrow, panel), BF), vm((SIDE, panel, panel), BF),
            vm((2, SIDE, arrow, panel), BF), vm((2, SIDE, arrow, panel), BF), vm((2, arrow, panel), F32),
            vm((2, arrow, panel), F32), vm((2, SIDE, own_arrow, panel), F32),
            vm((panel, panel), BF), vm((2, SIDE, panel, panel), F32), vm((2, SIDE, panel, panel), BF), vm((2, SIDE, SIDE, row, panel), BF),
            vm(arrow_inverse.shape, F32),
            pltpu.SemaphoreType.DMA((210,)), pltpu.SemaphoreType.DMA((210,)),
            pltpu.SemaphoreType.DMA((2, 6)), pltpu.SemaphoreType.DMA((28,)), pltpu.SemaphoreType.DMA((4,)),
        ]
        return pl.pallas_call(
            functools.partial(kernel, planes, (row, node, panel, own_arrow)),
            out_shape=(
                jax.ShapeDtypeStruct(inverse_diag.shape, F32),
                jax.ShapeDtypeStruct(arrow_rows.shape, F32),
            ),
            in_specs=[pl.BlockSpec(memory_space=pl.ANY)] * 4,
            out_specs=(pl.BlockSpec(memory_space=vm),) * 2,
            scratch_shapes=scratch,
            compiler_params=pltpu.CompilerParams(
                collective_id=0, has_side_effects=True, vmem_limit_bytes=62 << 20),
            name="selected_inverse",
        )(inverse_diag, sub_diag, arrow_rows, arrow_inverse)

    placed = P("chain", "tile", None)
    return jax.shard_map(
        on_device, mesh=mesh, in_specs=(placed, placed, placed, P()), out_specs=(placed, placed), check_vma=False)
```
